32 devices in a mesh: dp: 8 (over z, y), seq: 4 (over x, core).
Axes of the slice: x: 2, y: 2, z: 4, core: 2. Of those that a mesh axis runs over, the one named last changes fastest.
Arguments:
- patches: bfloat16 [32, 544, 768], P('dp', 'seq'), may hold values from -6 to 6
- cotangent: bfloat16 [32, 544, 768], P('dp', 'seq'), may hold values from -8 to 8
- lengths: int32 [32], P('dp'), may hold values from 40 to 529, as said below
- w_qkv: float32 [2304, 768], P('dp'), may hold values from -0.21875 to 0.21875
- w_out: float32 [768, 768], P('dp'), may hold values from -0.875 to 0.875
- w_fc1: float32 [3072, 768], P('dp'), may hold values from -0.28867513 to 0.28867513
- w_fc2: float32 [3072, 768], P('dp'), may hold values from -0.14433757 to 0.14433757
- mom_qkv: float32 [2304, 768], P('dp'), may hold values from -0.0026311536 to 0.0026311536
- mom_out: float32 [768, 768], P('dp'), may hold values from -0.0026311536 to 0.0026311536
- mom_fc1: float32 [3072, 768], P('dp'), may hold values from -0.0026311536 to 0.0026311536
- mom_fc2: float32 [3072, 768], P('dp'), may hold values from -0.0026311536 to 0.0026311536
- vectors: float32 [9216], P('dp'), may hold values from -1 to 2
- vec_first: float32 [9216], P('dp'), may hold values from -0.015625 to 0.015625
- vec_second: float32 [9216], P('dp'), may hold values from 6.357829e-07 to 1.0172526e-05
Outputs:
- mixed: bfloat16 [32, 544, 768], P('dp', 'seq')
- grad_patches: bfloat16 [32, 544, 768], P('dp', 'seq')
- grad_norm: float32 [], replicated
- mom_qkv_new: float32 [2304, 768], P('dp')
- w_qkv_new: float32 [2304, 768], P('dp')
- mom_out_new: float32 [768, 768], P('dp')
- w_out_new: float32 [768, 768], P('dp')
- mom_fc1_new: float32 [3072, 768], P('dp')
- w_fc1_new: float32 [3072, 768], P('dp')
- mom_fc2_new: float32 [3072, 768], P('dp')
- w_fc2_new: float32 [3072, 768], P('dp')
- vec_first_new: float32 [9216], P('dp')
- vec_second_new: float32 [9216], P('dp')
- vectors_new: float32 [9216], P('dp')
The draws below stay inside these ranges and needn't reach their ends.
Inputs may be any that keep to these rules, and one draw needn't show every extreme that they name: `lengths`: each index of dp holds 4 consecutive strips; one of them has exactly 529 filled patches; the others vary from seed to seed.
All inputs are finite; a program needn't handle non-finite values.
Results may differ from the reference program's by a relative error of at most 0.014.
The reference program's roundings to bfloat16 on the way count: a program that leaves them out, or rounds other values in their place, can miss the bound.
Values may be sent and summed in bfloat16 or wider, within the bound.
No kernel may reach another device: no remote copies, remote signals or barrier semaphores. Data moves between devices by JAX's collectives and lax.ppermute only.
A program may use at most 192 MiB of HBM per device.

```python
import math
import jax
import jax.numpy as jnp
from jax import lax

D = 768
FF = 3072
HEADS = 12
SEQS_DEV = 4
SLOTS = 544
PATCHES = 529
LEN_MIN = 40
ITERS = 5
ADAM_STEP = 10
STRIPS = 32
VEC = 9216


def ramp_rows(count, low_end, high_end):
    return low_end + (high_end - low_end) * jnp.arange(count, dtype=jnp.float32) / (count - 1)


def moment_scale():
    return (4 * D * D + 2 * D * FF) ** (-0.5)


def draw_cotangent(key, part):
    key = jax.random.fold_in(key, 11)
    base = jnp.clip(jax.random.normal(key, (STRIPS, SLOTS, D), jnp.float32), -4.0, 4.0)
    ramp = ramp_rows(D, 0.6, 1.8)
    return (base * ramp[None, None, :]).astype(jnp.bfloat16)


def draw_w_fc1(key, part):
    key = jax.random.fold_in(key, 21)
    base = jnp.clip(jax.random.normal(key, (FF, D), jnp.float32), -4.0, 4.0)
    ramp = ramp_rows(FF, 0.6, 1.8)
    return base * ramp[:, None] * D ** (-0.5)


def draw_w_fc2(key, part):
    key = jax.random.fold_in(key, 22)
    base = jnp.clip(jax.random.normal(key, (FF, D), jnp.float32), -4.0, 4.0)
    ramp = ramp_rows(FF, 0.6, 1.8)
    return base * ramp[:, None] * FF ** (-0.5)


def draw_mom_qkv(key, part):
    key = jax.random.fold_in(key, 51)
    base = jnp.clip(jax.random.normal(key, (3 * D, D), jnp.float32), -4.0, 4.0)
    ramp = ramp_rows(3 * D, 0.5, 1.5)
    return base * ramp[:, None] * moment_scale()


def draw_mom_out(key, part):
    key = jax.random.fold_in(key, 52)
    base = jnp.clip(jax.random.normal(key, (D, D), jnp.float32), -4.0, 4.0)
    ramp = ramp_rows(D, 0.5, 1.5)
    return base * ramp[:, None] * moment_scale()


def draw_mom_fc1(key, part):
    key = jax.random.fold_in(key, 53)
    base = jnp.clip(jax.random.normal(key, (FF, D), jnp.float32), -4.0, 4.0)
    ramp = ramp_rows(FF, 0.5, 1.5)
    return base * ramp[:, None] * moment_scale()


def draw_mom_fc2(key, part):
    key = jax.random.fold_in(key, 54)
    base = jnp.clip(jax.random.normal(key, (FF, D), jnp.float32), -4.0, 4.0)
    ramp = ramp_rows(FF, 0.5, 1.5)
    return base * ramp[:, None] * moment_scale()


def draw_vectors(key, part):
    key = jax.random.fold_in(key, 31)
    positions = jnp.arange(VEC)
    is_gain = (positions < D) | (positions >= 5 * D) & (positions < 6 * D)
    noise = jnp.clip(jax.random.normal(key, (VEC,), jnp.float32), -4.0, 4.0)
    return jnp.where(is_gain, 1.0 + 0.15 * noise, 0.2 * noise)


def draw_lengths(key, part):
    key = jax.random.fold_in(key, 41)
    first_key, second_key = jax.random.split(key)
    drawn = jax.random.randint(first_key, (STRIPS,), LEN_MIN, PATCHES + 1)
    chosen = jax.random.randint(second_key, (STRIPS // SEQS_DEV,), 0, SEQS_DEV)
    strip_ids = jnp.arange(STRIPS, dtype=jnp.int32)
    longest = strip_ids % SEQS_DEV == chosen[strip_ids // SEQS_DEV]
    return jnp.where(longest, PATCHES, drawn).astype(jnp.int32)


def steps_of(key, extent, cuts, least, largest):
    def one(dim, parts):
        draws = jax.random.uniform(jax.random.fold_in(jax.random.fold_in(key, 6), dim), (parts,), jnp.float32, least / len(cuts), largest / len(cuts))
        return jnp.repeat(jnp.exp(draws), extent[dim] // parts).reshape((-1,) + (1,) * (len(extent) - dim - 1))

    loudness = one(*cuts[0])
    for cut in cuts[1:]:
        loudness = loudness * one(*cut)
    return loudness


def centred(rng, shape, scale, bound, cuts=(), kind=jnp.bfloat16):
    values = scale * jax.random.normal(rng, shape, jnp.float32)
    if cuts:
        values = values * steps_of(rng, shape, cuts, -0.22, 0.18)
    return jnp.clip(values, -bound, bound).astype(kind)


def setup_inputs(seed: int = 0) -> dict:
    streams_of = jax.random.split(jax.random.key(seed), 15)
    patches = centred(streams_of[0], (STRIPS, SLOTS, D), 1.0, 6.0, ((0, 8), (1, 4)))
    cotangent = draw_cotangent(jax.random.fold_in(streams_of[14], 71), 0)
    lengths = draw_lengths(jax.random.fold_in(streams_of[14], 71), 0)
    w_qkv = centred(streams_of[3], (3 * D, D), D ** -0.5, 0.21875, ((0, 8),), jnp.float32)
    w_out = centred(streams_of[4], (D, D), (D // 16) ** -0.5, 0.875, ((0, 8),), jnp.float32)
    w_fc1 = draw_w_fc1(jax.random.fold_in(streams_of[14], 71), 0)
    w_fc2 = draw_w_fc2(jax.random.fold_in(streams_of[14], 71), 0)
    mom_qkv = draw_mom_qkv(jax.random.fold_in(streams_of[14], 71), 0)
    mom_out = draw_mom_out(jax.random.fold_in(streams_of[14], 71), 0)
    mom_fc1 = draw_mom_fc1(jax.random.fold_in(streams_of[14], 71), 0)
    mom_fc2 = draw_mom_fc2(jax.random.fold_in(streams_of[14], 71), 0)
    vectors = draw_vectors(jax.random.fold_in(streams_of[14], 71), 0)
    vec_first = centred(streams_of[12], (VEC,), (3 * (4 * D * D + 2 * D * FF) ** -0.5), 0.015625, ((0, 8),), jnp.float32)
    vec_second = jnp.clip(jnp.exp(math.log(1.0172526344831567e-05) - 2.7725887 * jax.random.uniform(streams_of[13], (VEC,), jnp.float32) ** steps_of(streams_of[13], (VEC,), ((0, 8),), -0.2, 0.2)), 6.35782896551973e-07, 1.0172526344831567e-05)
    return {"patches": patches, "cotangent": cotangent, "lengths": lengths, "w_qkv": w_qkv, "w_out": w_out, "w_fc1": w_fc1, "w_fc2": w_fc2, "mom_qkv": mom_qkv, "mom_out": mom_out, "mom_fc1": mom_fc1, "mom_fc2": mom_fc2, "vectors": vectors, "vec_first": vec_first, "vec_second": vec_second}


HIGHEST = lax.Precision.HIGHEST
NEG_BIG = -1e+30
LN_EPS = 1e-06
NS_COEFFS = (3.4445, -4.775, 2.0315)
MOMENTUM = 0.5
CLIP = 1.0
DECAY = 0.01
MATRIX_RATES = (1.0, 3.0, 1.0, 0.6)
VEC_RATE = 0.1
BETA_ONE = 0.5
BETA_TWO = 0.5

@jax.custom_vjp
def low(v):
    return lax.optimization_barrier(v.astype(jnp.bfloat16)).astype(jnp.float32)

@jax.custom_vjp
def low_back(v):
    return v

def low_keep(v):
    return (low(v), None)

def low_pass(kept, grad):
    return (grad,)

def back_keep(v):
    return (v, None)

def back_low(kept, grad):
    return (low(grad),)
low.defvjp(low_keep, low_pass)
low_back.defvjp(back_keep, back_low)

def layer_norm(values, gain, offset):
    centre = values - lax.optimization_barrier(jnp.mean(values, axis=-1, keepdims=True))
    spread = lax.optimization_barrier(jnp.mean(centre * centre, axis=-1, keepdims=True))
    return centre * lax.rsqrt(spread + LN_EPS) * gain + offset

def split_vector(vector):
    bounds = [0, D, 2 * D, 3 * D, 4 * D, 5 * D, 6 * D, 7 * D, 7 * D + FF, 8 * D + FF]
    return [vector[bounds[position]:bounds[position + 1]] for position in range(9)]

def attend(item):
    queries, keys_in, values_in, key_mask = item
    scale = 1.0 / math.sqrt(D // HEADS)
    scores = jnp.einsum('qhd,khd->hqk', queries, keys_in, precision=HIGHEST) * scale
    scores = low_back(scores)
    scores = jnp.where(key_mask[None, None, :], scores, NEG_BIG)
    row_max = lax.optimization_barrier(jnp.max(scores, axis=-1, keepdims=True))
    raised = jnp.exp(scores - row_max)
    softmaxed = raised / lax.optimization_barrier(jnp.sum(raised, axis=-1, keepdims=True))
    return jnp.einsum('hqk,khd->qhd', low(softmaxed), values_in, precision=HIGHEST)

def forward(patches_f, w_qkv, w_out, w_fc1, w_fc2, vectors, key_mask):
    strip_count = patches_f.shape[0]
    rows_all = strip_count * SLOTS
    pieces = split_vector(low(vectors))
    gain_one, bias_one, query_bias, value_bias, out_bias, gain_two, bias_two, fc1_bias, fc2_bias = pieces
    flat = patches_f.reshape(rows_all, D)
    normed = low(layer_norm(flat, gain_one, bias_one))
    joint_bias = jnp.concatenate([query_bias, jnp.zeros((D,), jnp.float32), value_bias])
    projected = jnp.dot(normed, low(w_qkv).T, precision=HIGHEST) + joint_bias
    projected = low(low_back(projected)).reshape(strip_count, SLOTS, 3, HEADS, D // HEADS)
    attended = lax.map(jax.checkpoint(attend), (projected[:, :, 0], projected[:, :, 1], projected[:, :, 2], key_mask))
    attended = low(low_back(attended.reshape(rows_all, D)))
    mixed_attn = low_back(jnp.dot(attended, low(w_out).T, precision=HIGHEST))
    first_sum = flat + mixed_attn + out_bias
    normed_two = low(layer_norm(first_sum, gain_two, bias_two))
    hidden_pre = low_back(jnp.dot(normed_two, low(w_fc1).T, precision=HIGHEST) + fc1_bias)
    activated = low(jax.nn.gelu(hidden_pre, approximate=False))
    second_sum = first_sum + jnp.dot(activated, low(w_fc2), precision=HIGHEST) + fc2_bias
    return second_sum.reshape(strip_count, SLOTS, D)

def newton_schulz(moment):
    scaled = moment / (jnp.sqrt(jnp.sum(moment * moment)) + 1e-07)
    for sweep_index in range(ITERS):
        gram = jnp.dot(scaled.T, scaled, precision=HIGHEST)
        product = jnp.dot(scaled, gram, precision=HIGHEST)
        scaled = NS_COEFFS[0] * scaled + NS_COEFFS[1] * product + NS_COEFFS[2] * jnp.dot(product, gram, precision=HIGHEST)
    return scaled

def reference(patches, cotangent, lengths, w_qkv, w_out, w_fc1, w_fc2, mom_qkv, mom_out, mom_fc1, mom_fc2, vectors, vec_first, vec_second):
    group_count = STRIPS // SEQS_DEV
    inputs = patches.astype(jnp.float32).reshape(group_count, SEQS_DEV, SLOTS, D)
    upstream = cotangent.astype(jnp.float32).reshape(group_count, SEQS_DEV, SLOTS, D)
    grouped_lengths = lengths.reshape(group_count, SEQS_DEV)
    slot_ids = jnp.arange(SLOTS, dtype=jnp.int32)
    weights = (w_qkv, w_out, w_fc1, w_fc2, vectors)

    def one_group(totals, item):
        group_in, group_up, group_len = item
        key_mask = slot_ids[None, :] < group_len[:, None]

        def apply_layer(values, wqkv, wout, wone, wtwo, vector):
            return forward(values, wqkv, wout, wone, wtwo, vector, key_mask)
        result, pull = jax.vjp(apply_layer, group_in, *weights)
        grads = pull(group_up)
        new_totals = tuple((total + grad for total, grad in zip(totals, grads[1:])))
        return (new_totals, (result.astype(jnp.bfloat16), grads[0].astype(jnp.bfloat16)))
    start = tuple((jnp.zeros_like(weight) for weight in weights))
    totals, (results, input_grads) = lax.scan(one_group, start, (inputs, upstream, grouped_lengths))
    squares = jnp.float32(0.0)
    for grad in totals:
        squares = squares + jnp.sum(grad * grad)
    grad_norm = jnp.sqrt(squares)
    clip = jnp.minimum(1.0, CLIP / (grad_norm + 1e-06))
    outputs = []
    moments = (mom_qkv, mom_out, mom_fc1, mom_fc2)
    for position in range(4):
        weight = weights[position]
        moment_new = MOMENTUM * moments[position] + clip * totals[position]
        ortho = newton_schulz(moment_new)
        rate = MATRIX_RATES[position]
        ratio = math.sqrt(weight.shape[0] / D)
        outputs.append(moment_new)
        outputs.append(weight * (1.0 - rate * DECAY) - rate * ratio * ortho)
    vec_grad = clip * totals[4]
    first_new = BETA_ONE * vec_first + (1.0 - BETA_ONE) * vec_grad
    second_new = BETA_TWO * vec_second + (1.0 - BETA_TWO) * vec_grad * vec_grad
    first_hat = first_new / (1.0 - BETA_ONE ** ADAM_STEP)
    second_hat = second_new / (1.0 - BETA_TWO ** ADAM_STEP)
    vectors_new = vectors - VEC_RATE * first_hat / (jnp.sqrt(second_hat) + 1e-08)
    mixed = results.reshape(STRIPS, SLOTS, D)
    grad_patches = input_grads.reshape(STRIPS, SLOTS, D)
    return (mixed, grad_patches, grad_norm, outputs[0], outputs[1], outputs[2], outputs[3], outputs[4], outputs[5], outputs[6], outputs[7], first_new, second_new, vectors_new)
```

```python
import math

import jax
import jax.numpy as jnp
from jax import lax
from jax.experimental import pallas as pl
from jax.experimental.pallas import tpu as pltpu
from jax.sharding import PartitionSpec as P

D = 768
FF = 3072
HEADS = 12
ITERS = 5
ADAM_STEP = 10

NEG_BIG = -1e30
LN_EPS = 1e-06
NS_COEFFS = (3.4445, -4.775, 2.0315)
MOMENTUM = 0.5
CLIP = 1.0
DECAY = 0.01
MATRIX_RATES = (1.0, 3.0, 1.0, 0.6)
VEC_RATE = 0.1
BETA_ONE = 0.5
BETA_TWO = 0.5
ROWS_LAST = (((0,), (0,)), ((), ()))
COLS_LAST = (((1,), (1,)), ((), ()))
BOTH = ("dp", "seq")
VMEM_BYTES = 56 * 1024 * 1024
TILES = 8
BF = jnp.bfloat16
F32 = jnp.float32


def layer_norm(values, gain, offset):
    centre = values - jnp.mean(values, axis=-1, keepdims=True)
    spread = jnp.mean(centre * centre, axis=-1, keepdims=True)
    return centre * lax.rsqrt(spread + LN_EPS) * gain + offset


def split_vector(vector):
    bounds = [0, D, 2 * D, 3 * D, 4 * D, 5 * D, 6 * D, 7 * D, 7 * D + FF, 8 * D + FF]
    return [vector[bounds[position] : bounds[position + 1]] for position in range(9)]


def contract_rows(left, right):
    return lax.dot_general(left, right, ROWS_LAST, preferred_element_type=F32)


def contract_cols(left, right):
    return lax.dot_general(left, right, COLS_LAST, preferred_element_type=F32)


def place_kernel(order_ref, *refs):
    sources, out, sem = refs[:-2], refs[-2], refs[-1]
    copies = []
    for source in sources:
        for piece in range(source.shape[0]):
            at = len(copies)
            copies.append(pltpu.make_async_copy(source.at[piece], out.at[order_ref[at]], sem.at[at]))
            copies[-1].start()
    for copy in copies:
        copy.wait()


def place(order, *sources):
    count = sum(source.shape[0] for source in sources)
    piece = sources[0].shape[1:]
    return pl.pallas_call(
        place_kernel,
        out_shape=jax.ShapeDtypeStruct((count,) + piece, sources[0].dtype),
        in_specs=[pl.BlockSpec(memory_space=pltpu.SMEM)]
        + [pl.BlockSpec(memory_space=pl.ANY)] * len(sources),
        out_specs=pl.BlockSpec(memory_space=pltpu.VMEM),
        scratch_shapes=[pltpu.SemaphoreType.DMA((count,))],
        compiler_params=pltpu.CompilerParams(vmem_limit_bytes=VMEM_BYTES),
    )(order, *sources)


class Plain:
    def __init__(self, dp, seq):
        self.dp, self.seq = dp, seq
        self.dp_at, self.seq_at = lax.axis_index("dp"), lax.axis_index("seq")

    def gather_rows(self, block):
        return lax.all_gather(block, "dp", axis=0, tiled=True)

    def gather_tiles(self, block):
        return jnp.split(self.gather_rows(block), TILES)

    def tile_order(self):
        return jnp.arange(32), jnp.arange(32)

    def reduce_tiles(self, tiles):
        return self.reduce_rows(jnp.concatenate(tiles, axis=0))

    def gather_vector(self, block):
        return lax.all_gather(block, "dp", axis=0, tiled=True)

    def reduce_rows(self, grad):
        return lax.psum_scatter(grad.astype(F32), BOTH, scatter_dimension=0, tiled=True)

    def sum_all(self, value):
        return lax.psum(value, BOTH)

    def sum_dp(self, value):
        return lax.psum(value, "dp")

    def gather_seq(self, block):
        return lax.all_gather(block, "seq")

    def to_strip(self, parts):
        return lax.all_to_all(parts, "seq", split_axis=0, concat_axis=0, tiled=True)

    def from_strip(self, parts):
        return lax.all_to_all(parts, "seq", split_axis=0, concat_axis=0, tiled=True)

    def owners(self):
        return jnp.arange(self.seq, dtype=jnp.int32)


class Paths(Plain):
    def __init__(self, dp, seq):
        super().__init__(dp, seq)
        self.me = self.dp_at * seq + self.seq_at
        self.low = self.me & 7
        self.z = self.me >> 3

    def swap(self, value, mask):
        return lax.ppermute(value, BOTH, [(d, d ^ mask) for d in range(32)])

    def climb(self, value, steps):
        return lax.ppermute(value, BOTH, [(d, (d + 8 * steps) % 32) for d in range(32)])

    def columns(self, block):
        rows = block.shape[0] // 4
        part = lax.dynamic_slice_in_dim(block, self.seq_at * rows, rows, 0)[None]
        column = jnp.concatenate([part] + [self.climb(part, k) for k in (1, 2, 3)], axis=0)
        near = [column] + [self.swap(column, mask) for mask in (2, 4, 6)]
        return near + [self.swap(v, 1) for v in near]

    def gather_rows(self, block):
        whole = place(self.tile_order()[0].astype(jnp.int32), *self.columns(block))
        return whole.reshape(-1, block.shape[1])

    def gather_tiles(self, block):
        return [v.reshape(-1, v.shape[-1]) for v in self.columns(block)]

    def tile_order(self):
        masks = (0, 2, 4, 6, 1, 3, 5, 7)
        order = [((self.z - k) & 3) * 8 + (self.low ^ mask) for mask in masks for k in range(4)]
        piece = jnp.arange(32)
        mask = (piece & 7) ^ self.low
        tile = (mask >> 1) + 4 * (mask & 1)
        return jnp.stack(order), tile * 4 + ((self.z - (piece >> 3)) & 3)

    def reduce_tiles(self, tiles):
        half = [
            tiles[at].astype(F32) + self.swap(tiles[at + 4], 1).astype(F32) for at in range(4)
        ]
        total = half[0]
        for at in (1, 2, 3):
            total = total + self.swap(half[at].astype(BF), 2 * at).astype(F32)
        levels = jnp.split(total, 4)
        result = levels[0]
        for k in (1, 2, 3):
            result = result + self.climb(levels[k].astype(BF), -k).astype(F32)
        return result

    def gather_vector(self, block):
        parts = [block] + [self.swap(block, 4 * k) for k in range(1, 8)]
        return jnp.stack(parts)[jnp.arange(8) ^ self.dp_at].reshape(-1)

    def reduce_rows(self, grad):
        rows, width = grad.shape[0] // 32, grad.shape[1]
        core, x, y = self.low & 1, (self.low >> 1) & 1, self.low >> 2
        cut = grad.reshape(16, 2, rows, width)
        pick = lambda at: lax.dynamic_index_in_dim(cut, at, 1, keepdims=False)
        half = pick(core).astype(F32) + self.swap(pick(1 - core).astype(BF), 1).astype(F32)
        half = half.reshape(4, 4, rows, width)
        place_xy = y * 2 + x
        quarter = lambda mask: lax.dynamic_index_in_dim(half, place_xy ^ mask, 1, keepdims=False)
        total = quarter(0)
        for mask in (1, 2, 3):
            total = total + self.swap(quarter(mask).astype(BF), 2 * mask).astype(F32)
        level = lambda k: lax.dynamic_index_in_dim(total, (self.z + k) & 3, 0, keepdims=False)
        result = level(0)
        for k in (1, 2, 3):
            result = result + self.climb(level(k).astype(BF), k).astype(F32)
        return result

    def sum_tree(self, value, masks):
        parts = [value] + [self.swap(value, mask) for mask in masks]
        while len(parts) > 1:
            parts = [parts[at] + parts[at + 1] for at in range(0, len(parts), 2)]
        return parts[0]

    def sum_all(self, value):
        return self.sum_tree(self.sum_tree(value, (1, 2, 3)), range(4, 32, 4))

    def sum_dp(self, value):
        rows = value.shape[0] // 8
        y = self.low >> 2
        halves = value.reshape((2, 4, rows) + value.shape[1:])
        pick = lambda at: lax.dynamic_index_in_dim(halves, at, 0, keepdims=False)
        half = pick(y) + self.swap(pick(1 - y), 4)
        level = lambda k: lax.dynamic_index_in_dim(half, (self.z + k) & 3, 0, keepdims=False)
        share = level(0)
        for k in (1, 2, 3):
            share = share + self.climb(level(k), k)
        column = jnp.stack([share] + [self.climb(share, k) for k in (1, 2, 3)])
        other = self.swap(column, 4)
        order = [y_at * 4 + ((self.z - k) & 3) for y_at in (y, 1 - y) for k in range(4)]
        return place(jnp.stack(order).astype(jnp.int32), column, other).reshape(value.shape)

    def gather_seq(self, block):
        first = jnp.stack([block, self.swap(block, 2)])
        second = self.swap(first, 1)
        order = [self.seq_at ^ mask for mask in (0, 2, 1, 3)]
        return place(jnp.stack(order).astype(jnp.int32), first, second)

    def exchange(self, parts, first):
        return [first] + [
            self.swap(lax.dynamic_index_in_dim(parts, self.seq_at ^ k, 0, keepdims=False), k)
            for k in (1, 2, 3)
        ]

    def to_strip(self, parts):
        own = lax.dynamic_index_in_dim(parts, self.seq_at, 0, keepdims=False)
        return jnp.stack(self.exchange(parts, own))

    def from_strip(self, parts):
        back = [parts[0]] + [self.swap(parts[k], k) for k in (1, 2, 3)]
        order = [self.seq_at ^ k for k in range(4)]
        return place(jnp.stack(order).astype(jnp.int32), *[v[None] for v in back])

    def owners(self):
        return jnp.arange(4, dtype=jnp.int32) ^ self.seq_at


def forward_kernel(mask_ref, q_ref, k_ref, v_ref, out_ref):
    keep = mask_ref[...] > 0.0
    for head in range(2):
        at = slice(64 * head, 64 * head + 64)
        scores = contract_cols(q_ref[:, at] * BF(0.125), k_ref[:, at])
        scores = jnp.where(keep, scores, NEG_BIG)
        raised = jnp.exp(scores - jnp.max(scores, axis=1, keepdims=True))
        totals = jnp.sum(raised, axis=1, keepdims=True)
        softmaxed = (raised * (1.0 / totals)).astype(BF)
        mixed = jnp.dot(softmaxed, v_ref[:, at], preferred_element_type=F32)
        out_ref[:, at] = mixed.astype(BF)


def backward_kernel(mask_ref, q_ref, k_ref, v_ref, up_ref, dq_ref, dk_ref, dv_ref, sums_ref):
    keep = mask_ref[...] > 0.0
    for head in range(2):
        at = slice(64 * head, 64 * head + 64)
        queries, keys_in, upstream = q_ref[:, at] * BF(0.125), k_ref[:, at], up_ref[:, at]
        scores = jnp.where(keep, contract_cols(keys_in, queries), NEG_BIG)
        raised = jnp.exp(scores - jnp.max(scores, axis=0, keepdims=True))
        softmaxed = raised * (1.0 / jnp.sum(raised, axis=0, keepdims=True))
        dprob = contract_cols(v_ref[:, at], upstream)
        weighted = jnp.sum(softmaxed * dprob, axis=0, keepdims=True)
        dscore = (softmaxed * (dprob - weighted)).astype(BF)
        dvalue = jnp.dot(softmaxed.astype(BF), upstream, preferred_element_type=F32).astype(BF)
        dkey = jnp.dot(dscore, queries, preferred_element_type=F32).astype(BF)
        dquery = (contract_rows(dscore, keys_in) * 0.125).astype(BF)
        dq_ref[:, at], dk_ref[:, at], dv_ref[:, at] = dquery, dkey, dvalue
        sums_ref[0:1, at] = jnp.sum(dquery.astype(F32), axis=0, keepdims=True)
        sums_ref[1:2, at] = jnp.sum(dvalue.astype(F32), axis=0, keepdims=True)


def head_pair(rows, shift):
    return pl.BlockSpec((rows, 128), lambda pair: (0, pair + shift))


def attend_forward(projected, key_mask):
    rows = projected.shape[0]
    return pl.pallas_call(
        forward_kernel,
        grid=(HEADS // 2,),
        out_shape=jax.ShapeDtypeStruct((rows, D), BF),
        in_specs=[pl.BlockSpec((1, rows), lambda pair: (0, 0))]
        + [head_pair(rows, HEADS // 2 * part) for part in range(3)],
        out_specs=head_pair(rows, 0),
        compiler_params=pltpu.CompilerParams(vmem_limit_bytes=VMEM_BYTES),
    )(key_mask.astype(F32)[None], projected, projected, projected)


def attend_backward(projected, key_mask, upstream):
    rows = projected.shape[0]
    return pl.pallas_call(
        backward_kernel,
        grid=(HEADS // 2,),
        out_shape=[jax.ShapeDtypeStruct((rows, D), BF)] * 3 + [jax.ShapeDtypeStruct((8, D), F32)],
        in_specs=[pl.BlockSpec((rows, 1), lambda pair: (0, 0))]
        + [head_pair(rows, HEADS // 2 * part) for part in range(3)]
        + [head_pair(rows, 0)],
        out_specs=[head_pair(rows, 0)] * 3 + [head_pair(8, 0)],
        compiler_params=pltpu.CompilerParams(vmem_limit_bytes=VMEM_BYTES),
    )(key_mask.astype(F32)[:, None], projected, projected, projected, upstream)


def upper_tail(values):
    t = 1.0 / (1.0 + 0.5 * values)
    series = 0.17087277
    for factor in (
        -0.82215223, 1.48851587, -1.13520398, 0.27886807, -0.18628806,
        0.09678418, 0.37409196, 1.00002368, -1.26551223,
    ):
        series = series * t + factor
    return t * jnp.exp(series - values * values)


def mlp_kernel(*refs):
    h_ref, up_ref, bias_ref = refs[:3]
    first_in, second_in = refs[3 : 3 + TILES], refs[3 + TILES : 3 + 2 * TILES]
    refs = refs[3 + 2 * TILES :]
    out_ref, dh_ref, dbias_ref = refs[:3]
    first_out, second_out = refs[3 : 3 + TILES], refs[3 + TILES : 3 + 2 * TILES]
    first, second, dfirst, dsecond, in_sem, out_sem = refs[3 + 2 * TILES :]
    loads, stores = [], []
    for tile in range(TILES):
        for kind, (source, held) in enumerate(((first_in, first), (second_in, second))):
            loads.append(
                pltpu.make_async_copy(source[tile], held.at[tile], in_sem.at[2 * tile + kind])
            )
            loads[-1].start()
    hidden, upstream = h_ref[...], up_ref[...]
    for tile in range(TILES):
        loads[2 * tile].wait()
        loads[2 * tile + 1].wait()
        w_first, w_second = first[tile], second[tile]
        width = w_first.shape[0]
        at = slice(tile * width, (tile + 1) * width)
        before = contract_cols(hidden, w_first) + bias_ref[:, at]
        dact = contract_cols(upstream, w_second)
        tail = 0.5 * upper_tail(jnp.abs(before) * math.sqrt(0.5))
        below = jnp.where(before < 0.0, tail, 1.0 - tail)
        slope = below + before * (jnp.exp(-0.5 * before * before) * (1.0 / math.sqrt(2.0 * math.pi)))
        active = (before * below).astype(BF)
        dbefore = (dact * slope).astype(BF)
        dbias_ref[:, at] = jnp.sum(dbefore.astype(F32), axis=0, keepdims=True)
        mixed = jnp.dot(active, w_second, preferred_element_type=F32)
        dhidden = jnp.dot(dbefore, w_first, preferred_element_type=F32)
        if tile == 0:
            out_ref[...], dh_ref[...] = mixed, dhidden
        else:
            out_ref[...] += mixed
            dh_ref[...] += dhidden
        dfirst[tile] = contract_rows(dbefore, hidden).astype(BF)
        dsecond[tile] = contract_rows(active, upstream).astype(BF)
        for kind, (held, target) in enumerate(((dfirst, first_out), (dsecond, second_out))):
            stores.append(
                pltpu.make_async_copy(held.at[tile], target[tile], out_sem.at[2 * tile + kind])
            )
            stores[-1].start()
    for store in stores:
        store.wait()


def mlp(hidden, upstream, bias, first, second):
    rows, tile = hidden.shape[0], first[0].shape
    vmem, anywhere = pl.BlockSpec(memory_space=pltpu.VMEM), pl.BlockSpec(memory_space=pl.ANY)
    result = pl.pallas_call(
        mlp_kernel,
        out_shape=[jax.ShapeDtypeStruct((rows, D), F32)] * 2
        + [jax.ShapeDtypeStruct((1, TILES * tile[0]), F32)]
        + [jax.ShapeDtypeStruct(tile, BF)] * (2 * TILES),
        in_specs=[vmem] * 3 + [anywhere] * (2 * TILES),
        out_specs=[vmem] * 3 + [anywhere] * (2 * TILES),
        scratch_shapes=[pltpu.VMEM((TILES,) + tile, BF)] * 4
        + [pltpu.SemaphoreType.DMA((2 * TILES,))] * 2,
        compiler_params=pltpu.CompilerParams(vmem_limit_bytes=VMEM_BYTES),
    )(hidden, upstream, bias[None], *first, *second)
    return result[0], result[1], result[2][0], result[3 : 3 + TILES], result[3 + TILES :]


def orthogonal(block, gram_sum):
    a, b, c = NS_COEFFS
    eye = jnp.eye(D, dtype=F32)
    inverse = 1.0 / (jnp.sqrt(jnp.sum(gram_sum * eye)) + 1e-07)
    gram = gram_sum * (inverse * inverse)
    rows = block * inverse
    for sweep in range(ITERS):
        precision = lax.Precision.HIGH
        dot = lambda p, q: jnp.dot(p, q, precision=precision, preferred_element_type=F32)
        square = dot(gram, gram)
        factor = b * gram + c * square
        if sweep < ITERS - 1:
            change = (2.0 * a) * factor + dot(factor, factor)
            gram = (a * a) * gram + dot(gram, change)
        rows = a * rows + jnp.dot(rows.astype(BF), factor.astype(BF), preferred_element_type=F32)
    return rows


def shards(
    patches, cotangent, lengths,
    w_qkv, w_out, w_fc1, w_fc2,
    mom_qkv, mom_out, mom_fc1, mom_fc2,
    vectors, vec_first, vec_second,
):
    strip_count, part_rows, width = patches.shape
    dp, seq = lax.axis_size("dp"), lax.axis_size("seq")
    assert strip_count == seq == 4
    net = (Paths if (dp, seq) == (8, 4) else Plain)(dp, seq)
    row_count = part_rows * seq

    strip = net.to_strip(patches).reshape(row_count, width)
    vec_low = net.gather_vector(lax.reduce_precision(vectors, 8, 7))
    w_query = net.gather_rows(w_qkv.astype(BF))
    w_proj = net.gather_rows(w_out.astype(BF))
    w_first = net.gather_tiles(w_fc1.astype(BF))
    w_second = net.gather_tiles(w_fc2.astype(BF))
    upstream_low = net.to_strip(cotangent).reshape(row_count, width)
    (gain_one, bias_one, query_bias, value_bias, out_bias,
     gain_two, bias_two, fc1_bias, fc2_bias) = split_vector(vec_low)

    owners = net.owners()
    places = (owners[:, None] * part_rows + jnp.arange(part_rows, dtype=jnp.int32)[None]).reshape(-1)
    length = lax.dynamic_index_in_dim(lengths, net.seq_at, 0, keepdims=False)
    key_mask = places < length

    flat = strip.astype(F32)
    normed_one, norm_one_pull = jax.vjp(layer_norm, flat, gain_one, bias_one)
    normed_low = normed_one.astype(BF)
    joint_bias = jnp.concatenate([query_bias, jnp.zeros_like(query_bias), value_bias])
    projected = (contract_cols(normed_low, w_query) + joint_bias).astype(BF)
    attn_low = attend_forward(projected, key_mask)
    first_sum = flat + contract_cols(attn_low, w_proj) + out_bias
    normed_two, norm_two_pull = jax.vjp(layer_norm, first_sum, gain_two, bias_two)
    normed_two_low = normed_two.astype(BF)
    there, back = net.tile_order()
    bias_there = fc1_bias.reshape(32, -1)[there].reshape(-1)
    mlp_out, grad_normed_two, grad_bias_there, grad_first, grad_second = mlp(
        normed_two_low, upstream_low, bias_there, w_first, w_second
    )
    second_sum = first_sum + mlp_out + fc2_bias
    mixed = net.from_strip(second_sum.astype(BF).reshape(seq, part_rows, width))

    upstream_f = upstream_low.astype(F32)
    grad_fc2_bias = jnp.sum(upstream_f, axis=0)
    grad_fc1_bias = grad_bias_there.reshape(32, -1)[back].reshape(-1)
    share_second = net.reduce_tiles(grad_second)
    share_first = net.reduce_tiles(grad_first)
    grad_sum_part, grad_gain_two, grad_bias_two = norm_two_pull(grad_normed_two)
    grad_first_sum = upstream_f + grad_sum_part
    grad_proj_low = grad_first_sum.astype(BF)
    grad_out_bias = jnp.sum(grad_first_sum, axis=0)
    grad_proj = contract_rows(grad_proj_low, attn_low)
    share_proj = net.reduce_rows(grad_proj.astype(BF))
    grad_attn = jnp.dot(grad_proj_low, w_proj, preferred_element_type=F32).astype(BF)
    *head_grads, head_sums = attend_backward(projected, key_mask, grad_attn)
    grad_projected = jnp.concatenate(head_grads, axis=1)
    grad_query = contract_rows(grad_projected, normed_low)
    share_query = net.reduce_rows(grad_query.astype(BF))
    grad_normed_one = jnp.dot(grad_projected, w_query, preferred_element_type=F32)
    grad_flat_part, grad_gain_one, grad_bias_one = norm_one_pull(grad_normed_one)
    grad_patches = (grad_first_sum + grad_flat_part).astype(BF)
    grad_patches = net.from_strip(grad_patches.reshape(seq, part_rows, width))
    grad_vector = net.sum_all(
        jnp.concatenate([
            grad_gain_one, grad_bias_one, head_sums[0], head_sums[1],
            grad_out_bias, grad_gain_two, grad_bias_two, grad_fc1_bias, grad_fc2_bias,
        ]).reshape(-1, 128)
    ).reshape(-1)

    shares = (share_query, share_proj, share_first, share_second)
    squares = sum(jnp.sum(share * share) for share in shares)
    total_squares = net.sum_all(jnp.full((8, 128), squares, F32))[0, 0]
    total_squares = total_squares + jnp.sum(grad_vector * grad_vector)
    grad_norm = jnp.sqrt(total_squares)
    clip = jnp.minimum(1.0, CLIP / (grad_norm + 1e-06))

    counts = [share.shape[0] for share in shares]
    packed = net.gather_seq(jnp.concatenate([share.astype(BF) for share in shares], axis=0))
    moments = (mom_qkv, mom_out, mom_fc1, mom_fc2)
    weights_old = (w_qkv, w_out, w_fc1, w_fc2)
    moments_new, start = [], 0
    for position, count in enumerate(counts):
        gradient = packed[:, start : start + count].reshape(seq * count, width).astype(F32)
        moments_new.append(MOMENTUM * moments[position] + clip * gradient)
        start += count

    most = max(moment.shape[0] for moment in moments)
    padded = [jnp.pad(m, ((0, most - m.shape[0]), (0, 0))) for m in moments_new]
    mine = padded[0]
    for position in range(1, 4):
        mine = jnp.where(net.seq_at == position, padded[position], mine)
    mine_low = mine.astype(BF)
    gram_part = contract_rows(mine_low, mine_low)
    third = width // 3
    blocks = [(i, j) for i in range(3) for j in range(i, 3)]
    upper = [gram_part[third * i : third * (i + 1), third * j : third * (j + 1)] for i, j in blocks]
    summed = net.sum_dp(jnp.concatenate(upper, axis=0)).reshape(6, third, third)
    lookup = {pair: summed[at] for at, pair in enumerate(blocks)}
    gram = jnp.concatenate([
        jnp.concatenate([lookup[i, j] if i <= j else lookup[j, i].T for j in range(3)], axis=1)
        for i in range(3)
    ], axis=0)
    ortho = net.gather_seq(orthogonal(mine, gram).astype(BF))

    row_totals = (3 * D, D, FF, FF)
    results = []
    for position in range(4):
        rate = MATRIX_RATES[position]
        ratio = math.sqrt(row_totals[position] / D)
        weight = weights_old[position]
        results.append(moments_new[position])
        results.append(
            weight * (1.0 - rate * DECAY)
            - rate * ratio * ortho[position, : weight.shape[0]].astype(F32)
        )
    entries = vectors.shape[0]
    vector_grad = clip * lax.dynamic_slice_in_dim(grad_vector, net.dp_at * entries, entries, 0)
    first_new = BETA_ONE * vec_first + (1.0 - BETA_ONE) * vector_grad
    second_new = BETA_TWO * vec_second + (1.0 - BETA_TWO) * vector_grad * vector_grad
    first_hat = first_new / (1.0 - BETA_ONE**ADAM_STEP)
    second_hat = second_new / (1.0 - BETA_TWO**ADAM_STEP)
    vectors_new = vectors - VEC_RATE * first_hat / (jnp.sqrt(second_hat) + 1e-08)
    return (mixed, grad_patches, grad_norm, *results, first_new, second_new, vectors_new)


def solution(mesh):
    rows, flat, full = P("dp", None), P("dp"), P("dp", "seq", None)
    return jax.shard_map(
        shards,
        mesh=mesh,
        in_specs=(full, full, flat) + (rows,) * 8 + (flat,) * 3,
        out_specs=(full, full, P()) + (rows,) * 8 + (flat,) * 3,
        check_vma=False,
    )
```

```python
import functools
import math

import jax
import jax.numpy as jnp
from jax import lax
from jax.experimental import pallas as pl
from jax.experimental.pallas import tpu as pltpu
from jax.sharding import PartitionSpec as P

D = 768
FF = 3072
HEADS = 12
ITERS = 5
ADAM_STEP = 10

NEG_BIG = -1e30
LN_EPS = 1e-06
NS_COEFFS = (3.4445, -4.775, 2.0315)
MOMENTUM = 0.5
CLIP = 1.0
DECAY = 0.01
MATRIX_RATES = (1.0, 3.0, 1.0, 0.6)
VEC_RATE = 0.1
BETA_ONE = 0.5
BETA_TWO = 0.5
ROWS_LAST = (((0,), (0,)), ((), ()))
COLS_LAST = (((1,), (1,)), ((), ()))
BOTH = ("dp", "seq")
VMEM_BYTES = 56 * 1024 * 1024
PIECES = 32
BF = jnp.bfloat16
F32 = jnp.float32


def layer_norm(values, gain, offset):
    centre = values - jnp.mean(values, axis=-1, keepdims=True)
    spread = jnp.mean(centre * centre, axis=-1, keepdims=True)
    return centre * lax.rsqrt(spread + LN_EPS) * gain + offset


def split_vector(vector):
    bounds = [0, D, 2 * D, 3 * D, 4 * D, 5 * D, 6 * D, 7 * D, 7 * D + FF, 8 * D + FF]
    return [vector[bounds[position] : bounds[position + 1]] for position in range(9)]


def contract_rows(left, right):
    return lax.dot_general(left, right, ROWS_LAST, preferred_element_type=F32)


def contract_cols(left, right):
    return lax.dot_general(left, right, COLS_LAST, preferred_element_type=F32)


def after(value, *others):
    return lax.optimization_barrier((value,) + others)[0]


def cost(microseconds):
    return pl.CostEstimate(
        flops=int(1e9 * microseconds), bytes_accessed=int(3e6 * microseconds), transcendentals=0
    )


def place_kernel(order_ref, *refs):
    sources, out, sem = refs[:-2], refs[-2], refs[-1]
    copies = []
    for source in sources:
        for piece in range(source.shape[0]):
            at = len(copies)
            copies.append(pltpu.make_async_copy(source.at[piece], out.at[order_ref[at]], sem.at[at]))
            copies[-1].start()
    for copy in copies:
        copy.wait()


def place(order, *sources):
    count = sum(source.shape[0] for source in sources)
    piece = sources[0].shape[1:]
    return pl.pallas_call(
        place_kernel,
        out_shape=jax.ShapeDtypeStruct((count,) + piece, sources[0].dtype),
        in_specs=[pl.BlockSpec(memory_space=pltpu.SMEM)]
        + [pl.BlockSpec(memory_space=pl.ANY)] * len(sources),
        out_specs=pl.BlockSpec(memory_space=pltpu.VMEM),
        scratch_shapes=[pltpu.SemaphoreType.DMA((count,))],
        cost_estimate=cost(0.3),
        compiler_params=pltpu.CompilerParams(vmem_limit_bytes=VMEM_BYTES),
    )(order, *sources)


class Plain:
    def __init__(self, dp, seq):
        self.dp, self.seq = dp, seq
        self.dp_at, self.seq_at = lax.axis_index("dp"), lax.axis_index("seq")
        self.owned = self.seq_at

    def piece(self, block):
        rows = block.shape[0] // self.seq
        return lax.dynamic_slice_in_dim(block, self.seq_at * rows, rows, 0)

    def gather_rows(self, blocks, vector):
        self.rows = [lax.all_gather(block, "dp", axis=0, tiled=True) for block in blocks]
        return lax.all_gather(vector, "dp", axis=0, tiled=True), None

    def gather_whole(self, block):
        return lax.all_gather(self.piece(block), BOTH).reshape(-1, block.shape[1])

    def gather_packed(self, blocks, first):
        wholes = [self.gather_whole(block).reshape(8, 4, -1, D) for block in blocks]
        self.packed = list(jnp.concatenate(wholes, axis=2))

    def later(self, value):
        return value

    def placed_rows(self, first):
        return self.rows

    def gather_diagonal(self, first):
        pass

    def packed_part(self, at):
        return self.packed[at]

    def order(self):
        return jnp.arange(PIECES), jnp.arange(PIECES)

    def reduce(self, near, far):
        whole = jnp.concatenate([near, far], axis=0).reshape(-1, D).astype(F32)
        return lax.psum_scatter(whole, BOTH, scatter_dimension=0, tiled=True)

    def hidden_ready(self, at, grads):
        self.hidden = getattr(self, "hidden", {}) | dict(zip(at, grads))

    def send_diagonal(self):
        return ()

    def send_neighbours(self):
        return ()

    def proj_ready(self, near, far):
        self.proj = (near, far)
        return ()

    def query_ready(self, near, far):
        whole = jnp.stack([self.hidden[at] for at in range(8)])
        first, second = [self.reduce(whole[:4, :, kind], whole[4:, :, kind]) for kind in range(2)]
        return self.reduce(near, far), self.reduce(*self.proj), first, second

    def sum_all(self, value):
        return lax.psum(value, BOTH)

    def to_owner(self, parts):
        return lax.all_to_all(parts, "seq", split_axis=0, concat_axis=0, tiled=True)

    def to_owner_and_sum(self, parts, value):
        return self.to_owner(parts), lax.psum(value, BOTH)

    def sum_owner(self, value, *others):
        return jnp.arange(8), lax.psum(value, "dp").reshape(2, 4, -1, value.shape[-1])

    def update(self, moments, shares, clip):
        result = []
        for moment, share in zip(moments, shares):
            gradient = lax.all_gather(share, "seq", axis=0, tiled=True)
            result.append(MOMENTUM * moment + clip * gradient)
        return result

    def finish(self, weights, rows):
        whole = lax.all_gather(rows, "seq")
        result = []
        for at, weight in enumerate(weights):
            keep, step = weight_factors(at)
            part = whole[at].reshape(self.seq, -1, D)[:, : weight.shape[0] // self.seq]
            result.append(weight * keep - step * part.reshape(weight.shape).astype(F32))
        return result

    def to_strip(self, parts):
        return lax.all_to_all(parts, "seq", split_axis=0, concat_axis=0, tiled=True)

    def query_there(self):
        return ()

    def from_strip(self, parts):
        return lax.all_to_all(parts, "seq", split_axis=0, concat_axis=0, tiled=True)

    def owners(self):
        return jnp.arange(self.seq, dtype=jnp.int32)


class Paths(Plain):
    def __init__(self, dp, seq):
        super().__init__(dp, seq)
        self.me = self.dp_at * seq + self.seq_at
        self.low = self.me & 7
        self.z = self.me >> 3
        self.owned = (self.me >> 1) & 3

    def swap(self, value, mask):
        return lax.ppermute(value, BOTH, [(d, d ^ mask) for d in range(32)])

    def climb(self, value, steps):
        return lax.ppermute(value, BOTH, [(d, (d + 8 * steps) % 32) for d in range(32)])

    def order(self):
        masks = (0, 2, 4, 6, 1, 3, 5, 7)
        order = [((self.z - k) & 3) * 8 + (self.low ^ mask) for mask in masks for k in range(4)]
        piece = jnp.arange(PIECES)
        mask = (piece & 7) ^ self.low
        tile = (mask >> 1) + 4 * (mask & 1)
        return jnp.stack(order), tile * 4 + ((self.z - (piece >> 3)) & 3)

    def column(self, part):
        part = part[None]
        return jnp.concatenate([part] + [self.climb(part, k) for k in (1, 2, 3)], axis=0)

    def gather_rows(self, blocks, vector):
        self.cuts = [block.shape[0] // 4 for block in blocks]
        part = jnp.concatenate([self.piece(block) for block in blocks], axis=0)[None]
        column = jnp.concatenate([part] + [self.climb(part, k) for k in (1, 2, 3)], axis=0)
        near = [column] + [self.swap(column, mask) for mask in (2, 4, 6)]
        held = vector[None]
        held = jnp.concatenate([held, self.swap(held, 4)], axis=0)
        first = held = jnp.concatenate([held, self.swap(after(held, column), 8)], axis=0)
        held = jnp.concatenate([held, self.swap(after(held, near[1]), 16)], axis=0)
        self.arrived = near[1:]
        self.pieces = near + [self.swap(v, 1) for v in near]
        return held[jnp.arange(8) ^ self.dp_at].reshape(-1), first

    def placed_rows(self, first):
        self.pieces[7] = after(self.pieces[7], first)
        whole = place(self.order()[0].astype(jnp.int32), *self.pieces)
        cut = self.cuts[0]
        return whole[:, :cut].reshape(-1, D), whole[:, cut:].reshape(-1, D)

    def later(self, value):
        return after(value, *self.arrived)

    def gather_packed(self, blocks, first):
        part = jnp.concatenate([self.piece(block) for block in blocks], axis=0)
        held = after(part, first)[None]
        for steps in (1, 2):
            held = jnp.concatenate([held, self.climb(held, steps)], axis=0)
        sent = self.later(held)
        self.packed = [held, self.swap(sent, 2), self.swap(sent, 4), None]

    def gather_diagonal(self, first):
        self.packed[3] = self.swap(after(self.packed[0], first, *self.packed[1:3]), 6)
        self.packed += [self.swap(v, 1) for v in self.packed]

    def packed_part(self, at):
        return self.packed[at]

    def both_cores(self, near, far):
        return near.astype(F32) + far.astype(F32)

    def hidden_ready(self, at, grads):
        held = getattr(self, "hidden", {})
        for place_at, grad in zip(at, grads):
            held[place_at] = self.swap(grad, 1) if place_at >= 4 else grad
        self.hidden = held

    def half(self, at):
        return self.both_cores(self.hidden[at], self.hidden[at + 4])

    def send_diagonal(self):
        sent = self.half(3).astype(BF)
        self.received.append(self.swap(sent, 6))
        return (sent,)

    def send_neighbours(self):
        sent = [self.half(at).astype(BF) for at in (1, 2)]
        self.received = [self.swap(sent[0], 2), self.swap(sent[1], 4)]
        return sent

    def proj_ready(self, near, far):
        self.proj = [near.reshape(4, 4, -1, D), self.swap(far, 1).reshape(4, 4, -1, D)]
        return (self.proj[1],)

    def query_ready(self, near, far):
        far = after(far, *self.received)
        query = [near.reshape(4, 4, -1, D), self.swap(far, 1).reshape(4, 4, -1, D)]
        joint = lambda at: jnp.concatenate(
            [self.both_cores(near[at], far[at]) for near, far in (query, self.proj)], axis=1
        )
        sent = [joint(at).astype(BF) for at in (1, 2, 3)]
        received = [self.swap(sent[at - 1], 2 * at) for at in (1, 2, 3)]
        self.query_received = received
        hidden = self.both_cores(self.hidden[0], self.hidden[4])
        for part in self.received:
            hidden = hidden + part.astype(F32)
        hidden = hidden.reshape(4, -1, D)
        low = hidden.astype(BF)
        both = hidden[0]
        climbed = [self.climb(low[k], -k) for k in (1, 2, 3)]
        total = joint(0)
        for part in received:
            total = total + part.astype(F32)
        low = after(total.astype(BF), *climbed)
        last = total[0]
        for k in (1, 2, 3):
            last = last + self.climb(low[k], -k).astype(F32)
            both = both + climbed[k - 1].astype(F32)
        cut, rows = query[0].shape[2], both.shape[0] // 2
        return last[:cut], last[cut:], both[:rows], both[rows:]

    def sum_all(self, value):
        for mask in (1, 8, 16, 2, 4):
            if mask == 2:
                value = after(value, *self.query_received)
            value = value + self.swap(value, mask)
        return value

    def pick(self, parts, at):
        return lax.dynamic_index_in_dim(parts, at, 0, keepdims=False)

    def to_owner(self, parts):
        own = self.pick(parts, self.owned)
        return jnp.stack(
            [own] + [self.swap(self.pick(parts, self.owned ^ j), 2 * j) for j in (1, 2, 3)]
        )

    def to_owner_and_sum(self, parts, value):
        terms, rest = [], value
        for _ in range(3):
            terms.append(lax.reduce_precision(rest, 8, 7))
            rest = rest - terms[-1]
        extra = jnp.concatenate([jnp.full((1, D), term, F32) for term in terms] + [jnp.zeros((5, D), F32)])
        extra = jnp.broadcast_to(extra.astype(BF)[None], (4, 8, D))
        whole = self.to_owner(jnp.concatenate([parts, extra], axis=1))
        count = parts.shape[1]
        sums = whole[:, count : count + 3, :128].astype(F32)
        sums = (sums[:, 0] + sums[:, 1]) + sums[:, 2]
        total = ((sums[0] + sums[1]) + (sums[2] + sums[3]))[None]
        total = total + self.swap(total, 1)
        one, two, three = [self.climb(total, k) for k in (1, 2, 3)]
        return whole[:, :count], ((total + two) + (one + three))[0, 0]

    def sum_owner(self, value, *others):
        rows, core = value.shape[0] // 8, self.low & 1
        halves = value.reshape((2, 4, rows) + value.shape[1:])
        half = self.pick(halves, core) + self.swap(self.pick(halves, 1 - core), 1)
        level = lambda k: self.pick(half, (self.z + k) & 3)
        share = level(0)
        for k in (1, 2, 3):
            share = share + self.climb(level(k), k)
        share = after(share, *others)
        column = jnp.stack([share] + [self.climb(share, k) for k in (1, 2, 3)])
        order = [at * 4 + ((self.z - k) & 3) for at in (core, 1 - core) for k in range(4)]
        return jnp.stack(order), jnp.stack([column, self.swap(column, 1)])

    def update(self, moments, shares, clip):
        block = jnp.concatenate([share.astype(BF) for share in shares], axis=0)
        first = jnp.stack([block, self.swap(block, 2)])
        second = self.swap(first, 1)
        places = [((q ^ self.seq_at) >> 1) + 2 * ((q ^ self.seq_at) & 1) for q in range(4)]
        return update_moments(jnp.stack(places), clip, first, second, moments)

    def finish(self, weights, rows):
        parts = rows.reshape(4, -1, D)
        mine, theirs = parts[:2], parts[2:]
        near = jnp.stack([mine, self.swap(mine, 2), self.swap(theirs, 4), self.swap(theirs, 6)])
        far = self.swap(near, 1)
        x, core = (self.low >> 1) & 1, self.low & 1
        places = []
        for matrix in range(4):
            j = self.owned ^ matrix
            for q in range(4):
                places.append((core ^ (q & 1)) * 8 + j * 2 + (x ^ (j & 1) ^ (q >> 1)))
        cut = (8,) + parts.shape[1:]
        return update_weights(jnp.stack(places), near.reshape(cut), far.reshape(cut), weights)

    def exchange(self, parts, first):
        return [first] + [self.swap(self.pick(parts, self.seq_at ^ k), k) for k in (1, 2, 3)]

    def to_strip(self, parts):
        return jnp.stack(self.exchange(parts, self.pick(parts, self.seq_at)))

    def query_there(self):
        return self.query_received

    def from_strip(self, parts):
        back = [parts[0]] + [self.swap(parts[k], k) for k in (1, 2, 3)]
        order = [self.seq_at ^ k for k in range(4)]
        return place(jnp.stack(order).astype(jnp.int32), *[v[None] for v in back])

    def owners(self):
        return jnp.arange(4, dtype=jnp.int32) ^ self.seq_at


def weight_factors(at):
    rate = MATRIX_RATES[at]
    return 1.0 - rate * DECAY, rate * math.sqrt((3 * D, D, FF, FF)[at] / D)


def update_moments_kernel(place_ref, clip_ref, near, far, *refs):
    moments, results, held, sem = refs[:4], refs[4:8], refs[8], refs[9]
    copies = [
        pltpu.make_async_copy(source, held.at[pl.ds(2 * at, 2)], sem.at[at])
        for at, source in enumerate((near, far))
    ]
    for copy in copies:
        copy.start()
    for copy in copies:
        copy.wait()
    for q in range(4):
        block = held[place_ref[q]].astype(F32) * clip_ref[0]
        start = 0
        for moment, result in zip(moments, results):
            rows = moment.shape[0] // 4
            at = slice(q * rows, (q + 1) * rows)
            result[at, :] = MOMENTUM * moment[at, :] + block[start : start + rows]
            start += rows


def update_moments(places, clip, near, far, moments):
    vmem, smem = pl.BlockSpec(memory_space=pltpu.VMEM), pl.BlockSpec(memory_space=pltpu.SMEM)
    anywhere = pl.BlockSpec(memory_space=pl.ANY)
    return pl.pallas_call(
        update_moments_kernel,
        out_shape=[jax.ShapeDtypeStruct(moment.shape, F32) for moment in moments],
        in_specs=[smem, smem, anywhere, anywhere] + [vmem] * 4,
        out_specs=[vmem] * 4,
        scratch_shapes=[
            pltpu.VMEM((4,) + near.shape[1:], BF),
            pltpu.SemaphoreType.DMA((2,)),
        ],
        cost_estimate=cost(0.3),
        compiler_params=pltpu.CompilerParams(vmem_limit_bytes=VMEM_BYTES),
    )(places.astype(jnp.int32), clip.reshape(1), near, far, *moments)


def update_weights_kernel(place_ref, near, far, *refs):
    weights, results, held, sem = refs[:4], refs[4:8], refs[8], refs[9]
    copies = [
        pltpu.make_async_copy(source, held.at[pl.ds(8 * at, 8)], sem.at[at])
        for at, source in enumerate((near, far))
    ]
    for copy in copies:
        copy.start()
    for copy in copies:
        copy.wait()
    for matrix, (weight, result) in enumerate(zip(weights, results)):
        keep, step = weight_factors(matrix)
        rows = weight.shape[0] // 4
        for q in range(4):
            at = slice(q * rows, (q + 1) * rows)
            block = held[place_ref[4 * matrix + q]].astype(F32)
            result[at, :] = weight[at, :] * keep - step * block[:rows]


def update_weights(places, near, far, weights):
    vmem, smem = pl.BlockSpec(memory_space=pltpu.VMEM), pl.BlockSpec(memory_space=pltpu.SMEM)
    anywhere = pl.BlockSpec(memory_space=pl.ANY)
    return pl.pallas_call(
        update_weights_kernel,
        out_shape=[jax.ShapeDtypeStruct(weight.shape, F32) for weight in weights],
        in_specs=[smem, anywhere, anywhere] + [vmem] * 4,
        out_specs=[vmem] * 4,
        scratch_shapes=[
            pltpu.VMEM((16,) + near.shape[1:], BF),
            pltpu.SemaphoreType.DMA((2,)),
        ],
        cost_estimate=cost(0.3),
        compiler_params=pltpu.CompilerParams(vmem_limit_bytes=VMEM_BYTES),
    )(places.astype(jnp.int32), near, far, *weights)


def forward_kernel(mask_ref, q_ref, k_ref, v_ref, out_ref):
    keep = mask_ref[...] > 0.0
    for head in range(2):
        at = slice(64 * head, 64 * head + 64)
        scores = contract_cols(q_ref[:, at] * BF(0.125), k_ref[:, at])
        scores = jnp.where(keep, scores, NEG_BIG)
        raised = jnp.exp(scores - jnp.max(scores, axis=1, keepdims=True))
        totals = jnp.sum(raised, axis=1, keepdims=True)
        softmaxed = (raised * (1.0 / totals)).astype(BF)
        mixed = jnp.dot(softmaxed, v_ref[:, at], preferred_element_type=F32)
        out_ref[:, at] = mixed.astype(BF)


def write_pieces(order_ref, source, near_ref, far_ref):
    rows = near_ref.shape[1]
    for at in range(PIECES):
        target = near_ref if at < PIECES // 2 else far_ref
        piece = source[pl.ds(pl.multiple_of(order_ref[at] * rows, 8), rows), :]
        target[at % (PIECES // 2)] = piece.astype(BF)


def backward_kernel(
    order_ref, mask_ref, q_ref, k_ref, v_ref, up_ref, h_ref, wq_ref, wk_ref, wv_ref,
    near_ref, far_ref, dh_ref, sums_ref, grad,
):
    pair = pl.program_id(0)
    keep = mask_ref[...] > 0.0
    grads = [[], [], []]
    for head in range(2):
        at = slice(64 * head, 64 * head + 64)
        queries, keys_in, upstream = q_ref[:, at] * BF(0.125), k_ref[:, at], up_ref[:, at]
        scores = jnp.where(keep, contract_cols(keys_in, queries), NEG_BIG)
        raised = jnp.exp(scores - jnp.max(scores, axis=0, keepdims=True))
        softmaxed = raised * (1.0 / jnp.sum(raised, axis=0, keepdims=True))
        dprob = contract_cols(v_ref[:, at], upstream)
        weighted = jnp.sum(softmaxed * dprob, axis=0, keepdims=True)
        dscore = (softmaxed * (dprob - weighted)).astype(BF)
        grads[2].append(jnp.dot(softmaxed.astype(BF), upstream, preferred_element_type=F32))
        grads[1].append(jnp.dot(dscore, queries, preferred_element_type=F32))
        grads[0].append(contract_rows(dscore, keys_in) * 0.125)
    joint = [jnp.concatenate(parts, axis=1).astype(BF) for parts in grads]
    sums_ref[0:1, :] = jnp.sum(joint[0].astype(F32), axis=0, keepdims=True)
    sums_ref[1:2, :] = jnp.sum(joint[2].astype(F32), axis=0, keepdims=True)
    dhidden = jnp.zeros(dh_ref.shape, F32)
    for part, (piece, w_ref) in enumerate(zip(joint, (wq_ref, wk_ref, wv_ref))):
        rows = pl.ds(pl.multiple_of(part * D + pair * 128, 128), 128)
        grad[rows, :] = contract_rows(piece, h_ref[...])
        dhidden += jnp.dot(piece, w_ref[...], preferred_element_type=F32)

    @pl.when(pair == 0)
    def _():
        dh_ref[...] = dhidden

    @pl.when(pair > 0)
    def _():
        dh_ref[...] += dhidden

    @pl.when(pair == HEADS // 2 - 1)
    def _():
        write_pieces(order_ref, grad, near_ref, far_ref)


def head_pair(rows, shift):
    return pl.BlockSpec((rows, 128), lambda pair: (0, pair + shift))


def attend_forward(projected, key_mask):
    rows = projected.shape[0]
    return pl.pallas_call(
        forward_kernel,
        grid=(HEADS // 2,),
        out_shape=jax.ShapeDtypeStruct((rows, D), BF),
        in_specs=[pl.BlockSpec((1, rows), lambda pair: (0, 0))]
        + [head_pair(rows, HEADS // 2 * part) for part in range(3)],
        out_specs=head_pair(rows, 0),
        cost_estimate=cost(0.3),
        compiler_params=pltpu.CompilerParams(vmem_limit_bytes=VMEM_BYTES),
    )(key_mask.astype(F32)[None], projected, projected, projected)


def attend_backward(order, projected, key_mask, upstream, hidden, weight):
    rows, pairs = projected.shape[0], HEADS // 2
    whole = lambda *shape: pl.BlockSpec(shape, lambda pair: (0,) * len(shape))
    band = lambda part: pl.BlockSpec((128, D), lambda pair: (pair + pairs * part, 0))
    half = (PIECES // 2, 3 * D // PIECES, D)
    return pl.pallas_call(
        backward_kernel,
        grid=(pairs,),
        out_shape=[jax.ShapeDtypeStruct(half, BF)] * 2
        + [jax.ShapeDtypeStruct((rows, D), F32), jax.ShapeDtypeStruct((8, D), F32)],
        in_specs=[pl.BlockSpec(memory_space=pltpu.SMEM), whole(rows, 1)]
        + [head_pair(rows, pairs * part) for part in range(3)]
        + [head_pair(rows, 0), whole(rows, D)]
        + [band(part) for part in range(3)],
        out_specs=[whole(*half)] * 2 + [whole(rows, D), head_pair(8, 0)],
        scratch_shapes=[pltpu.VMEM((3 * D, D), F32)],
        cost_estimate=cost(0.3),
        compiler_params=pltpu.CompilerParams(vmem_limit_bytes=VMEM_BYTES),
    )(
        order, key_mask.astype(F32)[:, None], projected, projected, projected, upstream,
        hidden, weight, weight, weight,
    )


def middle_kernel(
    order_ref, sum_ref, dh_ref, up_ref, attn_ref, w_ref, gain_ref,
    dsum_ref, dattn_ref, near_ref, far_ref, sums_ref, grad,
):
    values = sum_ref[...]
    centre = values - jnp.mean(values, axis=1, keepdims=True)
    scale = lax.rsqrt(jnp.mean(centre * centre, axis=1, keepdims=True) + LN_EPS)
    normed = centre * scale
    dhidden = dh_ref[...]
    dnormed = dhidden * gain_ref[...]
    inner = jnp.mean(dnormed * normed, axis=1, keepdims=True)
    change = scale * (dnormed - jnp.mean(dnormed, axis=1, keepdims=True) - normed * inner)
    dsum = up_ref[...].astype(F32) + change
    dsum_ref[...] = dsum
    low = dsum.astype(BF)
    dattn_ref[...] = jnp.dot(low, w_ref[...], preferred_element_type=F32).astype(BF)
    grad[...] = contract_rows(low, attn_ref[...])
    write_pieces(order_ref, grad, near_ref, far_ref)
    sums_ref[0:1, :] = jnp.sum(dhidden * normed, axis=0, keepdims=True)
    sums_ref[1:2, :] = jnp.sum(dhidden, axis=0, keepdims=True)
    sums_ref[2:3, :] = jnp.sum(dsum, axis=0, keepdims=True)


def middle(order, first_sum, dhidden, upstream, attended, weight, gain):
    rows = first_sum.shape[0]
    half = (PIECES // 2, D // PIECES, D)
    vmem = pl.BlockSpec(memory_space=pltpu.VMEM)
    return pl.pallas_call(
        middle_kernel,
        out_shape=[
            jax.ShapeDtypeStruct((rows, D), F32),
            jax.ShapeDtypeStruct((rows, D), BF),
            jax.ShapeDtypeStruct(half, BF),
            jax.ShapeDtypeStruct(half, BF),
            jax.ShapeDtypeStruct((8, D), F32),
        ],
        in_specs=[pl.BlockSpec(memory_space=pltpu.SMEM)] + [vmem] * 6,
        out_specs=[vmem] * 5,
        scratch_shapes=[pltpu.VMEM((D, D), F32)],
        cost_estimate=cost(0.3),
        compiler_params=pltpu.CompilerParams(vmem_limit_bytes=VMEM_BYTES),
    )(order, first_sum, dhidden, upstream, attended, weight, gain[None])


def upper_tail(values):
    t = 1.0 / (1.0 + 0.5 * values)
    series = 0.17087277
    for factor in (
        -0.82215223, 1.48851587, -1.13520398, 0.27886807, -0.18628806,
        0.09678418, 0.37409196, 1.00002368, -1.26551223,
    ):
        series = series * t + factor
    return t * jnp.exp(series - values * values)


def mlp_kernel(first, arrays, h_ref, up_ref, bias_ref, *refs):
    if not first:
        (out_in, dh_in), refs = refs[:2], refs[2:]
    packed, (out_ref, dh_ref, dbias_ref), targets = refs[:arrays], refs[arrays : arrays + 3], refs[arrays + 3 : -2]
    held, sem = refs[-2:]
    pieces, rows = held.shape[1], held.shape[2]
    count, copies, start = pieces // 4, [], 0
    for source in packed:
        for kind in range(2):
            copy = pltpu.make_async_copy(
                source.at[:, pl.ds(kind * rows, rows)],
                held.at[kind, pl.ds(start, source.shape[0])],
                sem.at[len(copies)],
            )
            copy.start()
            copies.append(copy)
        start += source.shape[0]
    for copy in copies:
        copy.wait()
    hidden, upstream = h_ref[...], up_ref[...]
    w_first = held[0].reshape(pieces * rows, D)
    w_second = held[1].reshape(pieces * rows, D)
    before = contract_cols(hidden, w_first) + bias_ref[...]
    dact = contract_cols(upstream, w_second)
    tail = 0.5 * upper_tail(jnp.abs(before) * math.sqrt(0.5))
    below = jnp.where(before < 0.0, tail, 1.0 - tail)
    slope = below + before * (jnp.exp(-0.5 * before * before) * (1.0 / math.sqrt(2.0 * math.pi)))
    active = (before * below).astype(BF)
    dbefore = (dact * slope).astype(BF)
    dbias_ref[...] = jnp.sum(dbefore.astype(F32), axis=0, keepdims=True)
    mixed = jnp.dot(active, w_second, preferred_element_type=F32)
    dhidden = jnp.dot(dbefore, w_first, preferred_element_type=F32)
    out_ref[...] = mixed if first else out_in[...] + mixed
    dh_ref[...] = dhidden if first else dh_in[...] + dhidden
    for kind, grad in enumerate((contract_rows(dbefore, hidden), contract_rows(active, upstream))):
        grad = grad.astype(BF).reshape(count, 4, rows, D)
        for at, target in enumerate(targets):
            target[:, kind] = grad[at]


def mlp(hidden, upstream, bias, packed, sums):
    rows, piece = hidden.shape[0], FF // PIECES
    pieces, arrays = sum(part.shape[0] for part in packed), len(packed)
    vmem, anywhere = pl.BlockSpec(memory_space=pltpu.VMEM), pl.BlockSpec(memory_space=pl.ANY)
    return pl.pallas_call(
        functools.partial(mlp_kernel, not sums, arrays),
        out_shape=[jax.ShapeDtypeStruct((rows, D), F32)] * 2
        + [jax.ShapeDtypeStruct((1, pieces * piece), F32)]
        + [jax.ShapeDtypeStruct((4, 2, piece, D), BF)] * (pieces // 4),
        in_specs=[vmem] * (3 + len(sums)) + [anywhere] * arrays,
        out_specs=[vmem] * (3 + pieces // 4),
        scratch_shapes=[
            pltpu.VMEM((2, pieces, piece, D), BF),
            pltpu.SemaphoreType.DMA((2 * arrays,)),
        ],
        input_output_aliases={3: 0, 4: 1} if sums else {},
        cost_estimate=cost(0.3),
        compiler_params=pltpu.CompilerParams(vmem_limit_bytes=VMEM_BYTES),
    )(hidden, upstream, bias.reshape(1, -1), *sums, *packed)


THIRD = D // 3
BLOCKS = [(i, j) for i in range(3) for j in range(i, 3)]


def add_diagonal(value, shift):
    row_ids = lax.broadcasted_iota(jnp.int32, (THIRD, D), 0)
    col_ids = lax.broadcasted_iota(jnp.int32, (THIRD, D), 1)
    bands = [
        value[THIRD * i : THIRD * (i + 1)] + jnp.where(col_ids == row_ids + THIRD * i, shift, 0.0)
        for i in range(3)
    ]
    return jnp.concatenate(bands, axis=0)


def mean_of_diagonal(value):
    row_ids = lax.broadcasted_iota(jnp.int32, (THIRD, THIRD), 0)
    col_ids = lax.broadcasted_iota(jnp.int32, (THIRD, THIRD), 1)
    total = sum(value[THIRD * i : THIRD * (i + 1), THIRD * i : THIRD * (i + 1)] for i in range(3))
    return jnp.sum(jnp.where(row_ids == col_ids, total, 0.0), keepdims=True) * (1.0 / D)


def product(left, right, fine):
    (shift_l, rest_l), (shift_r, rest_r) = left, right
    parts_l, parts_r = parts_of(rest_l, fine), parts_of(rest_r, fine)
    rows = [[None] * 3 for _ in range(3)]
    for i in range(3):
        total = None
        for at, part in enumerate(parts_l):
            for other in parts_r[: fine - at]:
                term = jnp.dot(
                    part[THIRD * i : THIRD * (i + 1)], other[:, THIRD * i :],
                    preferred_element_type=F32,
                )
                total = term if total is None else total + term
        for j in range(i, 3):
            block = total[:, THIRD * (j - i) : THIRD * (j - i + 1)]
            rows[i][j] = block
            if j > i:
                rows[j][i] = block.T
    whole = jnp.concatenate([jnp.concatenate(row, axis=1) for row in rows], axis=0)
    return add_diagonal(whole + shift_l * rest_r + shift_r * rest_l, shift_l * shift_r)


def parts_of(value, count):
    high = value.astype(BF)
    return [high] if count == 1 else [high, (value - high.astype(F32)).astype(BF)]


def shifted(value):
    mean = mean_of_diagonal(value)
    return mean, add_diagonal(value, -mean)


def orthogonal_kernel(order_ref, pieces_ref, rows_ref, out_ref, packed):
    a, b, c = NS_COEFFS
    height = pieces_ref.shape[2]
    for at in range(8):
        target = pl.ds(pl.multiple_of(order_ref[at] * height, 8), height)
        packed[target, :] = pieces_ref[at // 4, at % 4]
    held = {pair: packed[THIRD * at : THIRD * (at + 1), :] for at, pair in enumerate(BLOCKS)}
    gram = jnp.concatenate([
        jnp.concatenate([held[i, j] if i <= j else held[j, i].T for j in range(3)], axis=1)
        for i in range(3)
    ], axis=0)
    inverse = 1.0 / (jnp.sqrt(mean_of_diagonal(gram) * D) + 1e-07)
    gram = gram * (inverse * inverse)
    rows = rows_ref[...] * inverse
    for sweep in range(ITERS):
        cut = shifted(gram)
        factor = b * gram + c * product(cut, cut, 2 if sweep in (2, 3) else 1)
        shift, rest = cut_factor = shifted(factor)
        rows = (a + shift) * rows + jnp.dot(
            rows.astype(BF), rest.astype(BF), preferred_element_type=F32
        )
        if sweep < ITERS - 1:
            fine = 2 if sweep in (2, 3) else 1
            change = (2.0 * a) * factor + product(cut_factor, cut_factor, fine)
            gram = (a * a) * gram + product(cut, shifted(change), 1 if sweep == 0 else 2)
    out_ref[...] = rows.astype(BF)


def orthogonal(order, pieces, rows):
    vmem = pl.BlockSpec(memory_space=pltpu.VMEM)
    return pl.pallas_call(
        orthogonal_kernel,
        out_shape=jax.ShapeDtypeStruct(rows.shape, BF),
        in_specs=[pl.BlockSpec(memory_space=pltpu.SMEM)] + [vmem] * 2,
        out_specs=vmem,
        scratch_shapes=[pltpu.VMEM((len(BLOCKS) * THIRD, THIRD), F32)],
        cost_estimate=cost(0.3),
        compiler_params=pltpu.CompilerParams(vmem_limit_bytes=VMEM_BYTES),
    )(order.astype(jnp.int32), pieces, rows)


def shards(
    patches, cotangent, lengths,
    w_qkv, w_out, w_fc1, w_fc2,
    mom_qkv, mom_out, mom_fc1, mom_fc2,
    vectors, vec_first, vec_second,
):
    strip_count, part_rows, width = patches.shape
    dp, seq = lax.axis_size("dp"), lax.axis_size("seq")
    assert strip_count == seq == 4
    net = (Paths if (dp, seq) == (8, 4) else Plain)(dp, seq)
    row_count = part_rows * seq

    strip = net.to_strip(patches).reshape(row_count, width)
    vec_low, first = net.gather_rows(
        [w_qkv.astype(BF), w_out.astype(BF)], lax.reduce_precision(vectors, 8, 7)
    )
    net.gather_packed([w_fc1.astype(BF), w_fc2.astype(BF)], first)
    upstream_low = net.to_strip(net.later(cotangent)).reshape(row_count, width)
    (gain_one, bias_one, query_bias, value_bias, out_bias,
     gain_two, bias_two, fc1_bias, fc2_bias) = split_vector(vec_low)
    flat = strip.astype(F32)
    normed_low = layer_norm(flat, gain_one, bias_one).astype(BF)
    w_query, w_proj = net.placed_rows(normed_low)

    owners = net.owners()
    places = (owners[:, None] * part_rows + jnp.arange(part_rows, dtype=jnp.int32)[None]).reshape(-1)
    length = lax.dynamic_index_in_dim(lengths, net.seq_at, 0, keepdims=False)
    key_mask = places < length
    there, back = net.order()
    order = there.astype(jnp.int32)

    _, norm_one_pull = jax.vjp(layer_norm, flat, gain_one, bias_one)
    joint_bias = jnp.concatenate([query_bias, jnp.zeros_like(query_bias), value_bias])
    projected = (contract_cols(normed_low, w_query) + joint_bias).astype(BF)
    attn_low = attend_forward(projected, key_mask)
    first_sum = flat + contract_cols(attn_low, w_proj) + out_bias
    normed_two_low = layer_norm(first_sum, gain_two, bias_two).astype(BF)
    net.gather_diagonal(normed_two_low)

    bias_there = fc1_bias.reshape(PIECES, -1)[there].reshape(8, -1)
    sums, grad_bias_there, tokens = [], {}, ()
    for parts in ((0, 4), (5, 6), (1, 2), (3, 7)):
        bias = jnp.concatenate([bias_there[at] for at in parts])
        packed = [net.packed_part(at) for at in parts]
        *sums, grad_bias, grads = (
            lambda out, dh, dbias, *grads: (out, dh, dbias, grads)
        )(*mlp(after(normed_two_low, *tokens), upstream_low, bias, packed, sums))
        grad_bias_there |= dict(zip(parts, grad_bias.reshape(len(parts), -1)))
        net.hidden_ready(parts, grads)
        tokens = net.send_neighbours() if parts == (1, 2) else ()
    second_sum = first_sum + sums[0] + fc2_bias
    mixed = net.from_strip(second_sum.astype(BF).reshape(seq, part_rows, width))
    grad_bias_there = jnp.stack([grad_bias_there[at] for at in range(8)]).reshape(PIECES, -1)
    grad_fc1_bias = grad_bias_there[back].reshape(-1)
    grad_fc2_bias = jnp.sum(upstream_low.astype(F32), axis=0)

    grad_first_sum, grad_attn, proj_near, proj_far, middle_sums = middle(
        order, first_sum, after(sums[1], *tokens), upstream_low, attn_low, w_proj, gain_two
    )
    tokens = (*net.proj_ready(proj_near, proj_far), *net.send_diagonal())
    query_near, query_far, grad_normed_one, head_sums = attend_backward(
        order, projected, key_mask, after(grad_attn, *tokens), normed_low, w_query
    )
    shares = net.query_ready(query_near, query_far)
    grad_flat_part, grad_gain_one, grad_bias_one = norm_one_pull(grad_normed_one)
    grad_patches = after((grad_first_sum + grad_flat_part).astype(BF), *net.query_there())
    grad_patches = net.from_strip(grad_patches.reshape(seq, part_rows, width))
    grad_vector = net.sum_all(
        jnp.concatenate([
            grad_gain_one, grad_bias_one, head_sums[0], head_sums[1],
            middle_sums[2], middle_sums[0], middle_sums[1], grad_fc1_bias, grad_fc2_bias,
        ]).reshape(-1, 128)
    ).reshape(-1)

    counts = [share.shape[0] for share in shares]
    most = max(counts)
    stack_low = lambda parts: jnp.stack(
        [jnp.pad(part.astype(BF), ((0, most - part.shape[0]), (0, 0))) for part in parts]
    )
    moments = (mom_qkv, mom_out, mom_fc1, mom_fc2)
    weights_old = (w_qkv, w_out, w_fc1, w_fc2)
    owned_moment = net.to_owner(stack_low([net.piece(moment) for moment in moments]))
    squares = sum(jnp.sum(share * share) for share in shares)
    owned_share, total_squares = net.to_owner_and_sum(stack_low(shares), squares)
    total_squares = total_squares + jnp.sum(grad_vector * grad_vector)
    grad_norm = jnp.sqrt(total_squares)
    clip = jnp.minimum(1.0, CLIP / (grad_norm + 1e-06))

    mine = MOMENTUM * owned_moment.astype(F32) + clip * owned_share.astype(F32)
    mine = mine.reshape(-1, width)
    mine_low = mine.astype(BF)
    gram_part = contract_rows(mine_low, mine_low)
    upper = [
        gram_part[THIRD * i : THIRD * (i + 1), THIRD * j : THIRD * (j + 1)] for i, j in BLOCKS
    ]
    moments_new = net.update(moments, shares, clip)
    order, pieces = net.sum_owner(
        jnp.concatenate(upper, axis=0), mixed, grad_patches, *moments_new
    )
    weights_new = net.finish(weights_old, orthogonal(order, pieces, mine))
    results = [value for pair in zip(moments_new, weights_new) for value in pair]
    entries = vectors.shape[0]
    vector_grad = clip * lax.dynamic_slice_in_dim(grad_vector, net.dp_at * entries, entries, 0)
    first_new = BETA_ONE * vec_first + (1.0 - BETA_ONE) * vector_grad
    second_new = BETA_TWO * vec_second + (1.0 - BETA_TWO) * vector_grad * vector_grad
    first_hat = first_new / (1.0 - BETA_ONE**ADAM_STEP)
    second_hat = second_new / (1.0 - BETA_TWO**ADAM_STEP)
    vectors_new = vectors - VEC_RATE * first_hat / (jnp.sqrt(second_hat) + 1e-08)
    return (mixed, grad_patches, grad_norm, *results, first_new, second_new, vectors_new)


def solution(mesh):
    rows, flat, full = P("dp", None), P("dp"), P("dp", "seq", None)
    return jax.shard_map(
        shards,
        mesh=mesh,
        in_specs=(full, full, flat) + (rows,) * 8 + (flat,) * 3,
        out_specs=(full, full, P()) + (rows,) * 8 + (flat,) * 3,
        check_vma=False,
    )
```

```python
import functools
import math

import jax
import jax.numpy as jnp
from jax import lax
from jax.experimental import pallas as pl
from jax.experimental.pallas import tpu as pltpu
from jax.sharding import PartitionSpec as P

D = 768
FF = 3072
HEADS = 12
ITERS = 5
ADAM_STEP = 10

NEG_BIG = -1e30
LN_EPS = 1e-06
NS_COEFFS = (3.4445, -4.775, 2.0315)
MOMENTUM = 0.5
CLIP = 1.0
DECAY = 0.01
MATRIX_RATES = (1.0, 3.0, 1.0, 0.6)
VEC_RATE = 0.1
BETA_ONE = 0.5
BETA_TWO = 0.5
ROWS_LAST = (((0,), (0,)), ((), ()))
COLS_LAST = (((1,), (1,)), ((), ()))
BOTH = ("dp", "seq")
MIB = 1024 * 1024
PIECES = 32
VECTOR_ROWS = 12
BF = jnp.bfloat16
F32 = jnp.float32


def layer_norm(values):
    centre = values - jnp.mean(values, axis=-1, keepdims=True)
    spread = jnp.mean(centre * centre, axis=-1, keepdims=True)
    return centre * lax.rsqrt(spread + LN_EPS)


def split_vector(vector):
    bounds = [0, D, 2 * D, 3 * D, 4 * D, 5 * D, 6 * D, 7 * D, 7 * D + FF, 8 * D + FF]
    return [vector[bounds[position] : bounds[position + 1]] for position in range(9)]


def contract_rows(left, right):
    return lax.dot_general(left, right, ROWS_LAST, preferred_element_type=F32)


def contract_cols(left, right):
    return lax.dot_general(left, right, COLS_LAST, preferred_element_type=F32)


def after(value, *others):
    return lax.optimization_barrier((value,) + others)[0]


def cost(microseconds):
    return pl.CostEstimate(
        flops=int(1e9 * microseconds), bytes_accessed=int(3e6 * microseconds), transcendentals=0
    )


def place_kernel(cuts, order_ref, *refs):
    sources, outs, sem = refs[: -len(cuts) - 1], refs[-len(cuts) - 1 : -1], refs[-1]
    copies = []
    for place_at, (source, piece) in enumerate(
        (source, piece) for source in sources for piece in range(source.shape[0])
    ):
        start = 0
        for cut, out in zip(cuts, outs):
            taken = source.at[piece, pl.ds(start, cut)] if len(cuts) > 1 else source.at[piece]
            target = out.at[order_ref[place_at]]
            copies.append(pltpu.make_async_copy(taken, target, sem.at[len(copies)]))
            start += cut
            copies[-1].start()
    for copy in copies:
        copy.wait()


def place(order, *sources, cuts=None, expected=0.3):
    count = sum(source.shape[0] for source in sources)
    cuts = cuts or [sources[0].shape[1]]
    return pl.pallas_call(
        functools.partial(place_kernel, tuple(cuts)),
        out_shape=[
            jax.ShapeDtypeStruct((count, cut) + sources[0].shape[2:], sources[0].dtype)
            for cut in cuts
        ],
        in_specs=[pl.BlockSpec(memory_space=pltpu.SMEM)]
        + [pl.BlockSpec(memory_space=pl.ANY)] * len(sources),
        out_specs=[pl.BlockSpec(memory_space=pltpu.VMEM)] * len(cuts),
        scratch_shapes=[pltpu.SemaphoreType.DMA((count * len(cuts),))],
        cost_estimate=cost(expected),
        compiler_params=pltpu.CompilerParams(vmem_limit_bytes=56 * MIB),
    )(order, *sources)


class Plain:
    def __init__(self, dp, seq):
        self.dp, self.seq = dp, seq
        self.dp_at, self.seq_at = lax.axis_index("dp"), lax.axis_index("seq")
        self.owned = self.seq_at

    def piece(self, block):
        rows = block.shape[0] // self.seq
        return lax.dynamic_slice_in_dim(block, self.seq_at * rows, rows, 0)

    def gather_rows(self, blocks, vector):
        self.rows = [lax.all_gather(block, "dp", axis=0, tiled=True) for block in (*blocks, vector)]

    def gather_whole(self, block):
        return lax.all_gather(self.piece(block), BOTH).reshape(-1, block.shape[1])

    def gather_packed(self, blocks, first):
        wholes = [self.gather_whole(block).reshape(8, 4, -1, D) for block in blocks]
        self.packed = list(jnp.concatenate(wholes, axis=2))

    def placed_rows(self, *first):
        return self.rows

    def gather_neighbours(self, first):
        pass

    def gather_diagonal(self, first):
        pass

    def packed_part(self, at):
        return self.packed[at]

    def order(self):
        return jnp.arange(PIECES), jnp.arange(PIECES)

    def reduce(self, near, far):
        whole = jnp.concatenate([near, far], axis=0).reshape(-1, D).astype(F32)
        return lax.psum_scatter(whole, BOTH, scatter_dimension=0, tiled=True)

    def hidden_ready(self, at, grads):
        self.hidden = getattr(self, "hidden", {}) | dict(zip(at, grads))

    def send_diagonal(self):
        return ()

    def send_neighbours(self):
        return ()

    def proj_ready(self, near, far):
        self.proj = (near, far)
        return ()

    def query_ready(self, near, far, vector):
        whole = jnp.stack([self.hidden[at] for at in range(8)])
        first, second = [self.reduce(whole[:4, :, kind], whole[4:, :, kind]) for kind in range(2)]
        entries = 12 * D // self.dp
        vector = jnp.concatenate([vector[:, 0], vector[:, 1, : D // 2]], axis=1).reshape(self.dp, entries)
        vector = lax.psum_scatter(lax.psum(vector, "seq"), "dp", scatter_dimension=0)
        return (self.reduce(near, far), self.reduce(*self.proj), first, second), vector

    def with_query(self, values):
        return values

    def vector_squares(self, vector):
        return jnp.full((D,), jnp.sum(vector * vector) / (D * self.seq), F32)

    def to_owner(self, parts):
        return lax.all_to_all(parts, "seq", split_axis=0, concat_axis=0, tiled=True)

    def to_owner_and_sum(self, parts, value):
        return self.to_owner(parts), jnp.sum(lax.psum(value, BOTH))

    def sum_owner(self, value, first, second):
        return jnp.arange(8), lax.psum(value, "dp").reshape(2, 4, -1, value.shape[-1])

    def update(self, moments, shares, clip):
        result = []
        for moment, share in zip(moments, shares):
            gradient = lax.all_gather(share, "seq", axis=0, tiled=True)
            result.append(MOMENTUM * moment + clip * gradient)
        return result

    def finish(self, weights, rows):
        whole = lax.all_gather(rows, "seq")
        result = []
        for at, weight in enumerate(weights):
            keep, step = weight_factors(at)
            part = whole[at].reshape(self.seq, -1, D)[:, : weight.shape[0] // self.seq]
            result.append(weight * keep - step * part.reshape(weight.shape).astype(F32))
        return result

    def to_strip(self, parts):
        parts = lax.all_to_all(parts, "seq", split_axis=0, concat_axis=0, tiled=True)
        return [parts[:, at].reshape(-1, D) for at in range(2)]

    def from_strip(self, parts):
        parts = lax.all_to_all(parts, "seq", split_axis=0, concat_axis=0, tiled=True)
        return [parts[:, at] for at in range(parts.shape[1])]

    def owners(self):
        return jnp.arange(self.seq, dtype=jnp.int32)


class Paths(Plain):
    def __init__(self, dp, seq):
        super().__init__(dp, seq)
        self.me = self.dp_at * seq + self.seq_at
        self.low = self.me & 7
        self.z = self.me >> 3
        self.owned = (self.me >> 1) & 3

    def swap(self, value, mask):
        return lax.ppermute(value, BOTH, [(d, d ^ mask) for d in range(32)])

    def climb(self, value, steps):
        return lax.ppermute(value, BOTH, [(d, (d + 8 * steps) % 32) for d in range(32)])

    def order(self):
        masks = (0, 2, 4, 6, 1, 3, 5, 7)
        order = [((self.z - k) & 3) * 8 + (self.low ^ mask) for mask in masks for k in range(4)]
        piece = jnp.arange(PIECES)
        mask = (piece & 7) ^ self.low
        tile = (mask >> 1) + 4 * (mask & 1)
        return jnp.stack(order), tile * 4 + ((self.z - (piece >> 3)) & 3)

    def column(self, part):
        part = part[None]
        return jnp.concatenate([part] + [self.climb(part, k) for k in (1, 2, 3)], axis=0)

    def gather_rows(self, blocks, vector):
        self.entries = vector.shape[0] // 4
        extra = lax.dynamic_slice_in_dim(vector, self.seq_at * self.entries, self.entries, 0)
        extra = jnp.pad(extra[None], ((0, 7), (0, D - self.entries)))
        parts = [self.piece(block) for block in blocks] + [extra]
        self.cuts = [part.shape[0] for part in parts]
        part = jnp.concatenate(parts, axis=0)[None]
        column = jnp.concatenate([part] + [self.climb(part, k) for k in (1, 2, 3)], axis=0)
        self.arrived = [self.swap(column, mask) for mask in (2, 4, 6)]
        near = [column] + self.arrived
        self.pieces = near + [self.swap(v, 1) for v in near]
        return column

    def placed_rows(self, *first):
        order = self.order()[0].astype(jnp.int32)
        self.pieces[7] = after(self.pieces[7], *first)
        *parts, extra = place(order, *self.pieces, cuts=self.cuts)
        return *[part.reshape(-1, D) for part in parts], extra[:, 0, : self.entries].reshape(-1)

    def gather_packed(self, blocks, first):
        held = jnp.concatenate([self.piece(block) for block in blocks], axis=0)[None]
        held = jnp.concatenate([held, self.climb(held, 1)], axis=0)
        self.packed = [held, self.climb(after(held, first), 2)]

    def gather_neighbours(self, first):
        held, climbed = self.packed
        sent = jnp.concatenate([held, after(climbed, first)], axis=0)
        self.packed = [sent, self.swap(sent, 2), self.swap(sent, 4), None]

    def gather_diagonal(self, first):
        self.packed[3] = self.swap(after(self.packed[0], first, *self.packed[1:3]), 6)
        self.packed += [self.swap(v, 1) for v in self.packed]

    def packed_part(self, at):
        return self.packed[at]

    def both_cores(self, near, far):
        return near.astype(F32) + far.astype(F32)

    def hidden_ready(self, at, grads):
        held = getattr(self, "hidden", {})
        for place_at, grad in zip(at, grads):
            held[place_at] = self.swap(grad, 1) if place_at >= 4 else grad
        self.hidden = held

    def half(self, at):
        return self.both_cores(self.hidden[at], self.hidden[at + 4])

    def send_diagonal(self):
        sent = self.half(3).astype(BF)
        self.received.append(self.swap(sent, 6))
        return (sent,)

    def send_neighbours(self):
        sent = [self.half(at).astype(BF) for at in (1, 2)]
        self.received = [self.swap(sent[0], 2), self.swap(sent[1], 4)]
        return sent

    def proj_ready(self, near, far):
        self.proj = [near.reshape(4, 4, -1, D), self.swap(far, 1).reshape(4, 4, -1, D)]
        return (self.proj[1],)

    def query_ready(self, near, far, vector):
        far = after(far, *self.received)
        query = [near.reshape(4, 4, -1, D), self.swap(far, 1).reshape(4, 4, -1, D)]
        vector = (vector + self.swap(vector, 1)).astype(BF)
        levels = jnp.stack([((self.z - k) & 3) * 2 + (self.low >> 2) for k in range(4)])
        vector = [vector[levels], vector[levels ^ 1]]
        joint = lambda at: jnp.concatenate(
            [self.both_cores(near[at], far[at]) for near, far in (query, self.proj)]
            + [vector[at >> 1].astype(F32)],
            axis=1,
        )
        sent = [joint(at).astype(BF) for at in (1, 2, 3)]
        received = [self.swap(sent[at - 1], 2 * at) for at in (1, 2, 3)]
        self.query_received = received
        self.received = [after(part, *sent) for part in self.received]
        hidden = self.both_cores(self.hidden[0], self.hidden[4])
        for part in self.received:
            hidden = hidden + part.astype(F32)
        hidden = hidden.reshape(4, -1, D)
        low = hidden.astype(BF)
        both = hidden[0]
        climbed = [self.climb(low[k], -k) for k in (1, 2, 3)]
        total = joint(0)
        for part in received:
            total = total + part.astype(F32)
        low = after(total.astype(BF), *climbed)
        last = total[0]
        for k in (1, 2, 3):
            last = last + self.climb(low[k], -k).astype(F32)
            both = both + climbed[k - 1].astype(F32)
        cut, end, rows = query[0].shape[2], last.shape[0] - 8, both.shape[0] // 2
        return (
            (last[:cut], last[cut:end], both[:rows], both[rows:]),
            jnp.concatenate([last[end], last[end + 1, : D // 2]]),
        )

    def with_query(self, values):
        return lax.optimization_barrier((*values, *self.query_received))[: len(values)]

    def vector_squares(self, vector):
        terms = vector * vector * (1.0 / self.seq)
        return terms[:D] + jnp.pad(terms[D:], (0, D // 2))

    def pick(self, parts, at):
        return lax.dynamic_index_in_dim(parts, at, 0, keepdims=False)

    def to_owner(self, parts):
        own = self.pick(parts, self.owned)
        return jnp.stack(
            [own] + [self.swap(self.pick(parts, self.owned ^ j), 2 * j) for j in (1, 2, 3)]
        )

    def to_owner_and_sum(self, parts, value):
        terms, rest = [], value
        for _ in range(3):
            terms.append(lax.reduce_precision(rest, 8, 7))
            rest = rest - terms[-1]
        extra = jnp.stack(terms + [jnp.zeros((D,), F32)] * 5)
        extra = jnp.broadcast_to(extra.astype(BF)[None], (4, 8, D))
        whole = self.to_owner(jnp.concatenate([parts, extra], axis=1))
        count = parts.shape[1]
        sums = whole[:, count : count + 3].astype(F32)
        sums = (sums[:, 0] + sums[:, 1]) + sums[:, 2]
        total = ((sums[0] + sums[1]) + (sums[2] + sums[3]))[None]
        total = total + self.swap(total, 1)
        one, two, three = [self.climb(total, k) for k in (1, 2, 3)]
        return whole[:, :count], jnp.sum((total + two) + (one + three))

    def sum_owner(self, value, first, second):
        rows, core = value.shape[0] // 8, self.low & 1
        halves = value.reshape((2, 4, rows) + value.shape[1:])
        half = self.pick(halves, core) + self.swap(self.pick(halves, 1 - core), 1)
        level = lambda k: self.pick(half, (self.z + k) & 3)
        share = level(0)
        for k in (1, 2, 3):
            share = share + self.climb(level(k), k)
        share = after(share, *first)
        column = after(jnp.stack([share] + [self.climb(share, k) for k in (1, 2, 3)]), *second)
        order = [at * 4 + ((self.z - k) & 3) for at in (core, 1 - core) for k in range(4)]
        return jnp.stack(order), jnp.stack([column, self.swap(column, 1)])

    def update(self, moments, shares, clip):
        block = jnp.concatenate([share.astype(BF) for share in shares], axis=0)
        first = jnp.stack([block, self.swap(block, 2)])
        second = self.swap(first, 1)
        places = [((q ^ self.seq_at) >> 1) + 2 * ((q ^ self.seq_at) & 1) for q in range(4)]
        return update_moments(jnp.stack(places), clip, first, second, moments)

    def finish(self, weights, rows):
        parts = rows.reshape(4, -1, D)
        mine, theirs = parts[:2], parts[2:]
        near = jnp.stack([mine, self.swap(mine, 2), self.swap(theirs, 4), self.swap(theirs, 6)])
        far = self.swap(near, 1)
        x, core = (self.low >> 1) & 1, self.low & 1
        places = []
        for matrix in range(4):
            j = self.owned ^ matrix
            for q in range(4):
                places.append((core ^ (q & 1)) * 8 + j * 2 + (x ^ (j & 1) ^ (q >> 1)))
        cut = (8,) + parts.shape[1:]
        return update_weights(jnp.stack(places), near.reshape(cut), far.reshape(cut), weights)

    def exchange(self, parts, first):
        return [first] + [self.swap(self.pick(parts, self.seq_at ^ k), k) for k in (1, 2, 3)]

    def to_strip(self, parts):
        parts = self.exchange(parts, self.pick(parts, self.seq_at))
        return [jnp.concatenate([part[at] for part in parts], axis=0) for at in range(2)]

    def from_strip(self, parts):
        (parts,) = self.with_query([parts])
        back = [parts[0]] + [self.swap(parts[k], k) for k in (1, 2, 3)]
        order = jnp.stack([self.seq_at ^ k for k in range(4)]).astype(jnp.int32)
        cut = parts.shape[2]
        flat = [v.reshape(1, -1, parts.shape[-1]) for v in back]
        return place(order, *flat, cuts=[cut] * parts.shape[1], expected=4)

    def owners(self):
        return jnp.arange(4, dtype=jnp.int32) ^ self.seq_at


def weight_factors(at):
    rate = MATRIX_RATES[at]
    return 1.0 - rate * DECAY, rate * math.sqrt((3 * D, D, FF, FF)[at] / D)


def update_moments_kernel(place_ref, clip_ref, near, far, *refs):
    moments, results, held, sem = refs[:4], refs[4:8], refs[8], refs[9]
    copies = [
        pltpu.make_async_copy(source, held.at[pl.ds(2 * at, 2)], sem.at[at])
        for at, source in enumerate((near, far))
    ]
    for copy in copies:
        copy.start()
    for copy in copies:
        copy.wait()
    for q in range(4):
        block = held[place_ref[q]].astype(F32) * clip_ref[0]
        start = 0
        for moment, result in zip(moments, results):
            rows = moment.shape[0] // 4
            at = slice(q * rows, (q + 1) * rows)
            result[at, :] = MOMENTUM * moment[at, :] + block[start : start + rows]
            start += rows


def update_moments(places, clip, near, far, moments):
    vmem, smem = pl.BlockSpec(memory_space=pltpu.VMEM), pl.BlockSpec(memory_space=pltpu.SMEM)
    anywhere = pl.BlockSpec(memory_space=pl.ANY)
    return pl.pallas_call(
        update_moments_kernel,
        out_shape=[jax.ShapeDtypeStruct(moment.shape, F32) for moment in moments],
        in_specs=[smem, smem, anywhere, anywhere] + [vmem] * 4,
        out_specs=[vmem] * 4,
        scratch_shapes=[
            pltpu.VMEM((4,) + near.shape[1:], BF),
            pltpu.SemaphoreType.DMA((2,)),
        ],
        cost_estimate=cost(6),
        compiler_params=pltpu.CompilerParams(vmem_limit_bytes=16 * MIB),
    )(places.astype(jnp.int32), clip.reshape(1), near, far, *moments)


def update_weights_kernel(place_ref, near, far, *refs):
    weights, results, held, sem = refs[:4], refs[4:8], refs[8], refs[9]
    copies = [
        pltpu.make_async_copy(source, held.at[pl.ds(8 * at, 8)], sem.at[at])
        for at, source in enumerate((near, far))
    ]
    for copy in copies:
        copy.start()
    for copy in copies:
        copy.wait()
    for matrix, (weight, result) in enumerate(zip(weights, results)):
        keep, step = weight_factors(matrix)
        rows = weight.shape[0] // 4
        for q in range(4):
            at = slice(q * rows, (q + 1) * rows)
            block = held[place_ref[4 * matrix + q]].astype(F32)
            result[at, :] = weight[at, :] * keep - step * block[:rows]


def update_weights(places, near, far, weights):
    vmem, smem = pl.BlockSpec(memory_space=pltpu.VMEM), pl.BlockSpec(memory_space=pltpu.SMEM)
    anywhere = pl.BlockSpec(memory_space=pl.ANY)
    return pl.pallas_call(
        update_weights_kernel,
        out_shape=[jax.ShapeDtypeStruct(weight.shape, F32) for weight in weights],
        in_specs=[smem, anywhere, anywhere] + [vmem] * 4,
        out_specs=[vmem] * 4,
        scratch_shapes=[
            pltpu.VMEM((16,) + near.shape[1:], BF),
            pltpu.SemaphoreType.DMA((2,)),
        ],
        cost_estimate=cost(0.3),
        compiler_params=pltpu.CompilerParams(vmem_limit_bytes=16 * MIB),
    )(places.astype(jnp.int32), near, far, *weights)


def forward_kernel(mask_ref, q_ref, k_ref, v_ref, out_ref):
    keep = mask_ref[...] > 0.0
    for head in range(2):
        at = slice(64 * head, 64 * head + 64)
        scores = contract_cols(q_ref[:, at] * BF(0.125), k_ref[:, at])
        scores = jnp.where(keep, scores, NEG_BIG)
        raised = jnp.exp(scores - jnp.max(scores, axis=1, keepdims=True))
        totals = jnp.sum(raised, axis=1, keepdims=True)
        softmaxed = (raised * (1.0 / totals)).astype(BF)
        mixed = jnp.dot(softmaxed, v_ref[:, at], preferred_element_type=F32)
        out_ref[:, at] = mixed.astype(BF)


def write_pieces(order_ref, source, near_ref, far_ref):
    rows = near_ref.shape[1]
    for at in range(PIECES):
        target = near_ref if at < PIECES // 2 else far_ref
        piece = source[pl.ds(pl.multiple_of(order_ref[at] * rows, 8), rows), :]
        target[at % (PIECES // 2)] = piece.astype(BF)


def backward_kernel(
    order_ref, mask_ref, q_ref, k_ref, v_ref, up_ref, h_ref, wq_ref, wk_ref, wv_ref,
    strip_ref, dsum_ref, gain_ref, middle_ref, first_ref, second_ref,
    near_ref, far_ref, out_ref, blocks_ref, sums, grad, dh_ref,
):
    pair = pl.program_id(0)
    keep = mask_ref[...] > 0.0
    grads = [[], [], []]
    for head in range(2):
        at = slice(64 * head, 64 * head + 64)
        queries, keys_in, upstream = q_ref[:, at] * BF(0.125), k_ref[:, at], up_ref[:, at]
        scores = jnp.where(keep, contract_cols(keys_in, queries), NEG_BIG)
        raised = jnp.exp(scores - jnp.max(scores, axis=0, keepdims=True))
        softmaxed = raised * (1.0 / jnp.sum(raised, axis=0, keepdims=True))
        dprob = contract_cols(v_ref[:, at], upstream)
        weighted = jnp.sum(softmaxed * dprob, axis=0, keepdims=True)
        dscore = (softmaxed * (dprob - weighted)).astype(BF)
        grads[2].append(jnp.dot(softmaxed.astype(BF), upstream, preferred_element_type=F32))
        grads[1].append(jnp.dot(dscore, queries, preferred_element_type=F32))
        grads[0].append(contract_rows(dscore, keys_in) * 0.125)
    joint = [jnp.concatenate(parts, axis=1).astype(BF) for parts in grads]
    lanes = pl.ds(pl.multiple_of(pair * 128, 128), 128)
    sums[2:3, lanes] = jnp.sum(joint[0].astype(F32), axis=0, keepdims=True)
    sums[3:4, lanes] = jnp.sum(joint[2].astype(F32), axis=0, keepdims=True)
    dhidden = jnp.zeros(dh_ref.shape, F32)
    for part, (piece, w_ref) in enumerate(zip(joint, (wq_ref, wk_ref, wv_ref))):
        rows = pl.ds(pl.multiple_of(part * D + pair * 128, 128), 128)
        grad[rows, :] = contract_rows(piece, h_ref[...])
        dhidden += jnp.dot(piece, w_ref[...], preferred_element_type=F32)

    @pl.when(pair == 0)
    def _():
        dh_ref[...] = dhidden

    @pl.when(pair > 0)
    def _():
        dh_ref[...] += dhidden

    @pl.when(pair == HEADS // 2 - 1)
    def _():
        write_pieces(order_ref, grad, near_ref, far_ref)
        change = norm_backward(strip_ref[...].astype(F32), dh_ref[...], gain_ref[...], sums)
        out_ref[...] = (dsum_ref[...] + change).astype(BF)
        sums[4:5, :] = middle_ref[2:3, :]
        sums[5:7, :] = middle_ref[0:2, :]
        sums[7:11, :] = first_ref[...]
        sums[11:12, :] = second_ref[...]
        blocks_ref[...] = jnp.zeros(blocks_ref.shape, F32)
        half = D // 2
        for at in range(0, VECTOR_ROWS, 3):
            one, two, three = [sums[row : row + 1, :] for row in range(at, at + 3)]
            even, odd = 2 * at // 3, 2 * at // 3 + 1
            blocks_ref[even, 0:1, :] = one
            blocks_ref[even, 1:2, :half] = two[:, :half]
            blocks_ref[odd, 0:1, :half] = two[:, half:]
            blocks_ref[odd, 0:1, half:] = three[:, :half]
            blocks_ref[odd, 1:2, :half] = three[:, half:]


def norm_backward(values, dhidden, gain, sums_ref):
    centre = values - jnp.mean(values, axis=1, keepdims=True)
    scale = lax.rsqrt(jnp.mean(centre * centre, axis=1, keepdims=True) + LN_EPS)
    normed = centre * scale
    dnormed = dhidden * gain
    inner = jnp.mean(dnormed * normed, axis=1, keepdims=True)
    sums_ref[0:1, :] = jnp.sum(dhidden * normed, axis=0, keepdims=True)
    sums_ref[1:2, :] = jnp.sum(dhidden, axis=0, keepdims=True)
    return scale * (dnormed - jnp.mean(dnormed, axis=1, keepdims=True) - normed * inner)


def head_pair(rows, shift):
    return pl.BlockSpec((rows, 128), lambda pair: (0, pair + shift))


def attend_forward(projected, key_mask):
    rows = projected.shape[0]
    return pl.pallas_call(
        forward_kernel,
        grid=(HEADS // 2,),
        out_shape=jax.ShapeDtypeStruct((rows, D), BF),
        in_specs=[pl.BlockSpec((1, rows), lambda pair: (0, 0))]
        + [head_pair(rows, HEADS // 2 * part) for part in range(3)],
        out_specs=head_pair(rows, 0),
        cost_estimate=cost(0.3),
        compiler_params=pltpu.CompilerParams(vmem_limit_bytes=14 * MIB),
    )(key_mask.astype(F32)[None], projected, projected, projected)


def attend_backward(order, projected, key_mask, upstream, hidden, weight, strip, dsum, gain, vectors):
    rows, pairs = projected.shape[0], HEADS // 2
    whole = lambda *shape: pl.BlockSpec(shape, lambda pair: (0,) * len(shape))
    band = lambda part: pl.BlockSpec((128, D), lambda pair: (pair + pairs * part, 0))
    half = (PIECES // 2, 3 * D // PIECES, D)
    return pl.pallas_call(
        backward_kernel,
        grid=(pairs,),
        out_shape=[jax.ShapeDtypeStruct(half, BF)] * 2
        + [jax.ShapeDtypeStruct((rows, D), BF), jax.ShapeDtypeStruct((8, 8, D), F32)],
        in_specs=[pl.BlockSpec(memory_space=pltpu.SMEM), whole(rows, 1)]
        + [head_pair(rows, pairs * part) for part in range(3)]
        + [head_pair(rows, 0), whole(rows, D)]
        + [band(part) for part in range(3)]
        + [whole(rows, D)] * 2
        + [whole(1, D), whole(8, D), whole(4, D), whole(1, D)],
        out_specs=[whole(*half)] * 2 + [whole(rows, D), whole(8, 8, D)],
        scratch_shapes=[
            pltpu.VMEM((16, D), F32),
            pltpu.VMEM((3 * D, D), F32),
            pltpu.VMEM((rows, D), F32),
        ],
        cost_estimate=cost(0.3),
        compiler_params=pltpu.CompilerParams(vmem_limit_bytes=28 * MIB),
    )(
        order, key_mask.astype(F32)[:, None], projected, projected, projected, upstream,
        hidden, weight, weight, weight, strip, dsum, gain[None], *vectors,
    )


def middle_kernel(
    order_ref, sum_ref, dh_ref, up_ref, attn_ref, w_ref, gain_ref,
    dsum_ref, dattn_ref, near_ref, far_ref, sums_ref, grad,
):
    change = norm_backward(sum_ref[...], dh_ref[...], gain_ref[...], sums_ref)
    dsum = up_ref[...].astype(F32) + change
    dsum_ref[...] = dsum
    low = dsum.astype(BF)
    dattn_ref[...] = jnp.dot(low, w_ref[...], preferred_element_type=F32).astype(BF)
    grad[...] = contract_rows(low, attn_ref[...])
    write_pieces(order_ref, grad, near_ref, far_ref)
    sums_ref[2:3, :] = jnp.sum(dsum, axis=0, keepdims=True)


def middle(order, first_sum, dhidden, upstream, attended, weight, gain):
    rows = first_sum.shape[0]
    half = (PIECES // 2, D // PIECES, D)
    vmem = pl.BlockSpec(memory_space=pltpu.VMEM)
    return pl.pallas_call(
        middle_kernel,
        out_shape=[
            jax.ShapeDtypeStruct((rows, D), F32),
            jax.ShapeDtypeStruct((rows, D), BF),
            jax.ShapeDtypeStruct(half, BF),
            jax.ShapeDtypeStruct(half, BF),
            jax.ShapeDtypeStruct((8, D), F32),
        ],
        in_specs=[pl.BlockSpec(memory_space=pltpu.SMEM)] + [vmem] * 6,
        out_specs=[vmem] * 5,
        scratch_shapes=[pltpu.VMEM((D, D), F32)],
        cost_estimate=cost(0.3),
        compiler_params=pltpu.CompilerParams(vmem_limit_bytes=18 * MIB),
    )(order, first_sum, dhidden, upstream, attended, weight, gain[None])


def upper_tail(values):
    t = 1.0 / (1.0 + 0.5 * values)
    series = 0.17087277
    for factor in (
        -0.82215223, 1.48851587, -1.13520398, 0.27886807, -0.18628806,
        0.09678418, 0.37409196, 1.00002368, -1.26551223,
    ):
        series = series * t + factor
    return t * jnp.exp(series - values * values)


def mlp_kernel(first, arrays, h_ref, up_ref, bias_ref, *refs):
    if not first:
        (out_in, dh_in), refs = refs[:2], refs[2:]
    packed, (out_ref, dh_ref, dbias_ref), targets = refs[:arrays], refs[arrays : arrays + 3], refs[arrays + 3 : -2]
    held, sem = refs[-2:]
    pieces, rows = held.shape[1], held.shape[2]
    count, copies, start = pieces // 4, [], 0
    for source in packed:
        for kind in range(2):
            copy = pltpu.make_async_copy(
                source.at[:, pl.ds(kind * rows, rows)],
                held.at[kind, pl.ds(start, source.shape[0])],
                sem.at[len(copies)],
            )
            copy.start()
            copies.append(copy)
        start += source.shape[0]
    for copy in copies:
        copy.wait()
    hidden, upstream = h_ref[...], up_ref[...]
    w_first = held[0].reshape(pieces * rows, D)
    w_second = held[1].reshape(pieces * rows, D)
    before = contract_cols(hidden, w_first) + bias_ref[...]
    dact = contract_cols(upstream, w_second)
    tail = 0.5 * upper_tail(jnp.abs(before) * math.sqrt(0.5))
    below = jnp.where(before < 0.0, tail, 1.0 - tail)
    slope = below + before * (jnp.exp(-0.5 * before * before) * (1.0 / math.sqrt(2.0 * math.pi)))
    active = (before * below).astype(BF)
    dbefore = (dact * slope).astype(BF)
    dbias_ref[...] = jnp.sum(dbefore.astype(F32), axis=0, keepdims=True)
    mixed = jnp.dot(active, w_second, preferred_element_type=F32)
    dhidden = jnp.dot(dbefore, w_first, preferred_element_type=F32)
    out_ref[...] = mixed if first else out_in[...] + mixed
    dh_ref[...] = dhidden if first else dh_in[...] + dhidden
    for kind, grad in enumerate((contract_rows(dbefore, hidden), contract_rows(active, upstream))):
        grad = grad.astype(BF).reshape(count, 4, rows, D)
        for at, target in enumerate(targets):
            target[:, kind] = grad[at]


def mlp(hidden, upstream, bias, packed, sums):
    rows, piece = hidden.shape[0], FF // PIECES
    pieces, arrays = sum(part.shape[0] for part in packed), len(packed)
    vmem, anywhere = pl.BlockSpec(memory_space=pltpu.VMEM), pl.BlockSpec(memory_space=pl.ANY)
    return pl.pallas_call(
        functools.partial(mlp_kernel, not sums, arrays),
        out_shape=[jax.ShapeDtypeStruct((rows, D), F32)] * 2
        + [jax.ShapeDtypeStruct((1, pieces * piece), F32)]
        + [jax.ShapeDtypeStruct((4, 2, piece, D), BF)] * (pieces // 4),
        in_specs=[vmem] * (3 + len(sums)) + [anywhere] * arrays,
        out_specs=[vmem] * (3 + pieces // 4),
        scratch_shapes=[
            pltpu.VMEM((2, pieces, piece, D), BF),
            pltpu.SemaphoreType.DMA((2 * arrays,)),
        ],
        input_output_aliases={3: 0, 4: 1} if sums else {},
        cost_estimate=cost(0.3),
        compiler_params=pltpu.CompilerParams(vmem_limit_bytes=20 * MIB),
    )(hidden, upstream, bias.reshape(1, -1), *sums, *packed)


THIRD = D // 3
BLOCKS = [(i, j) for i in range(3) for j in range(i, 3)]


def band(i):
    return slice(THIRD * i, THIRD * (i + 1))


def split_to(blocks, high, low):
    for (i, j), block in blocks.items():
        top = block.astype(BF)
        for target, part in ((high, top), (low, None if low is None else block - top.astype(F32))):
            if target is not None:
                part = part.astype(BF)
                target[band(i), band(j)] = part
                if i != j:
                    target[band(j), band(i)] = part.T


def product(*pairs):
    blocks = {}
    for i in range(3):
        total = None
        for left, right in pairs:
            term = jnp.dot(left[band(i), :], right[:, THIRD * i :], preferred_element_type=F32)
            total = term if total is None else total + term
        for j in range(i, 3):
            blocks[i, j] = total[:, band(j - i)]
    return blocks


def combined(*terms):
    return {at: sum(factor * blocks[at] for factor, blocks in terms) for at in BLOCKS}


def on_diagonal():
    shape = (THIRD, THIRD)
    return lax.broadcasted_iota(jnp.int32, shape, 0) == lax.broadcasted_iota(jnp.int32, shape, 1)


def diagonal_mean(blocks):
    total = blocks[0, 0] + blocks[1, 1] + blocks[2, 2]
    return jnp.sum(jnp.where(on_diagonal(), total, 0.0), keepdims=True) * (1.0 / D)


def without(blocks, mean):
    shift = jnp.where(on_diagonal(), mean, 0.0)
    return {(i, j): block - shift if i == j else block for (i, j), block in blocks.items()}


def orthogonal_kernel(
    order_ref, pieces_ref, rows_ref, out_ref, packed, rest_h, rest_l, change_h, twice_h, twice_l
):
    a, b, c = NS_COEFFS
    height = pieces_ref.shape[2]
    for at in range(8):
        target = pl.ds(pl.multiple_of(order_ref[at] * height, 8), height)
        packed[target, :] = pieces_ref[at // 4, at % 4]
    gram = {pair: packed[THIRD * at : THIRD * (at + 1), :] for at, pair in enumerate(BLOCKS)}
    mean = diagonal_mean(gram)
    inverse = 1.0 / (jnp.sqrt(mean * D) + 1e-07)
    rows = rows_ref[...] * inverse
    square = inverse * inverse
    mean = mean * square
    rest = without(combined((square, gram)), mean)
    for sweep in range(ITERS):
        last, fine = sweep == ITERS - 1, 0 < sweep < ITERS - 1
        split_to(rest, rest_h, rest_l if fine else None)
        p0 = a + b * mean + c * mean * mean
        p1 = b + 2.0 * c * mean
        change = combined((p1, rest), (c, product((rest_h, rest_h))))
        split_to(change, change_h, None)
        rows = p0 * rows + jnp.dot(rows.astype(BF), change_h[...], preferred_element_type=F32)
        if not last:
            twice = combined((2.0 * p0, change), (1.0, product((change_h, change_h))))
            split_to(twice, twice_h, twice_l if fine else None)
            pairs = [(rest_h, twice_h)] + [(rest_h, twice_l), (rest_l, twice_h)] * fine
            rest = combined((p0 * p0, rest), (mean, twice), (1.0, product(*pairs)))
            shift = diagonal_mean(rest)
            rest = without(rest, shift)
            mean = mean * p0 * p0 + shift
    out_ref[...] = rows.astype(BF)


def orthogonal(order, pieces, rows):
    vmem = pl.BlockSpec(memory_space=pltpu.VMEM)
    return pl.pallas_call(
        orthogonal_kernel,
        out_shape=jax.ShapeDtypeStruct(rows.shape, BF),
        in_specs=[pl.BlockSpec(memory_space=pltpu.SMEM)] + [vmem] * 2,
        out_specs=vmem,
        scratch_shapes=[pltpu.VMEM((len(BLOCKS) * THIRD, THIRD), F32)] + [pltpu.VMEM((D, D), BF)] * 5,
        cost_estimate=cost(0.3),
        compiler_params=pltpu.CompilerParams(vmem_limit_bytes=20 * MIB),
    )(order.astype(jnp.int32), pieces, rows)


def shards(
    patches, cotangent, lengths,
    w_qkv, w_out, w_fc1, w_fc2,
    mom_qkv, mom_out, mom_fc1, mom_fc2,
    vectors, vec_first, vec_second,
):
    strip_count, part_rows, width = patches.shape
    dp, seq = lax.axis_size("dp"), lax.axis_size("seq")
    assert strip_count == seq == 4
    net = (Paths if (dp, seq) == (8, 4) else Plain)(dp, seq)
    row_count = part_rows * seq

    strip, upstream_low = net.to_strip(jnp.stack([patches, cotangent], axis=1))
    first = net.gather_rows([w_qkv.astype(BF), w_out.astype(BF)], vectors.astype(BF))
    net.gather_packed([w_fc1.astype(BF), w_fc2.astype(BF)], first)
    flat = strip.astype(F32)
    normed = layer_norm(flat)
    w_query, w_proj, vec_low = net.placed_rows(normed, upstream_low)
    (gain_one, bias_one, query_bias, value_bias, out_bias,
     gain_two, bias_two, fc1_bias, fc2_bias) = split_vector(vec_low.astype(F32))
    normed_low = (normed * gain_one + bias_one).astype(BF)

    owners = net.owners()
    places = (owners[:, None] * part_rows + jnp.arange(part_rows, dtype=jnp.int32)[None]).reshape(-1)
    length = lax.dynamic_index_in_dim(lengths, net.seq_at, 0, keepdims=False)
    key_mask = places < length
    there, back = net.order()
    order = there.astype(jnp.int32)

    joint_bias = jnp.concatenate([query_bias, jnp.zeros_like(query_bias), value_bias])
    projected = (contract_cols(normed_low, w_query) + joint_bias).astype(BF)
    net.gather_neighbours(projected)
    attn_low = attend_forward(projected, key_mask)
    first_sum = flat + contract_cols(attn_low, w_proj) + out_bias
    normed_two_low = (layer_norm(first_sum) * gain_two + bias_two).astype(BF)
    net.gather_diagonal(normed_two_low)

    bias_there = fc1_bias.reshape(PIECES, -1)[there].reshape(8, -1)
    sums, grad_bias_there, tokens = [], {}, ()
    for parts in ((0, 4), (5, 6), (1, 2), (3, 7)):
        bias = jnp.concatenate([bias_there[at] for at in parts])
        packed = [net.packed_part(at) for at in parts]
        *sums, grad_bias, grads = (
            lambda out, dh, dbias, *grads: (out, dh, dbias, grads)
        )(*mlp(after(normed_two_low, *tokens), upstream_low, bias, packed, sums))
        grad_bias_there |= dict(zip(parts, grad_bias.reshape(len(parts), -1)))
        net.hidden_ready(parts, grads)
        tokens = net.send_neighbours() if parts == (1, 2) else ()
    second_sum = first_sum + sums[0] + fc2_bias
    grad_bias_there = jnp.stack([grad_bias_there[at] for at in range(8)]).reshape(PIECES, -1)
    grad_fc1_bias = grad_bias_there[back].reshape(-1)
    grad_fc2_bias = jnp.sum(upstream_low.astype(F32), axis=0)

    grad_first_sum, grad_attn, proj_near, proj_far, middle_sums = middle(
        order, first_sum, after(sums[1], *tokens), upstream_low, attn_low, w_proj, gain_two
    )
    tokens = (*net.proj_ready(proj_near, proj_far), *net.send_diagonal())
    query_near, query_far, grad_patches, vector_blocks = attend_backward(
        order, projected, key_mask, after(grad_attn, *tokens), normed_low, w_query,
        strip, grad_first_sum, gain_one,
        (middle_sums, grad_fc1_bias.reshape(4, width), grad_fc2_bias[None]),
    )
    shares, share_vector = net.query_ready(query_near, query_far, vector_blocks)
    mixed, grad_patches = net.from_strip(
        jnp.stack([v.reshape(seq, part_rows, width) for v in (second_sum.astype(BF), grad_patches)], axis=1)
    )

    counts = [share.shape[0] for share in shares]
    most = max(counts)
    stack_low = lambda parts: jnp.stack(
        [jnp.pad(part.astype(BF), ((0, most - part.shape[0]), (0, 0))) for part in parts]
    )
    moments = (mom_qkv, mom_out, mom_fc1, mom_fc2)
    weights_old = (w_qkv, w_out, w_fc1, w_fc2)
    owned_moment = net.to_owner(stack_low([net.piece(moment) for moment in net.with_query(moments)]))
    squares = sum(jnp.sum(share * share, axis=0) for share in shares)
    squares = squares + net.vector_squares(share_vector)
    owned_share, total_squares = net.to_owner_and_sum(stack_low(shares), squares)
    grad_norm = jnp.sqrt(total_squares)
    clip = jnp.minimum(1.0, CLIP / (grad_norm + 1e-06))

    mine = MOMENTUM * owned_moment.astype(F32) + clip * owned_share.astype(F32)
    mine = mine.reshape(-1, width)
    gram_part = lax.dot_general(
        mine, mine, ROWS_LAST, precision=lax.Precision.HIGH, preferred_element_type=F32
    )
    upper = [
        gram_part[THIRD * i : THIRD * (i + 1), THIRD * j : THIRD * (j + 1)] for i, j in BLOCKS
    ]
    moments_new = net.update(moments, shares, clip)
    order, pieces = net.sum_owner(
        jnp.concatenate(upper, axis=0), (mixed, grad_patches), moments_new
    )
    weights_new = net.finish(weights_old, orthogonal(order, pieces, mine))
    results = [value for pair in zip(moments_new, weights_new) for value in pair]
    vector_grad = clip * share_vector
    first_new = BETA_ONE * vec_first + (1.0 - BETA_ONE) * vector_grad
    second_new = BETA_TWO * vec_second + (1.0 - BETA_TWO) * vector_grad * vector_grad
    first_hat = first_new / (1.0 - BETA_ONE**ADAM_STEP)
    second_hat = second_new / (1.0 - BETA_TWO**ADAM_STEP)
    vectors_new = vectors - VEC_RATE * first_hat / (jnp.sqrt(second_hat) + 1e-08)
    return (mixed, grad_patches, grad_norm, *results, first_new, second_new, vectors_new)


def solution(mesh):
    rows, flat, full = P("dp", None), P("dp"), P("dp", "seq", None)
    return jax.shard_map(
        shards,
        mesh=mesh,
        in_specs=(full, full, flat) + (rows,) * 8 + (flat,) * 3,
        out_specs=(full, full, P()) + (rows,) * 8 + (flat,) * 3,
        check_vma=False,
    )
```

```python
import functools
import math

import jax
import jax.numpy as jnp
from jax import lax
from jax.experimental import pallas as pl
from jax.experimental.pallas import tpu as pltpu
from jax.sharding import PartitionSpec as P

D = 768
FF = 3072
HEADS = 12
ITERS = 5
ADAM_STEP = 10

NEG_BIG = -1e30
LN_EPS = 1e-06
NS_COEFFS = (3.4445, -4.775, 2.0315)
MOMENTUM = 0.5
CLIP = 1.0
DECAY = 0.01
MATRIX_RATES = (1.0, 3.0, 1.0, 0.6)
VEC_RATE = 0.1
BETA_ONE = 0.5
BETA_TWO = 0.5
ROWS_LAST = (((0,), (0,)), ((), ()))
COLS_LAST = (((1,), (1,)), ((), ()))
BOTH = ("dp", "seq")
MIB = 1024 * 1024
PIECES = 32
VECTOR_ROWS = 12
BF = jnp.bfloat16
F32 = jnp.float32


def layer_norm(values):
    centre = values - jnp.mean(values, axis=-1, keepdims=True)
    spread = jnp.mean(centre * centre, axis=-1, keepdims=True)
    return centre * lax.rsqrt(spread + LN_EPS)


def split_vector(vector):
    bounds = [0, D, 2 * D, 3 * D, 4 * D, 5 * D, 6 * D, 7 * D, 7 * D + FF, 8 * D + FF]
    return [vector[bounds[position] : bounds[position + 1]] for position in range(9)]


def contract_rows(left, right):
    return lax.dot_general(left, right, ROWS_LAST, preferred_element_type=F32)


def contract_cols(left, right):
    return lax.dot_general(left, right, COLS_LAST, preferred_element_type=F32)


def after(value, *others):
    return lax.optimization_barrier((value,) + others)[0]


def cost(microseconds):
    return pl.CostEstimate(
        flops=int(1e9 * microseconds), bytes_accessed=int(3e6 * microseconds), transcendentals=0
    )


def place_kernel(cuts, order_ref, *refs):
    sources, outs, sem = refs[: -len(cuts) - 1], refs[-len(cuts) - 1 : -1], refs[-1]
    copies = []
    for place_at, (source, piece) in enumerate(
        (source, piece) for source in sources for piece in range(source.shape[0])
    ):
        start = 0
        for cut, out in zip(cuts, outs):
            taken = source.at[piece, pl.ds(start, cut)] if len(cuts) > 1 else source.at[piece]
            target = out.at[order_ref[place_at]]
            copies.append(pltpu.make_async_copy(taken, target, sem.at[len(copies)]))
            start += cut
            copies[-1].start()
    for copy in copies:
        copy.wait()


def place(order, *sources, cuts=None, expected=0.3):
    count = sum(source.shape[0] for source in sources)
    cuts = cuts or [sources[0].shape[1]]
    return pl.pallas_call(
        functools.partial(place_kernel, tuple(cuts)),
        out_shape=[
            jax.ShapeDtypeStruct((count, cut) + sources[0].shape[2:], sources[0].dtype)
            for cut in cuts
        ],
        in_specs=[pl.BlockSpec(memory_space=pltpu.SMEM)]
        + [pl.BlockSpec(memory_space=pl.ANY)] * len(sources),
        out_specs=[pl.BlockSpec(memory_space=pltpu.VMEM)] * len(cuts),
        scratch_shapes=[pltpu.SemaphoreType.DMA((count * len(cuts),))],
        cost_estimate=cost(expected),
        compiler_params=pltpu.CompilerParams(vmem_limit_bytes=56 * MIB),
    )(order, *sources)


class Plain:
    def __init__(self, dp, seq):
        self.dp, self.seq = dp, seq
        self.dp_at, self.seq_at = lax.axis_index("dp"), lax.axis_index("seq")
        self.owned = self.seq_at

    def piece(self, block):
        rows = block.shape[0] // self.seq
        return lax.dynamic_slice_in_dim(block, self.seq_at * rows, rows, 0)

    def gather_rows(self, blocks, vector):
        self.rows = [lax.all_gather(block, "dp", axis=0, tiled=True) for block in (*blocks, vector)]

    def gather_whole(self, block):
        return lax.all_gather(self.piece(block), BOTH).reshape(-1, block.shape[1])

    def gather_packed(self, blocks, first):
        wholes = [self.gather_whole(block).reshape(8, 4, -1, D) for block in blocks]
        self.packed = list(jnp.concatenate(wholes, axis=2))

    def placed_rows(self, *first):
        return self.rows

    def gather_neighbours(self, first):
        pass

    def gather_diagonal(self, first):
        pass

    def packed_part(self, at):
        return self.packed[at]

    def order(self):
        return jnp.arange(PIECES), jnp.arange(PIECES)

    def reduce(self, near, far):
        whole = jnp.concatenate([near, far], axis=0).reshape(-1, D).astype(F32)
        return lax.psum_scatter(whole, BOTH, scatter_dimension=0, tiled=True)

    def hidden_ready(self, at, grads):
        self.hidden = getattr(self, "hidden", {}) | dict(zip(at, grads))

    def send_diagonal(self):
        return ()

    def send_neighbours(self):
        return ()

    def proj_ready(self, near, far):
        self.proj = (near, far)
        return ()

    def query_ready(self, near, far, vector):
        whole = jnp.stack([self.hidden[at] for at in range(8)])
        first, second = [self.reduce(whole[:4, :, kind], whole[4:, :, kind]) for kind in range(2)]
        entries = 12 * D // self.dp
        vector = jnp.concatenate([vector[:, 0], vector[:, 1, : D // 2]], axis=1).reshape(self.dp, entries)
        vector = lax.psum_scatter(lax.psum(vector, "seq"), "dp", scatter_dimension=0)
        return (self.reduce(near, far), self.reduce(*self.proj), first, second), vector

    def with_query(self, values):
        return values

    def vector_squares(self, vector):
        return jnp.full((D,), jnp.sum(vector * vector) / (D * self.seq), F32)

    def to_owner(self, parts):
        return lax.all_to_all(parts, "seq", split_axis=0, concat_axis=0, tiled=True)

    def to_owner_and_sum(self, parts, value, shares):
        return self.to_owner(parts), jnp.sum(lax.psum(value, BOTH))

    def sum_owner(self, value, others):
        total = lax.psum(value, "dp").reshape(2, 4, -1, value.shape[-1])
        return jnp.arange(8), total, total

    def update(self, moments, shares, clip):
        result = []
        for moment, share in zip(moments, shares):
            gradient = lax.all_gather(share, "seq", axis=0, tiled=True)
            result.append(MOMENTUM * moment + clip * gradient)
        return result

    def finish(self, weights, rows):
        whole = lax.all_gather(rows, "seq")
        result = []
        for at, weight in enumerate(weights):
            keep, step = weight_factors(at)
            part = whole[at].reshape(self.seq, -1, D)[:, : weight.shape[0] // self.seq]
            result.append(weight * keep - step * part.reshape(weight.shape).astype(F32))
        return result

    def to_strip(self, parts):
        parts = lax.all_to_all(parts, "seq", split_axis=0, concat_axis=0, tiled=True)
        return [parts[:, at].reshape(-1, D) for at in range(2)]

    def from_strip(self, parts, first):
        parts = lax.all_to_all(parts, "seq", split_axis=0, concat_axis=0, tiled=True)
        self.strips = [parts[:, at] for at in range(parts.shape[1])]

    def placed_strips(self):
        return self.strips

    def owners(self):
        return jnp.arange(self.seq, dtype=jnp.int32)


class Paths(Plain):
    def __init__(self, dp, seq):
        super().__init__(dp, seq)
        self.me = self.dp_at * seq + self.seq_at
        self.low = self.me & 7
        self.z = self.me >> 3
        self.owned = (self.me >> 1) & 3

    def swap(self, value, mask):
        return lax.ppermute(value, BOTH, [(d, d ^ mask) for d in range(32)])

    def climb(self, value, steps):
        return lax.ppermute(value, BOTH, [(d, (d + 8 * steps) % 32) for d in range(32)])

    def order(self):
        masks = (0, 2, 4, 6, 1, 3, 5, 7)
        order = [((self.z - k) & 3) * 8 + (self.low ^ mask) for mask in masks for k in range(4)]
        piece = jnp.arange(PIECES)
        mask = (piece & 7) ^ self.low
        tile = (mask >> 1) + 4 * (mask & 1)
        return jnp.stack(order), tile * 4 + ((self.z - (piece >> 3)) & 3)

    def column(self, part):
        part = part[None]
        return jnp.concatenate([part] + [self.climb(part, k) for k in (1, 2, 3)], axis=0)

    def gather_rows(self, blocks, vector):
        self.entries = vector.shape[0] // 4
        extra = lax.dynamic_slice_in_dim(vector, self.seq_at * self.entries, self.entries, 0)
        extra = jnp.pad(extra[None], ((0, 7), (0, D - self.entries)))
        parts = [self.piece(block) for block in blocks] + [extra]
        self.cuts = [part.shape[0] for part in parts]
        part = jnp.concatenate(parts, axis=0)[None]
        column = jnp.concatenate([part] + [self.climb(part, k) for k in (1, 2, 3)], axis=0)
        self.arrived = [self.swap(column, mask) for mask in (2, 4, 6)]
        near = [column] + self.arrived
        self.pieces = near + [self.swap(v, 1) for v in near]
        return column

    def placed_rows(self, *first):
        order = self.order()[0].astype(jnp.int32)
        self.pieces[7] = after(self.pieces[7], *first)
        *parts, extra = place(order, *self.pieces, cuts=self.cuts)
        return *[part.reshape(-1, D) for part in parts], extra[:, 0, : self.entries].reshape(-1)

    def gather_packed(self, blocks, first):
        held = jnp.concatenate([self.piece(block) for block in blocks], axis=0)[None]
        held = jnp.concatenate([held, self.climb(held, 1)], axis=0)
        self.packed = [held, self.climb(after(held, first), 2)]

    def gather_neighbours(self, first):
        held, climbed = self.packed
        sent = jnp.concatenate([held, after(climbed, first)], axis=0)
        self.packed = [sent, self.swap(sent, 2), self.swap(sent, 4), None]

    def gather_diagonal(self, first):
        self.packed[3] = self.swap(after(self.packed[0], first, *self.packed[1:3]), 6)
        self.packed += [self.swap(v, 1) for v in self.packed]

    def packed_part(self, at):
        return self.packed[at]

    def both_cores(self, near, far):
        return near.astype(F32) + far.astype(F32)

    def hidden_ready(self, at, grads):
        held = getattr(self, "hidden", {})
        for place_at, grad in zip(at, grads):
            held[place_at] = self.swap(grad, 1) if place_at >= 4 else grad
        self.hidden = held

    def half(self, at):
        return self.both_cores(self.hidden[at], self.hidden[at + 4])

    def send_diagonal(self):
        sent = self.half(3).astype(BF)
        self.received.append(self.swap(sent, 6))
        return (sent,)

    def send_neighbours(self):
        sent = [self.half(at).astype(BF) for at in (1, 2)]
        self.received = [self.swap(sent[0], 2), self.swap(sent[1], 4)]
        return sent

    def proj_ready(self, near, far):
        self.proj = [near.reshape(4, 4, -1, D), self.swap(far, 1).reshape(4, 4, -1, D)]
        return (self.proj[1],)

    def query_ready(self, near, far, vector):
        far = after(far, *self.received)
        query = [near.reshape(4, 4, -1, D), self.swap(far, 1).reshape(4, 4, -1, D)]
        vector = (vector + self.swap(vector, 1)).astype(BF)
        levels = jnp.stack([((self.z - k) & 3) * 2 + (self.low >> 2) for k in range(4)])
        vector = [vector[levels], vector[levels ^ 1]]
        joint = lambda at: jnp.concatenate(
            [self.both_cores(near[at], far[at]) for near, far in (query, self.proj)]
            + [vector[at >> 1].astype(F32)],
            axis=1,
        )
        sent = [joint(at).astype(BF) for at in (1, 2, 3)]
        received = [self.swap(sent[at - 1], 2 * at) for at in (1, 2, 3)]
        self.query_received = received
        self.received = [after(part, *sent) for part in self.received]
        hidden = self.both_cores(self.hidden[0], self.hidden[4])
        for part in self.received:
            hidden = hidden + part.astype(F32)
        hidden = hidden.reshape(4, -1, D)
        low = hidden.astype(BF)
        both = hidden[0]
        climbed = [self.climb(low[k] if k < 3 else after(low[k], received[0]), -k) for k in (1, 2, 3)]
        total = joint(0)
        for part in received:
            total = total + part.astype(F32)
        low = total.astype(BF)
        last = total[0]
        for k in (1, 2, 3):
            last = last + self.climb(low[k], -k).astype(F32)
            both = both + climbed[k - 1].astype(F32)
        cut, end, rows = query[0].shape[2], last.shape[0] - 8, both.shape[0] // 2
        return (
            (last[:cut], last[cut:end], both[:rows], both[rows:]),
            jnp.concatenate([last[end], last[end + 1, : D // 2]]),
        )

    def with_query(self, values):
        return lax.optimization_barrier((*values, *self.query_received))[: len(values)]

    def vector_squares(self, vector):
        terms = vector * vector * (1.0 / self.seq)
        return terms[:D] + jnp.pad(terms[D:], (0, D // 2))

    def pick(self, parts, at):
        return lax.dynamic_index_in_dim(parts, at, 0, keepdims=False)

    def to_owner(self, parts):
        own = self.pick(parts, self.owned)
        return jnp.stack(
            [own] + [self.swap(self.pick(parts, self.owned ^ j), 2 * j) for j in (1, 2, 3)]
        )

    def to_owner_and_sum(self, parts, value, shares):
        terms, rest = [], value
        for _ in range(3):
            terms.append(lax.reduce_precision(rest, 8, 7))
            rest = rest - terms[-1]
        extra = jnp.stack(terms + [jnp.zeros((D,), F32)] * 5)
        extra = jnp.broadcast_to(extra.astype(BF)[None], (4, 8, D))
        whole = self.to_owner(jnp.concatenate([parts, extra], axis=1))
        count = parts.shape[1]
        sums = whole[:, count : count + 3].astype(F32)
        sums = (sums[:, 0] + sums[:, 1]) + sums[:, 2]
        total = ((sums[0] + sums[1]) + (sums[2] + sums[3]))[None]
        total = total + self.swap(total, 1)
        one, two, three = [self.climb(total, k) for k in (1, 2, 3)]
        block = jnp.concatenate([share.astype(BF) for share in shares], axis=0)
        self.blocks = [block, self.swap(after(block, whole), 2)]
        three = after(three, self.blocks[1])
        return whole[:, :count], jnp.sum((total + two) + (one + three))

    def sum_owner(self, value, others):
        rows, core = value.shape[0] // 8, self.low & 1
        halves = value.reshape((2, 4, rows) + value.shape[1:])
        half = self.pick(halves, core) + self.swap(self.pick(halves, 1 - core), 1)
        level = lambda k: self.pick(half, (self.z + k) & 3)
        share = level(0)
        for k in (1, 2, 3):
            share = share + self.climb(level(k), k)
        column = after(jnp.stack([share] + [self.climb(share, k) for k in (1, 2, 3)]), *others)
        order = [at * 4 + ((self.z - k) & 3) for at in (core, 1 - core) for k in range(4)]
        return jnp.stack(order), jnp.stack([column, self.swap(column, 1)]), share

    def update(self, moments, shares, clip):
        first = jnp.stack(self.blocks)
        second = self.swap(first, 1)
        places = [((q ^ self.seq_at) >> 1) + 2 * ((q ^ self.seq_at) & 1) for q in range(4)]
        return update_moments(jnp.stack(places), clip, first, second, moments)

    def finish(self, weights, rows):
        parts = after(rows.reshape(4, -1, D), *self.back[1:])
        mine, theirs = parts[:2], parts[2:]
        near = jnp.stack([mine, self.swap(mine, 2), self.swap(theirs, 4), self.swap(theirs, 6)])
        far = self.swap(near, 1)
        x, core = (self.low >> 1) & 1, self.low & 1
        places = []
        for matrix in range(4):
            j = self.owned ^ matrix
            for q in range(4):
                places.append((core ^ (q & 1)) * 8 + j * 2 + (x ^ (j & 1) ^ (q >> 1)))
        cut = (8,) + parts.shape[1:]
        return update_weights(jnp.stack(places), near.reshape(cut), far.reshape(cut), weights)

    def exchange(self, parts, first):
        return [first] + [self.swap(self.pick(parts, self.seq_at ^ k), k) for k in (1, 2, 3)]

    def to_strip(self, parts):
        parts = self.exchange(parts, self.pick(parts, self.seq_at))
        return [jnp.concatenate([part[at] for part in parts], axis=0) for at in range(2)]

    def from_strip(self, parts, first):
        parts = after(parts, first)
        self.back = [parts[0]] + [self.swap(parts[k], k) for k in (1, 2, 3)]

    def placed_strips(self):
        order = jnp.stack([self.seq_at ^ k for k in range(4)]).astype(jnp.int32)
        cuts = [self.back[0].shape[1]] * self.back[0].shape[0]
        flat = [v.reshape(1, -1, D) for v in self.back]
        return place(order, *flat, cuts=cuts, expected=4)

    def owners(self):
        return jnp.arange(4, dtype=jnp.int32) ^ self.seq_at


def weight_factors(at):
    rate = MATRIX_RATES[at]
    return 1.0 - rate * DECAY, rate * math.sqrt((3 * D, D, FF, FF)[at] / D)


def update_moments_kernel(place_ref, clip_ref, near, far, *refs):
    moments, results, held, sem = refs[:4], refs[4:8], refs[8], refs[9]
    copies = [
        pltpu.make_async_copy(source, held.at[pl.ds(2 * at, 2)], sem.at[at])
        for at, source in enumerate((near, far))
    ]
    for copy in copies:
        copy.start()
    for copy in copies:
        copy.wait()
    for q in range(4):
        block = held[place_ref[q]].astype(F32) * clip_ref[0]
        start = 0
        for moment, result in zip(moments, results):
            rows = moment.shape[0] // 4
            at = slice(q * rows, (q + 1) * rows)
            result[at, :] = MOMENTUM * moment[at, :] + block[start : start + rows]
            start += rows


def update_moments(places, clip, near, far, moments):
    vmem, smem = pl.BlockSpec(memory_space=pltpu.VMEM), pl.BlockSpec(memory_space=pltpu.SMEM)
    anywhere = pl.BlockSpec(memory_space=pl.ANY)
    return pl.pallas_call(
        update_moments_kernel,
        out_shape=[jax.ShapeDtypeStruct(moment.shape, F32) for moment in moments],
        in_specs=[smem, smem, anywhere, anywhere] + [vmem] * 4,
        out_specs=[vmem] * 4,
        scratch_shapes=[
            pltpu.VMEM((4,) + near.shape[1:], BF),
            pltpu.SemaphoreType.DMA((2,)),
        ],
        cost_estimate=cost(6),
        compiler_params=pltpu.CompilerParams(vmem_limit_bytes=16 * MIB),
    )(places.astype(jnp.int32), clip.reshape(1), near, far, *moments)


def update_weights_kernel(place_ref, near, far, *refs):
    weights, results, held, sem = refs[:4], refs[4:8], refs[8], refs[9]
    copies = [
        pltpu.make_async_copy(source, held.at[pl.ds(8 * at, 8)], sem.at[at])
        for at, source in enumerate((near, far))
    ]
    for copy in copies:
        copy.start()
    for copy in copies:
        copy.wait()
    for matrix, (weight, result) in enumerate(zip(weights, results)):
        keep, step = weight_factors(matrix)
        rows = weight.shape[0] // 4
        for q in range(4):
            at = slice(q * rows, (q + 1) * rows)
            block = held[place_ref[4 * matrix + q]].astype(F32)
            result[at, :] = weight[at, :] * keep - step * block[:rows]


def update_weights(places, near, far, weights):
    vmem, smem = pl.BlockSpec(memory_space=pltpu.VMEM), pl.BlockSpec(memory_space=pltpu.SMEM)
    anywhere = pl.BlockSpec(memory_space=pl.ANY)
    return pl.pallas_call(
        update_weights_kernel,
        out_shape=[jax.ShapeDtypeStruct(weight.shape, F32) for weight in weights],
        in_specs=[smem, anywhere, anywhere] + [vmem] * 4,
        out_specs=[vmem] * 4,
        scratch_shapes=[
            pltpu.VMEM((16,) + near.shape[1:], BF),
            pltpu.SemaphoreType.DMA((2,)),
        ],
        cost_estimate=cost(0.3),
        compiler_params=pltpu.CompilerParams(vmem_limit_bytes=16 * MIB),
    )(places.astype(jnp.int32), near, far, *weights)


def forward_kernel(mask_ref, q_ref, k_ref, v_ref, out_ref):
    keep = mask_ref[...] > 0.0
    for head in range(2):
        at = slice(64 * head, 64 * head + 64)
        scores = contract_cols(q_ref[:, at] * BF(0.125), k_ref[:, at])
        scores = jnp.where(keep, scores, NEG_BIG)
        raised = jnp.exp(scores - jnp.max(scores, axis=1, keepdims=True))
        totals = jnp.sum(raised, axis=1, keepdims=True)
        softmaxed = (raised * (1.0 / totals)).astype(BF)
        mixed = jnp.dot(softmaxed, v_ref[:, at], preferred_element_type=F32)
        out_ref[:, at] = mixed.astype(BF)


def write_pieces(order_ref, source, near_ref, far_ref):
    rows = near_ref.shape[1]
    for at in range(PIECES):
        target = near_ref if at < PIECES // 2 else far_ref
        piece = source[pl.ds(pl.multiple_of(order_ref[at] * rows, 8), rows), :]
        target[at % (PIECES // 2)] = piece.astype(BF)


def backward_kernel(
    order_ref, mask_ref, q_ref, k_ref, v_ref, up_ref, h_ref, wq_ref, wk_ref, wv_ref,
    strip_ref, dsum_ref, gain_ref, middle_ref, first_ref, second_ref,
    near_ref, far_ref, out_ref, blocks_ref, sums, grad, dh_ref,
):
    pair = pl.program_id(0)
    keep = mask_ref[...] > 0.0
    grads = [[], [], []]
    for head in range(2):
        at = slice(64 * head, 64 * head + 64)
        queries, keys_in, upstream = q_ref[:, at] * BF(0.125), k_ref[:, at], up_ref[:, at]
        scores = jnp.where(keep, contract_cols(keys_in, queries), NEG_BIG)
        raised = jnp.exp(scores - jnp.max(scores, axis=0, keepdims=True))
        softmaxed = raised * (1.0 / jnp.sum(raised, axis=0, keepdims=True))
        dprob = contract_cols(v_ref[:, at], upstream)
        weighted = jnp.sum(softmaxed * dprob, axis=0, keepdims=True)
        dscore = (softmaxed * (dprob - weighted)).astype(BF)
        grads[2].append(jnp.dot(softmaxed.astype(BF), upstream, preferred_element_type=F32))
        grads[1].append(jnp.dot(dscore, queries, preferred_element_type=F32))
        grads[0].append(contract_rows(dscore, keys_in) * 0.125)
    joint = [jnp.concatenate(parts, axis=1).astype(BF) for parts in grads]
    lanes = pl.ds(pl.multiple_of(pair * 128, 128), 128)
    sums[2:3, lanes] = jnp.sum(joint[0].astype(F32), axis=0, keepdims=True)
    sums[3:4, lanes] = jnp.sum(joint[2].astype(F32), axis=0, keepdims=True)
    joint = jnp.concatenate(joint, axis=1)
    band_grads = contract_rows(joint, h_ref[...])
    for part in range(3):
        rows = pl.ds(pl.multiple_of(part * D + pair * 128, 128), 128)
        grad[rows, :] = band_grads[128 * part : 128 * part + 128]
    weight = jnp.concatenate([wq_ref[...], wk_ref[...], wv_ref[...]], axis=0)
    dhidden = jnp.dot(joint, weight, preferred_element_type=F32)

    @pl.when(pair == 0)
    def _():
        dh_ref[...] = dhidden

    @pl.when(pair > 0)
    def _():
        dh_ref[...] += dhidden

    @pl.when(pair == HEADS // 2 - 1)
    def _():
        write_pieces(order_ref, grad, near_ref, far_ref)
        change = norm_backward(strip_ref[...].astype(F32), dh_ref[...], gain_ref[...], sums)
        out_ref[...] = (dsum_ref[...] + change).astype(BF)
        sums[4:5, :] = middle_ref[2:3, :]
        sums[5:7, :] = middle_ref[0:2, :]
        sums[7:11, :] = first_ref[...]
        sums[11:12, :] = second_ref[...]
        blocks_ref[...] = jnp.zeros(blocks_ref.shape, F32)
        half = D // 2
        for at in range(0, VECTOR_ROWS, 3):
            one, two, three = [sums[row : row + 1, :] for row in range(at, at + 3)]
            even, odd = 2 * at // 3, 2 * at // 3 + 1
            blocks_ref[even, 0:1, :] = one
            blocks_ref[even, 1:2, :half] = two[:, :half]
            blocks_ref[odd, 0:1, :half] = two[:, half:]
            blocks_ref[odd, 0:1, half:] = three[:, :half]
            blocks_ref[odd, 1:2, :half] = three[:, half:]


def norm_backward(values, dhidden, gain, sums_ref):
    centre = values - jnp.mean(values, axis=1, keepdims=True)
    scale = lax.rsqrt(jnp.mean(centre * centre, axis=1, keepdims=True) + LN_EPS)
    normed = centre * scale
    dnormed = dhidden * gain
    inner = jnp.mean(dnormed * normed, axis=1, keepdims=True)
    sums_ref[0:1, :] = jnp.sum(dhidden * normed, axis=0, keepdims=True)
    sums_ref[1:2, :] = jnp.sum(dhidden, axis=0, keepdims=True)
    return scale * (dnormed - jnp.mean(dnormed, axis=1, keepdims=True) - normed * inner)


def head_pair(rows, shift):
    return pl.BlockSpec((rows, 128), lambda pair: (0, pair + shift))


def attend_forward(projected, key_mask):
    rows = projected.shape[0]
    return pl.pallas_call(
        forward_kernel,
        grid=(HEADS // 2,),
        out_shape=jax.ShapeDtypeStruct((rows, D), BF),
        in_specs=[pl.BlockSpec((1, rows), lambda pair: (0, 0))]
        + [head_pair(rows, HEADS // 2 * part) for part in range(3)],
        out_specs=head_pair(rows, 0),
        cost_estimate=cost(0.3),
        compiler_params=pltpu.CompilerParams(vmem_limit_bytes=14 * MIB),
    )(key_mask.astype(F32)[None], projected, projected, projected)


def attend_backward(order, projected, key_mask, upstream, hidden, weight, strip, dsum, gain, vectors):
    rows, pairs = projected.shape[0], HEADS // 2
    whole = lambda *shape: pl.BlockSpec(shape, lambda pair: (0,) * len(shape))
    band = lambda part: pl.BlockSpec((128, D), lambda pair: (pair + pairs * part, 0))
    half = (PIECES // 2, 3 * D // PIECES, D)
    return pl.pallas_call(
        backward_kernel,
        grid=(pairs,),
        out_shape=[jax.ShapeDtypeStruct(half, BF)] * 2
        + [jax.ShapeDtypeStruct((rows, D), BF), jax.ShapeDtypeStruct((8, 8, D), F32)],
        in_specs=[pl.BlockSpec(memory_space=pltpu.SMEM), whole(rows, 1)]
        + [head_pair(rows, pairs * part) for part in range(3)]
        + [head_pair(rows, 0), whole(rows, D)]
        + [band(part) for part in range(3)]
        + [whole(rows, D)] * 2
        + [whole(1, D), whole(8, D), whole(4, D), whole(1, D)],
        out_specs=[whole(*half)] * 2 + [whole(rows, D), whole(8, 8, D)],
        scratch_shapes=[
            pltpu.VMEM((16, D), F32),
            pltpu.VMEM((3 * D, D), F32),
            pltpu.VMEM((rows, D), F32),
        ],
        cost_estimate=cost(0.3),
        compiler_params=pltpu.CompilerParams(vmem_limit_bytes=28 * MIB),
    )(
        order, key_mask.astype(F32)[:, None], projected, projected, projected, upstream,
        hidden, weight, weight, weight, strip, dsum, gain[None], *vectors,
    )


def middle_kernel(
    order_ref, sum_ref, dh_ref, up_ref, attn_ref, w_ref, gain_ref,
    dsum_ref, dattn_ref, near_ref, far_ref, sums_ref, grad,
):
    change = norm_backward(sum_ref[...], dh_ref[...], gain_ref[...], sums_ref)
    dsum = up_ref[...].astype(F32) + change
    dsum_ref[...] = dsum
    low = dsum.astype(BF)
    dattn_ref[...] = jnp.dot(low, w_ref[...], preferred_element_type=F32).astype(BF)
    grad[...] = contract_rows(low, attn_ref[...])
    write_pieces(order_ref, grad, near_ref, far_ref)
    sums_ref[2:3, :] = jnp.sum(dsum, axis=0, keepdims=True)


def middle(order, first_sum, dhidden, upstream, attended, weight, gain):
    rows = first_sum.shape[0]
    half = (PIECES // 2, D // PIECES, D)
    vmem = pl.BlockSpec(memory_space=pltpu.VMEM)
    return pl.pallas_call(
        middle_kernel,
        out_shape=[
            jax.ShapeDtypeStruct((rows, D), F32),
            jax.ShapeDtypeStruct((rows, D), BF),
            jax.ShapeDtypeStruct(half, BF),
            jax.ShapeDtypeStruct(half, BF),
            jax.ShapeDtypeStruct((8, D), F32),
        ],
        in_specs=[pl.BlockSpec(memory_space=pltpu.SMEM)] + [vmem] * 6,
        out_specs=[vmem] * 5,
        scratch_shapes=[pltpu.VMEM((D, D), F32)],
        cost_estimate=cost(0.3),
        compiler_params=pltpu.CompilerParams(vmem_limit_bytes=18 * MIB),
    )(order, first_sum, dhidden, upstream, attended, weight, gain[None])


def upper_tail(values):
    t = 1.0 / (1.0 + 0.5 * values)
    series = 0.17087277
    for factor in (
        -0.82215223, 1.48851587, -1.13520398, 0.27886807, -0.18628806,
        0.09678418, 0.37409196, 1.00002368, -1.26551223,
    ):
        series = series * t + factor
    return t * jnp.exp(series - values * values)


def mlp_kernel(first, arrays, h_ref, up_ref, bias_ref, *refs):
    if not first:
        (out_in, dh_in), refs = refs[:2], refs[2:]
    packed, (out_ref, dh_ref, dbias_ref), targets = refs[:arrays], refs[arrays : arrays + 3], refs[arrays + 3 : -2]
    held, sem = refs[-2:]
    pieces, rows = held.shape[1], held.shape[2]
    count, copies, start = pieces // 4, [], 0
    for source in packed:
        for kind in range(2):
            copy = pltpu.make_async_copy(
                source.at[:, pl.ds(kind * rows, rows)],
                held.at[kind, pl.ds(start, source.shape[0])],
                sem.at[len(copies)],
            )
            copy.start()
            copies.append(copy)
        start += source.shape[0]
    for copy in copies:
        copy.wait()
    hidden, upstream = h_ref[...], up_ref[...]
    w_first = held[0].reshape(pieces * rows, D)
    w_second = held[1].reshape(pieces * rows, D)
    before = contract_cols(hidden, w_first) + bias_ref[...]
    dact = contract_cols(upstream, w_second)
    tail = 0.5 * upper_tail(jnp.abs(before) * math.sqrt(0.5))
    below = jnp.where(before < 0.0, tail, 1.0 - tail)
    slope = below + before * (jnp.exp(-0.5 * before * before) * (1.0 / math.sqrt(2.0 * math.pi)))
    active = (before * below).astype(BF)
    dbefore = (dact * slope).astype(BF)
    dbias_ref[...] = jnp.sum(dbefore.astype(F32), axis=0, keepdims=True)
    mixed = jnp.dot(active, w_second, preferred_element_type=F32)
    dhidden = jnp.dot(dbefore, w_first, preferred_element_type=F32)
    out_ref[...] = mixed if first else out_in[...] + mixed
    dh_ref[...] = dhidden if first else dh_in[...] + dhidden
    for kind, grad in enumerate((contract_rows(dbefore, hidden), contract_rows(active, upstream))):
        grad = grad.astype(BF).reshape(count, 4, rows, D)
        for at, target in enumerate(targets):
            target[:, kind] = grad[at]


def mlp(hidden, upstream, bias, packed, sums):
    rows, piece = hidden.shape[0], FF // PIECES
    pieces, arrays = sum(part.shape[0] for part in packed), len(packed)
    vmem, anywhere = pl.BlockSpec(memory_space=pltpu.VMEM), pl.BlockSpec(memory_space=pl.ANY)
    return pl.pallas_call(
        functools.partial(mlp_kernel, not sums, arrays),
        out_shape=[jax.ShapeDtypeStruct((rows, D), F32)] * 2
        + [jax.ShapeDtypeStruct((1, pieces * piece), F32)]
        + [jax.ShapeDtypeStruct((4, 2, piece, D), BF)] * (pieces // 4),
        in_specs=[vmem] * (3 + len(sums)) + [anywhere] * arrays,
        out_specs=[vmem] * (3 + pieces // 4),
        scratch_shapes=[
            pltpu.VMEM((2, pieces, piece, D), BF),
            pltpu.SemaphoreType.DMA((2 * arrays,)),
        ],
        input_output_aliases={3: 0, 4: 1} if sums else {},
        cost_estimate=cost(0.3),
        compiler_params=pltpu.CompilerParams(vmem_limit_bytes=20 * MIB),
    )(hidden, upstream, bias.reshape(1, -1), *sums, *packed)


THIRD = D // 3
BLOCKS = [(i, j) for i in range(3) for j in range(i, 3)]


def band(i):
    return slice(THIRD * i, THIRD * (i + 1))


def split_to(blocks, high, low):
    for (i, j), block in blocks.items():
        top = block.astype(BF)
        for target, part in ((high, top), (low, None if low is None else block - top.astype(F32))):
            if target is not None:
                part = part.astype(BF)
                target[band(i), band(j)] = part
                if i != j:
                    target[band(j), band(i)] = part.T


def product(*pairs):
    blocks = {}
    for i in range(3):
        total = None
        for left, right in pairs:
            term = jnp.dot(left[band(i), :], right[:, THIRD * i :], preferred_element_type=F32)
            total = term if total is None else total + term
        for j in range(i, 3):
            blocks[i, j] = total[:, band(j - i)]
    return blocks


def combined(*terms):
    return {at: sum(factor * blocks[at] for factor, blocks in terms) for at in BLOCKS}


def on_diagonal():
    shape = (THIRD, THIRD)
    return lax.broadcasted_iota(jnp.int32, shape, 0) == lax.broadcasted_iota(jnp.int32, shape, 1)


def diagonal_mean(blocks):
    total = blocks[0, 0] + blocks[1, 1] + blocks[2, 2]
    return jnp.sum(jnp.where(on_diagonal(), total, 0.0), keepdims=True) * (1.0 / D)


def without(blocks, mean):
    shift = jnp.where(on_diagonal(), mean, 0.0)
    return {(i, j): block - shift if i == j else block for (i, j), block in blocks.items()}


def orthogonal_kernel(
    order_ref, pieces_ref, rows_ref, out_ref, packed, rest_h, rest_l, change_h, twice_h, twice_l
):
    a, b, c = NS_COEFFS
    height = pieces_ref.shape[2]
    for at in range(8):
        target = pl.ds(pl.multiple_of(order_ref[at] * height, 8), height)
        packed[target, :] = pieces_ref[at // 4, at % 4]
    gram = {pair: packed[THIRD * at : THIRD * (at + 1), :] for at, pair in enumerate(BLOCKS)}
    mean = diagonal_mean(gram)
    inverse = 1.0 / (jnp.sqrt(mean * D) + 1e-07)
    rows = rows_ref[...] * inverse
    square = inverse * inverse
    mean = mean * square
    rest = without(combined((square, gram)), mean)
    for sweep in range(ITERS):
        last, fine = sweep == ITERS - 1, 0 < sweep < ITERS - 1
        split_to(rest, rest_h, rest_l if fine else None)
        p0 = a + b * mean + c * mean * mean
        p1 = b + 2.0 * c * mean
        change = combined((p1, rest), (c, product((rest_h, rest_h))))
        split_to(change, change_h, None)
        rows = p0 * rows + jnp.dot(rows.astype(BF), change_h[...], preferred_element_type=F32)
        if not last:
            twice = combined((2.0 * p0, change), (1.0, product((change_h, change_h))))
            split_to(twice, twice_h, twice_l if fine else None)
            pairs = [(rest_h, twice_h)] + [(rest_h, twice_l), (rest_l, twice_h)] * fine
            rest = combined((p0 * p0, rest), (mean, twice), (1.0, product(*pairs)))
            shift = diagonal_mean(rest)
            rest = without(rest, shift)
            mean = mean * p0 * p0 + shift
    out_ref[...] = rows.astype(BF)


def orthogonal(order, pieces, rows):
    vmem = pl.BlockSpec(memory_space=pltpu.VMEM)
    return pl.pallas_call(
        orthogonal_kernel,
        out_shape=jax.ShapeDtypeStruct(rows.shape, BF),
        in_specs=[pl.BlockSpec(memory_space=pltpu.SMEM)] + [vmem] * 2,
        out_specs=vmem,
        scratch_shapes=[pltpu.VMEM((len(BLOCKS) * THIRD, THIRD), F32)] + [pltpu.VMEM((D, D), BF)] * 5,
        cost_estimate=cost(17),
        compiler_params=pltpu.CompilerParams(vmem_limit_bytes=20 * MIB),
    )(order.astype(jnp.int32), pieces, rows)


def shards(
    patches, cotangent, lengths,
    w_qkv, w_out, w_fc1, w_fc2,
    mom_qkv, mom_out, mom_fc1, mom_fc2,
    vectors, vec_first, vec_second,
):
    strip_count, part_rows, width = patches.shape
    dp, seq = lax.axis_size("dp"), lax.axis_size("seq")
    assert strip_count == seq == 4
    net = (Paths if (dp, seq) == (8, 4) else Plain)(dp, seq)
    row_count = part_rows * seq

    strip, upstream_low = net.to_strip(jnp.stack([patches, cotangent], axis=1))
    first = net.gather_rows([w_qkv.astype(BF), w_out.astype(BF)], vectors.astype(BF))
    net.gather_packed([w_fc1.astype(BF), w_fc2.astype(BF)], first)
    flat = strip.astype(F32)
    normed = layer_norm(flat)
    net.gather_neighbours(normed)
    w_query, w_proj, vec_low = net.placed_rows(normed, upstream_low)
    (gain_one, bias_one, query_bias, value_bias, out_bias,
     gain_two, bias_two, fc1_bias, fc2_bias) = split_vector(vec_low.astype(F32))
    normed_low = (normed * gain_one + bias_one).astype(BF)

    owners = net.owners()
    places = (owners[:, None] * part_rows + jnp.arange(part_rows, dtype=jnp.int32)[None]).reshape(-1)
    length = lax.dynamic_index_in_dim(lengths, net.seq_at, 0, keepdims=False)
    key_mask = places < length
    there, back = net.order()
    order = there.astype(jnp.int32)

    joint_bias = jnp.concatenate([query_bias, jnp.zeros_like(query_bias), value_bias])
    projected = (contract_cols(normed_low, w_query) + joint_bias).astype(BF)
    attn_low = attend_forward(projected, key_mask)
    first_sum = flat + contract_cols(attn_low, w_proj) + out_bias
    normed_two_low = (layer_norm(first_sum) * gain_two + bias_two).astype(BF)
    net.gather_diagonal(normed_two_low)

    bias_there = fc1_bias.reshape(PIECES, -1)[there].reshape(8, -1)
    sums, grad_bias_there, tokens = [], {}, ()
    for parts in ((0, 4), (5, 6), (1, 2), (3, 7)):
        bias = jnp.concatenate([bias_there[at] for at in parts])
        packed = [net.packed_part(at) for at in parts]
        *sums, grad_bias, grads = (
            lambda out, dh, dbias, *grads: (out, dh, dbias, grads)
        )(*mlp(after(normed_two_low, *tokens), upstream_low, bias, packed, sums))
        grad_bias_there |= dict(zip(parts, grad_bias.reshape(len(parts), -1)))
        net.hidden_ready(parts, grads)
        tokens = net.send_neighbours() if parts == (1, 2) else ()
    second_sum = first_sum + sums[0] + fc2_bias
    grad_bias_there = jnp.stack([grad_bias_there[at] for at in range(8)]).reshape(PIECES, -1)
    grad_fc1_bias = grad_bias_there[back].reshape(-1)
    grad_fc2_bias = jnp.sum(upstream_low.astype(F32), axis=0)

    grad_first_sum, grad_attn, proj_near, proj_far, middle_sums = middle(
        order, first_sum, after(sums[1], *tokens), upstream_low, attn_low, w_proj, gain_two
    )
    tokens = (*net.proj_ready(proj_near, proj_far), *net.send_diagonal())
    query_near, query_far, grad_patches, vector_blocks = attend_backward(
        order, projected, key_mask, after(grad_attn, *tokens), normed_low, w_query,
        strip, grad_first_sum, gain_one,
        (middle_sums, grad_fc1_bias.reshape(4, width), grad_fc2_bias[None]),
    )
    shares, share_vector = net.query_ready(query_near, query_far, vector_blocks)
    counts = [share.shape[0] for share in shares]
    most = max(counts)
    stack_low = lambda parts: jnp.stack(
        [jnp.pad(part.astype(BF), ((0, most - part.shape[0]), (0, 0))) for part in parts]
    )
    moments = (mom_qkv, mom_out, mom_fc1, mom_fc2)
    weights_old = (w_qkv, w_out, w_fc1, w_fc2)
    owned_moment = net.to_owner(stack_low([net.piece(moment) for moment in net.with_query(moments)]))
    squares = sum(jnp.sum(share * share, axis=0) for share in shares)
    squares = squares + net.vector_squares(share_vector)
    owned_share, total_squares = net.to_owner_and_sum(stack_low(shares), squares, shares)
    grad_norm = jnp.sqrt(total_squares)
    clip = jnp.minimum(1.0, CLIP / (grad_norm + 1e-06))

    mine = MOMENTUM * owned_moment.astype(F32) + clip * owned_share.astype(F32)
    mine = mine.reshape(-1, width)
    gram_part = lax.dot_general(
        mine, mine, ROWS_LAST, precision=lax.Precision.HIGH, preferred_element_type=F32
    )
    upper = [
        gram_part[THIRD * i : THIRD * (i + 1), THIRD * j : THIRD * (j + 1)] for i, j in BLOCKS
    ]
    moments_new = net.update(moments, shares, clip)
    vector_grad = clip * share_vector
    first_new = BETA_ONE * vec_first + (1.0 - BETA_ONE) * vector_grad
    second_new = BETA_TWO * vec_second + (1.0 - BETA_TWO) * vector_grad * vector_grad
    first_hat = first_new / (1.0 - BETA_ONE**ADAM_STEP)
    second_hat = second_new / (1.0 - BETA_TWO**ADAM_STEP)
    vectors_new = vectors - VEC_RATE * first_hat / (jnp.sqrt(second_hat) + 1e-08)
    strips = jnp.stack([v.reshape(seq, part_rows, width) for v in (second_sum.astype(BF), grad_patches)], axis=1)
    order, pieces, share = net.sum_owner(jnp.concatenate(upper, axis=0), (*moments_new, vectors_new))
    net.from_strip(strips, share)
    weights_new = net.finish(weights_old, orthogonal(order, pieces, mine))
    mixed, grad_patches = net.placed_strips()
    results = [value for pair in zip(moments_new, weights_new) for value in pair]
    return (mixed, grad_patches, grad_norm, *results, first_new, second_new, vectors_new)


def solution(mesh):
    rows, flat, full = P("dp", None), P("dp"), P("dp", "seq", None)
    return jax.shard_map(
        shards,
        mesh=mesh,
        in_specs=(full, full, flat) + (rows,) * 8 + (flat,) * 3,
        out_specs=(full, full, P()) + (rows,) * 8 + (flat,) * 3,
        check_vma=False,
    )
```

```python
import functools
import math

import jax
import jax.numpy as jnp
from jax import lax
from jax.experimental import pallas as pl
from jax.experimental.pallas import tpu as pltpu
from jax.sharding import PartitionSpec as P

D = 768
FF = 3072
HEADS = 12
ITERS = 5
ADAM_STEP = 10

NEG_BIG = -1e30
LN_EPS = 1e-06
NS_COEFFS = (3.4445, -4.775, 2.0315)
MOMENTUM = 0.5
CLIP = 1.0
DECAY = 0.01
MATRIX_RATES = (1.0, 3.0, 1.0, 0.6)
VEC_RATE = 0.1
BETA_ONE = 0.5
BETA_TWO = 0.5
ROWS_LAST = (((0,), (0,)), ((), ()))
COLS_LAST = (((1,), (1,)), ((), ()))
BOTH = ("dp", "seq")
MIB = 1024 * 1024
PIECES = 32
VECTOR_ROWS = 12
BF = jnp.bfloat16
F32 = jnp.float32


def layer_norm(values):
    centre = values - jnp.mean(values, axis=-1, keepdims=True)
    spread = jnp.mean(centre * centre, axis=-1, keepdims=True)
    return centre * lax.rsqrt(spread + LN_EPS)


def split_vector(vector):
    bounds = [0, D, 2 * D, 3 * D, 4 * D, 5 * D, 6 * D, 7 * D, 7 * D + FF, 8 * D + FF]
    return [vector[bounds[position] : bounds[position + 1]] for position in range(9)]


def contract_rows(left, right):
    return lax.dot_general(left, right, ROWS_LAST, preferred_element_type=F32)


def contract_cols(left, right):
    return lax.dot_general(left, right, COLS_LAST, preferred_element_type=F32)


def after(value, *others):
    return lax.optimization_barrier((value,) + others)[0]


def cost(microseconds):
    return pl.CostEstimate(
        flops=int(1e9 * microseconds), bytes_accessed=int(3e6 * microseconds), transcendentals=0
    )


def place_kernel(cuts, order_ref, *refs):
    sources, outs, sem = refs[: -len(cuts) - 1], refs[-len(cuts) - 1 : -1], refs[-1]
    copies = []
    for place_at, (source, piece) in enumerate(
        (source, piece) for source in sources for piece in range(source.shape[0])
    ):
        start = 0
        for cut, out in zip(cuts, outs):
            taken = source.at[piece, pl.ds(start, cut)] if len(cuts) > 1 else source.at[piece]
            target = out.at[order_ref[place_at]]
            copies.append(pltpu.make_async_copy(taken, target, sem.at[len(copies)]))
            start += cut
            copies[-1].start()
    for copy in copies:
        copy.wait()


def place(order, *sources, cuts=None, expected=0.3):
    count = sum(source.shape[0] for source in sources)
    cuts = cuts or [sources[0].shape[1]]
    return pl.pallas_call(
        functools.partial(place_kernel, tuple(cuts)),
        out_shape=[
            jax.ShapeDtypeStruct((count, cut) + sources[0].shape[2:], sources[0].dtype)
            for cut in cuts
        ],
        in_specs=[pl.BlockSpec(memory_space=pltpu.SMEM)]
        + [pl.BlockSpec(memory_space=pl.ANY)] * len(sources),
        out_specs=[pl.BlockSpec(memory_space=pltpu.VMEM)] * len(cuts),
        scratch_shapes=[pltpu.SemaphoreType.DMA((count * len(cuts),))],
        cost_estimate=cost(expected),
        compiler_params=pltpu.CompilerParams(vmem_limit_bytes=56 * MIB),
    )(order, *sources)


class Plain:
    def __init__(self, dp, seq):
        self.dp, self.seq = dp, seq
        self.dp_at, self.seq_at = lax.axis_index("dp"), lax.axis_index("seq")
        self.owned = self.seq_at

    def piece(self, block):
        rows = block.shape[0] // self.seq
        return lax.dynamic_slice_in_dim(block, self.seq_at * rows, rows, 0)

    def gather_rows(self, blocks, vector):
        self.rows = [lax.all_gather(block, "dp", axis=0, tiled=True) for block in (*blocks, vector)]

    def gather_whole(self, block):
        return lax.all_gather(self.piece(block), BOTH).reshape(-1, block.shape[1])

    def gather_packed(self, blocks, first):
        wholes = [self.gather_whole(block).reshape(8, 4, -1, D) for block in blocks]
        self.packed = list(jnp.concatenate(wholes, axis=2))

    def placed_rows(self, *first):
        return self.rows

    def gather_neighbours(self, first):
        pass

    def gather_diagonal(self, first):
        pass

    def packed_part(self, at):
        return self.packed[at]

    def order(self):
        return jnp.arange(PIECES), jnp.arange(PIECES)

    def reduce(self, near, far):
        whole = jnp.concatenate([near, far], axis=0).reshape(-1, D).astype(F32)
        return lax.psum_scatter(whole, BOTH, scatter_dimension=0, tiled=True)

    def hidden_ready(self, at, grads):
        self.hidden = getattr(self, "hidden", {}) | dict(zip(at, grads))

    def send_diagonal(self):
        return ()

    def send_neighbours(self):
        return ()

    def proj_ready(self, near, far):
        self.proj = (near, far)
        return ()

    def query_ready(self, near, far, vector):
        whole = jnp.stack([self.hidden[at] for at in range(8)])
        first, second = [self.reduce(whole[:4, :, kind], whole[4:, :, kind]) for kind in range(2)]
        entries = 12 * D // self.dp
        vector = jnp.concatenate([vector[:, 0], vector[:, 1, : D // 2]], axis=1).reshape(self.dp, entries)
        vector = lax.psum_scatter(lax.psum(vector, "seq"), "dp", scatter_dimension=0)
        return (self.reduce(near, far), self.reduce(*self.proj), first, second), vector

    def with_query(self, values):
        return values

    def vector_squares(self, vector):
        return jnp.full((D,), jnp.sum(vector * vector) / (D * self.seq), F32)

    def to_owner(self, parts):
        return lax.all_to_all(parts, "seq", split_axis=0, concat_axis=0, tiled=True)

    def to_owner_and_sum(self, parts, value, shares):
        return self.to_owner(parts), jnp.sum(lax.psum(value, BOTH))

    def sum_owner(self, value, others):
        total = lax.psum(value, "dp").reshape(2, 4, -1, value.shape[-1])
        return jnp.arange(8), total, total

    def update(self, moments, shares, clip):
        result = []
        for moment, share in zip(moments, shares):
            gradient = lax.all_gather(share, "seq", axis=0, tiled=True)
            result.append(MOMENTUM * moment + clip * gradient)
        return result

    def finish(self, weights, rows):
        whole = lax.all_gather(rows, "seq")
        result = []
        for at, weight in enumerate(weights):
            keep, step = weight_factors(at)
            part = whole[at].reshape(self.seq, -1, D)[:, : weight.shape[0] // self.seq]
            result.append(weight * keep - step * part.reshape(weight.shape).astype(F32))
        return result

    def to_strip(self, parts):
        parts = lax.all_to_all(parts, "seq", split_axis=0, concat_axis=0, tiled=True)
        return [parts[:, at].reshape(-1, D) for at in range(2)]

    def from_strip(self, parts, first):
        parts = lax.all_to_all(parts, "seq", split_axis=0, concat_axis=0, tiled=True)
        self.strips = [parts[:, at] for at in range(parts.shape[1])]

    def placed_strips(self):
        return self.strips

    def owners(self):
        return jnp.arange(self.seq, dtype=jnp.int32)


class Paths(Plain):
    def __init__(self, dp, seq):
        super().__init__(dp, seq)
        self.me = self.dp_at * seq + self.seq_at
        self.low = self.me & 7
        self.z = self.me >> 3
        self.owned = (self.me >> 1) & 3

    def swap(self, value, mask):
        return lax.ppermute(value, BOTH, [(d, d ^ mask) for d in range(32)])

    def climb(self, value, steps):
        return lax.ppermute(value, BOTH, [(d, (d + 8 * steps) % 32) for d in range(32)])

    def order(self):
        masks = (0, 2, 4, 6, 1, 3, 5, 7)
        order = [((self.z - k) & 3) * 8 + (self.low ^ mask) for mask in masks for k in range(4)]
        piece = jnp.arange(PIECES)
        mask = (piece & 7) ^ self.low
        tile = (mask >> 1) + 4 * (mask & 1)
        return jnp.stack(order), tile * 4 + ((self.z - (piece >> 3)) & 3)

    def column(self, part):
        part = part[None]
        return jnp.concatenate([part] + [self.climb(part, k) for k in (1, 2, 3)], axis=0)

    def gather_rows(self, blocks, vector):
        self.entries = vector.shape[0] // 4
        extra = lax.dynamic_slice_in_dim(vector, self.seq_at * self.entries, self.entries, 0)
        extra = jnp.pad(extra[None], ((0, 7), (0, D - self.entries)))
        parts = [self.piece(block) for block in blocks] + [extra]
        self.cuts = [part.shape[0] for part in parts]
        part = jnp.concatenate(parts, axis=0)[None]
        column = jnp.concatenate([part] + [self.climb(part, k) for k in (1, 2, 3)], axis=0)
        self.arrived = [self.swap(column, mask) for mask in (2, 4, 6)]
        near = [column] + self.arrived
        self.pieces = near + [self.swap(v, 1) for v in near]
        return column

    def placed_rows(self, *first):
        order = self.order()[0].astype(jnp.int32)
        self.pieces[7] = after(self.pieces[7], *first)
        *parts, extra = place(order, *self.pieces, cuts=self.cuts)
        return *[part.reshape(-1, D) for part in parts], extra[:, 0, : self.entries].reshape(-1)

    def gather_packed(self, blocks, first):
        held = jnp.concatenate([self.piece(block) for block in blocks], axis=0)[None]
        held = jnp.concatenate([held, self.climb(held, 1)], axis=0)
        self.packed = [held, self.climb(after(held, first), 2)]

    def gather_neighbours(self, first):
        held, climbed = self.packed
        sent = jnp.concatenate([held, after(climbed, first)], axis=0)
        self.packed = [sent, self.swap(sent, 2), self.swap(sent, 4), None]

    def gather_diagonal(self, first):
        self.packed[3] = self.swap(after(self.packed[0], first, *self.packed[1:3]), 6)
        self.packed += [self.swap(v, 1) for v in self.packed]

    def packed_part(self, at):
        return self.packed[at]

    def both_cores(self, near, far):
        return near.astype(F32) + far.astype(F32)

    def hidden_ready(self, at, grads):
        held = getattr(self, "hidden", {})
        for place_at, grad in zip(at, grads):
            held[place_at] = self.swap(grad, 1) if place_at >= 4 else grad
        self.hidden = held

    def half(self, at):
        return self.both_cores(self.hidden[at], self.hidden[at + 4])

    def send_diagonal(self):
        sent = self.half(3).astype(BF)
        self.received.append(self.swap(sent, 6))
        return (sent,)

    def send_neighbours(self):
        sent = [self.half(at).astype(BF) for at in (1, 2)]
        self.received = [self.swap(sent[0], 2), self.swap(sent[1], 4)]
        return sent

    def proj_ready(self, near, far):
        self.proj = [near.reshape(4, 4, -1, D), self.swap(far, 1).reshape(4, 4, -1, D)]
        return (self.proj[1],)

    def query_ready(self, near, far, vector):
        far = after(far, *self.received)
        query = [near.reshape(4, 4, -1, D), self.swap(far, 1).reshape(4, 4, -1, D)]
        vector = (vector + self.swap(vector, 1)).astype(BF)
        levels = jnp.stack([((self.z - k) & 3) * 2 + (self.low >> 2) for k in range(4)])
        vector = [vector[levels], vector[levels ^ 1]]
        joint = lambda at: jnp.concatenate(
            [self.both_cores(near[at], far[at]) for near, far in (query, self.proj)]
            + [vector[at >> 1].astype(F32)],
            axis=1,
        )
        sent = [joint(at).astype(BF) for at in (1, 2, 3)]
        received = [self.swap(sent[at - 1], 2 * at) for at in (1, 2, 3)]
        self.query_received = received
        self.received = [after(part, *sent) for part in self.received]
        hidden = self.both_cores(self.hidden[0], self.hidden[4])
        for part in self.received:
            hidden = hidden + part.astype(F32)
        hidden = hidden.reshape(4, -1, D)
        low = hidden.astype(BF)
        both = hidden[0]
        climbed = [self.climb(low[k] if k < 3 else after(low[k], received[0]), -k) for k in (1, 2, 3)]
        total = joint(0)
        for part in received:
            total = total + part.astype(F32)
        low = total.astype(BF)
        last = total[0]
        for k in (1, 2, 3):
            last = last + self.climb(low[k], -k).astype(F32)
            both = both + climbed[k - 1].astype(F32)
        cut, end, rows = query[0].shape[2], last.shape[0] - 8, both.shape[0] // 2
        return (
            (last[:cut], last[cut:end], both[:rows], both[rows:]),
            jnp.concatenate([last[end], last[end + 1, : D // 2]]),
        )

    def with_query(self, values):
        return lax.optimization_barrier((*values, *self.query_received))[: len(values)]

    def vector_squares(self, vector):
        terms = vector * vector * (1.0 / self.seq)
        return terms[:D] + jnp.pad(terms[D:], (0, D // 2))

    def pick(self, parts, at):
        return lax.dynamic_index_in_dim(parts, at, 0, keepdims=False)

    def to_owner(self, parts):
        own = self.pick(parts, self.owned)
        return jnp.stack(
            [own] + [self.swap(self.pick(parts, self.owned ^ j), 2 * j) for j in (1, 2, 3)]
        )

    def to_owner_and_sum(self, parts, value, shares):
        terms, rest = [], value
        for _ in range(3):
            terms.append(lax.reduce_precision(rest, 8, 7))
            rest = rest - terms[-1]
        extra = jnp.stack(terms + [jnp.zeros((D,), F32)] * 5)
        extra = jnp.broadcast_to(extra.astype(BF)[None], (4, 8, D))
        whole = self.to_owner(jnp.concatenate([parts, extra], axis=1))
        count = parts.shape[1]
        sums = whole[:, count : count + 3].astype(F32)
        sums = (sums[:, 0] + sums[:, 1]) + sums[:, 2]
        total = ((sums[0] + sums[1]) + (sums[2] + sums[3]))[None]
        total = total + self.swap(total, 1)
        one, two, three = [self.climb(total, k) for k in (1, 2, 3)]
        block = jnp.concatenate([share.astype(BF) for share in shares], axis=0)
        self.blocks = [block, self.swap(after(block, whole), 2)]
        three = after(three, self.blocks[1])
        return whole[:, :count], jnp.sum((total + two) + (one + three))

    def sum_owner(self, value, others):
        rows, core = value.shape[0] // 8, self.low & 1
        halves = value.reshape((2, 4, rows) + value.shape[1:])
        half = self.pick(halves, core) + self.swap(self.pick(halves, 1 - core), 1)
        level = lambda k: self.pick(half, (self.z + k) & 3)
        share = level(0)
        for k in (1, 2, 3):
            share = share + self.climb(level(k), k)
        column = after(jnp.stack([share] + [self.climb(share, k) for k in (1, 2, 3)]), *others)
        order = [at * 4 + ((self.z - k) & 3) for at in (core, 1 - core) for k in range(4)]
        return jnp.stack(order), jnp.stack([column, self.swap(column, 1)]), share

    def update(self, moments, shares, clip):
        first = jnp.stack(self.blocks)
        second = self.swap(first, 1)
        places = [((q ^ self.seq_at) >> 1) + 2 * ((q ^ self.seq_at) & 1) for q in range(4)]
        return update_moments(jnp.stack(places), clip, first, second, moments)

    def finish(self, weights, rows):
        parts = after(rows.reshape(4, -1, D), *self.back[1:])
        mine, theirs = parts[:2], parts[2:]
        near = [mine, self.swap(mine, 2), self.swap(theirs, 4), self.swap(theirs, 6)]
        self.strips = self.place_strips()
        near[3] = after(near[3], *self.strips)
        far = [self.swap(v, 1) for v in near]
        x, core = (self.low >> 1) & 1, self.low & 1
        places = []
        for matrix in range(4):
            j = self.owned ^ matrix
            for q in range(4):
                places.append((core ^ (q & 1)) * 8 + j * 2 + (x ^ (j & 1) ^ (q >> 1)))
        return update_weights(jnp.stack(places), near + far, weights)

    def exchange(self, parts, first):
        return [first] + [self.swap(self.pick(parts, self.seq_at ^ k), k) for k in (1, 2, 3)]

    def to_strip(self, parts):
        parts = self.exchange(parts, self.pick(parts, self.seq_at))
        return [jnp.concatenate([part[at] for part in parts], axis=0) for at in range(2)]

    def from_strip(self, parts, first):
        parts = after(parts, first)
        self.back = [parts[0]] + [self.swap(parts[k], k) for k in (1, 2, 3)]

    def placed_strips(self):
        return self.strips

    def place_strips(self):
        order = jnp.stack([self.seq_at ^ k for k in range(4)]).astype(jnp.int32)
        cuts = [self.back[0].shape[1]] * self.back[0].shape[0]
        flat = [v.reshape(1, -1, D) for v in self.back]
        return place(order, *flat, cuts=cuts, expected=4)

    def owners(self):
        return jnp.arange(4, dtype=jnp.int32) ^ self.seq_at


def weight_factors(at):
    rate = MATRIX_RATES[at]
    return 1.0 - rate * DECAY, rate * math.sqrt((3 * D, D, FF, FF)[at] / D)


def update_moments_kernel(place_ref, clip_ref, near, far, *refs):
    moments, results, held, sem = refs[:4], refs[4:8], refs[8], refs[9]
    copies = [
        pltpu.make_async_copy(source, held.at[pl.ds(2 * at, 2)], sem.at[at])
        for at, source in enumerate((near, far))
    ]
    for copy in copies:
        copy.start()
    for copy in copies:
        copy.wait()
    for q in range(4):
        block = held[place_ref[q]].astype(F32) * clip_ref[0]
        start = 0
        for moment, result in zip(moments, results):
            rows = moment.shape[0] // 4
            at = slice(q * rows, (q + 1) * rows)
            result[at, :] = MOMENTUM * moment[at, :] + block[start : start + rows]
            start += rows


def update_moments(places, clip, near, far, moments):
    vmem, smem = pl.BlockSpec(memory_space=pltpu.VMEM), pl.BlockSpec(memory_space=pltpu.SMEM)
    anywhere = pl.BlockSpec(memory_space=pl.ANY)
    return pl.pallas_call(
        update_moments_kernel,
        out_shape=[jax.ShapeDtypeStruct(moment.shape, F32) for moment in moments],
        in_specs=[smem, smem, anywhere, anywhere] + [vmem] * 4,
        out_specs=[vmem] * 4,
        scratch_shapes=[
            pltpu.VMEM((4,) + near.shape[1:], BF),
            pltpu.SemaphoreType.DMA((2,)),
        ],
        cost_estimate=cost(6),
        compiler_params=pltpu.CompilerParams(vmem_limit_bytes=16 * MIB),
    )(places.astype(jnp.int32), clip.reshape(1), near, far, *moments)


def update_weights_kernel(place_ref, *refs):
    sources, weights, results, held, sem = refs[:8], refs[8:12], refs[12:16], refs[16], refs[17]
    copies = [
        pltpu.make_async_copy(source, held.at[pl.ds(2 * at, 2)], sem.at[at])
        for at, source in enumerate(sources)
    ]
    for copy in copies:
        copy.start()
    for copy in copies:
        copy.wait()
    for matrix, (weight, result) in enumerate(zip(weights, results)):
        keep, step = weight_factors(matrix)
        rows = weight.shape[0] // 4
        for q in range(4):
            at = slice(q * rows, (q + 1) * rows)
            block = held[place_ref[4 * matrix + q]].astype(F32)
            result[at, :] = weight[at, :] * keep - step * block[:rows]


def update_weights(places, parts, weights):
    vmem, smem = pl.BlockSpec(memory_space=pltpu.VMEM), pl.BlockSpec(memory_space=pltpu.SMEM)
    anywhere = pl.BlockSpec(memory_space=pl.ANY)
    return pl.pallas_call(
        update_weights_kernel,
        out_shape=[jax.ShapeDtypeStruct(weight.shape, F32) for weight in weights],
        in_specs=[smem] + [anywhere] * 8 + [vmem] * 4,
        out_specs=[vmem] * 4,
        scratch_shapes=[
            pltpu.VMEM((16,) + parts[0].shape[1:], BF),
            pltpu.SemaphoreType.DMA((8,)),
        ],
        cost_estimate=cost(0.3),
        compiler_params=pltpu.CompilerParams(vmem_limit_bytes=16 * MIB),
    )(places.astype(jnp.int32), *parts, *weights)


def forward_kernel(mask_ref, q_ref, k_ref, v_ref, out_ref):
    keep = mask_ref[...] > 0.0
    for head in range(2):
        at = slice(64 * head, 64 * head + 64)
        scores = contract_cols(q_ref[:, at] * BF(0.125), k_ref[:, at])
        scores = jnp.where(keep, scores, NEG_BIG)
        raised = jnp.exp(scores - jnp.max(scores, axis=1, keepdims=True))
        totals = jnp.sum(raised, axis=1, keepdims=True)
        softmaxed = (raised * (1.0 / totals)).astype(BF)
        mixed = jnp.dot(softmaxed, v_ref[:, at], preferred_element_type=F32)
        out_ref[:, at] = mixed.astype(BF)


def write_pieces(order_ref, source, near_ref, far_ref):
    rows = near_ref.shape[1]
    for at in range(PIECES):
        target = near_ref if at < PIECES // 2 else far_ref
        piece = source[pl.ds(pl.multiple_of(order_ref[at] * rows, 8), rows), :]
        target[at % (PIECES // 2)] = piece.astype(BF)


def backward_kernel(
    order_ref, mask_ref, q_ref, k_ref, v_ref, up_ref, h_ref, wq_ref, wk_ref, wv_ref,
    strip_ref, dsum_ref, gain_ref, middle_ref, first_ref, second_ref,
    near_ref, far_ref, out_ref, blocks_ref, sums, grad, dh_ref,
):
    pair = pl.program_id(0)
    keep = mask_ref[...] > 0.0
    grads = [[], [], []]
    for head in range(2):
        at = slice(64 * head, 64 * head + 64)
        queries, keys_in, upstream = q_ref[:, at] * BF(0.125), k_ref[:, at], up_ref[:, at]
        scores = jnp.where(keep, contract_cols(keys_in, queries), NEG_BIG)
        raised = jnp.exp(scores - jnp.max(scores, axis=0, keepdims=True))
        softmaxed = raised * (1.0 / jnp.sum(raised, axis=0, keepdims=True))
        dprob = contract_cols(v_ref[:, at], upstream)
        weighted = jnp.sum(softmaxed * dprob, axis=0, keepdims=True)
        dscore = (softmaxed * (dprob - weighted)).astype(BF)
        grads[2].append(jnp.dot(softmaxed.astype(BF), upstream, preferred_element_type=F32))
        grads[1].append(jnp.dot(dscore, queries, preferred_element_type=F32))
        grads[0].append(contract_rows(dscore, keys_in) * 0.125)
    joint = [jnp.concatenate(parts, axis=1).astype(BF) for parts in grads]
    lanes = pl.ds(pl.multiple_of(pair * 128, 128), 128)
    sums[2:3, lanes] = jnp.sum(joint[0].astype(F32), axis=0, keepdims=True)
    sums[3:4, lanes] = jnp.sum(joint[2].astype(F32), axis=0, keepdims=True)
    joint = jnp.concatenate(joint, axis=1)
    band_grads = contract_rows(joint, h_ref[...])
    for part in range(3):
        rows = pl.ds(pl.multiple_of(part * D + pair * 128, 128), 128)
        grad[rows, :] = band_grads[128 * part : 128 * part + 128]
    weight = jnp.concatenate([wq_ref[...], wk_ref[...], wv_ref[...]], axis=0)
    dhidden = jnp.dot(joint, weight, preferred_element_type=F32)

    @pl.when(pair == 0)
    def _():
        dh_ref[...] = dhidden

    @pl.when(pair > 0)
    def _():
        dh_ref[...] += dhidden

    @pl.when(pair == HEADS // 2 - 1)
    def _():
        write_pieces(order_ref, grad, near_ref, far_ref)
        change = norm_backward(strip_ref[...].astype(F32), dh_ref[...], gain_ref[...], sums)
        out_ref[...] = (dsum_ref[...] + change).astype(BF)
        sums[4:5, :] = middle_ref[2:3, :]
        sums[5:7, :] = middle_ref[0:2, :]
        sums[7:11, :] = first_ref[...]
        sums[11:12, :] = second_ref[...]
        blocks_ref[...] = jnp.zeros(blocks_ref.shape, F32)
        half = D // 2
        for at in range(0, VECTOR_ROWS, 3):
            one, two, three = [sums[row : row + 1, :] for row in range(at, at + 3)]
            even, odd = 2 * at // 3, 2 * at // 3 + 1
            blocks_ref[even, 0:1, :] = one
            blocks_ref[even, 1:2, :half] = two[:, :half]
            blocks_ref[odd, 0:1, :half] = two[:, half:]
            blocks_ref[odd, 0:1, half:] = three[:, :half]
            blocks_ref[odd, 1:2, :half] = three[:, half:]


def norm_backward(values, dhidden, gain, sums_ref):
    centre = values - jnp.mean(values, axis=1, keepdims=True)
    scale = lax.rsqrt(jnp.mean(centre * centre, axis=1, keepdims=True) + LN_EPS)
    normed = centre * scale
    dnormed = dhidden * gain
    inner = jnp.mean(dnormed * normed, axis=1, keepdims=True)
    sums_ref[0:1, :] = jnp.sum(dhidden * normed, axis=0, keepdims=True)
    sums_ref[1:2, :] = jnp.sum(dhidden, axis=0, keepdims=True)
    return scale * (dnormed - jnp.mean(dnormed, axis=1, keepdims=True) - normed * inner)


def head_pair(rows, shift):
    return pl.BlockSpec((rows, 128), lambda pair: (0, pair + shift))


def attend_forward(projected, key_mask):
    rows = projected.shape[0]
    return pl.pallas_call(
        forward_kernel,
        grid=(HEADS // 2,),
        out_shape=jax.ShapeDtypeStruct((rows, D), BF),
        in_specs=[pl.BlockSpec((1, rows), lambda pair: (0, 0))]
        + [head_pair(rows, HEADS // 2 * part) for part in range(3)],
        out_specs=head_pair(rows, 0),
        cost_estimate=cost(0.3),
        compiler_params=pltpu.CompilerParams(vmem_limit_bytes=14 * MIB),
    )(key_mask.astype(F32)[None], projected, projected, projected)


def attend_backward(order, projected, key_mask, upstream, hidden, weight, strip, dsum, gain, vectors):
    rows, pairs = projected.shape[0], HEADS // 2
    whole = lambda *shape: pl.BlockSpec(shape, lambda pair: (0,) * len(shape))
    band = lambda part: pl.BlockSpec((128, D), lambda pair: (pair + pairs * part, 0))
    half = (PIECES // 2, 3 * D // PIECES, D)
    return pl.pallas_call(
        backward_kernel,
        grid=(pairs,),
        out_shape=[jax.ShapeDtypeStruct(half, BF)] * 2
        + [jax.ShapeDtypeStruct((rows, D), BF), jax.ShapeDtypeStruct((8, 8, D), F32)],
        in_specs=[pl.BlockSpec(memory_space=pltpu.SMEM), whole(rows, 1)]
        + [head_pair(rows, pairs * part) for part in range(3)]
        + [head_pair(rows, 0), whole(rows, D)]
        + [band(part) for part in range(3)]
        + [whole(rows, D)] * 2
        + [whole(1, D), whole(8, D), whole(4, D), whole(1, D)],
        out_specs=[whole(*half)] * 2 + [whole(rows, D), whole(8, 8, D)],
        scratch_shapes=[
            pltpu.VMEM((16, D), F32),
            pltpu.VMEM((3 * D, D), F32),
            pltpu.VMEM((rows, D), F32),
        ],
        cost_estimate=cost(0.3),
        compiler_params=pltpu.CompilerParams(vmem_limit_bytes=28 * MIB),
    )(
        order, key_mask.astype(F32)[:, None], projected, projected, projected, upstream,
        hidden, weight, weight, weight, strip, dsum, gain[None], *vectors,
    )


def middle_kernel(
    order_ref, sum_ref, dh_ref, up_ref, attn_ref, w_ref, gain_ref,
    dsum_ref, dattn_ref, near_ref, far_ref, sums_ref, grad,
):
    change = norm_backward(sum_ref[...], dh_ref[...], gain_ref[...], sums_ref)
    dsum = up_ref[...].astype(F32) + change
    dsum_ref[...] = dsum
    low = dsum.astype(BF)
    dattn_ref[...] = jnp.dot(low, w_ref[...], preferred_element_type=F32).astype(BF)
    grad[...] = contract_rows(low, attn_ref[...])
    write_pieces(order_ref, grad, near_ref, far_ref)
    sums_ref[2:3, :] = jnp.sum(dsum, axis=0, keepdims=True)


def middle(order, first_sum, dhidden, upstream, attended, weight, gain):
    rows = first_sum.shape[0]
    half = (PIECES // 2, D // PIECES, D)
    vmem = pl.BlockSpec(memory_space=pltpu.VMEM)
    return pl.pallas_call(
        middle_kernel,
        out_shape=[
            jax.ShapeDtypeStruct((rows, D), F32),
            jax.ShapeDtypeStruct((rows, D), BF),
            jax.ShapeDtypeStruct(half, BF),
            jax.ShapeDtypeStruct(half, BF),
            jax.ShapeDtypeStruct((8, D), F32),
        ],
        in_specs=[pl.BlockSpec(memory_space=pltpu.SMEM)] + [vmem] * 6,
        out_specs=[vmem] * 5,
        scratch_shapes=[pltpu.VMEM((D, D), F32)],
        cost_estimate=cost(0.3),
        compiler_params=pltpu.CompilerParams(vmem_limit_bytes=18 * MIB),
    )(order, first_sum, dhidden, upstream, attended, weight, gain[None])


def upper_tail(values):
    t = 1.0 / (1.0 + 0.5 * values)
    series = 0.17087277
    for factor in (
        -0.82215223, 1.48851587, -1.13520398, 0.27886807, -0.18628806,
        0.09678418, 0.37409196, 1.00002368, -1.26551223,
    ):
        series = series * t + factor
    return t * jnp.exp(series - values * values)


def mlp_kernel(first, arrays, h_ref, up_ref, bias_ref, *refs):
    if not first:
        (out_in, dh_in), refs = refs[:2], refs[2:]
    packed, (out_ref, dh_ref, dbias_ref), targets = refs[:arrays], refs[arrays : arrays + 3], refs[arrays + 3 : -2]
    held, sem = refs[-2:]
    pieces, rows = held.shape[1], held.shape[2]
    count, copies, start = pieces // 4, [], 0
    for source in packed:
        for kind in range(2):
            copy = pltpu.make_async_copy(
                source.at[:, pl.ds(kind * rows, rows)],
                held.at[kind, pl.ds(start, source.shape[0])],
                sem.at[len(copies)],
            )
            copy.start()
            copies.append(copy)
        start += source.shape[0]
    for copy in copies:
        copy.wait()
    hidden, upstream = h_ref[...], up_ref[...]
    w_first = held[0].reshape(pieces * rows, D)
    w_second = held[1].reshape(pieces * rows, D)
    before = contract_cols(hidden, w_first) + bias_ref[...]
    dact = contract_cols(upstream, w_second)
    tail = 0.5 * upper_tail(jnp.abs(before) * math.sqrt(0.5))
    below = jnp.where(before < 0.0, tail, 1.0 - tail)
    slope = below + before * (jnp.exp(-0.5 * before * before) * (1.0 / math.sqrt(2.0 * math.pi)))
    active = (before * below).astype(BF)
    dbefore = (dact * slope).astype(BF)
    dbias_ref[...] = jnp.sum(dbefore.astype(F32), axis=0, keepdims=True)
    mixed = jnp.dot(active, w_second, preferred_element_type=F32)
    dhidden = jnp.dot(dbefore, w_first, preferred_element_type=F32)
    out_ref[...] = mixed if first else out_in[...] + mixed
    dh_ref[...] = dhidden if first else dh_in[...] + dhidden
    for kind, grad in enumerate((contract_rows(dbefore, hidden), contract_rows(active, upstream))):
        grad = grad.astype(BF).reshape(count, 4, rows, D)
        for at, target in enumerate(targets):
            target[:, kind] = grad[at]


def mlp(hidden, upstream, bias, packed, sums):
    rows, piece = hidden.shape[0], FF // PIECES
    pieces, arrays = sum(part.shape[0] for part in packed), len(packed)
    vmem, anywhere = pl.BlockSpec(memory_space=pltpu.VMEM), pl.BlockSpec(memory_space=pl.ANY)
    return pl.pallas_call(
        functools.partial(mlp_kernel, not sums, arrays),
        out_shape=[jax.ShapeDtypeStruct((rows, D), F32)] * 2
        + [jax.ShapeDtypeStruct((1, pieces * piece), F32)]
        + [jax.ShapeDtypeStruct((4, 2, piece, D), BF)] * (pieces // 4),
        in_specs=[vmem] * (3 + len(sums)) + [anywhere] * arrays,
        out_specs=[vmem] * (3 + pieces // 4),
        scratch_shapes=[
            pltpu.VMEM((2, pieces, piece, D), BF),
            pltpu.SemaphoreType.DMA((2 * arrays,)),
        ],
        input_output_aliases={3: 0, 4: 1} if sums else {},
        cost_estimate=cost(0.3),
        compiler_params=pltpu.CompilerParams(vmem_limit_bytes=20 * MIB),
    )(hidden, upstream, bias.reshape(1, -1), *sums, *packed)


THIRD = D // 3
BLOCKS = [(i, j) for i in range(3) for j in range(i, 3)]


def band(i):
    return slice(THIRD * i, THIRD * (i + 1))


def split_to(blocks, high, low):
    for (i, j), block in blocks.items():
        top = block.astype(BF)
        for target, part in ((high, top), (low, None if low is None else block - top.astype(F32))):
            if target is not None:
                part = part.astype(BF)
                target[band(i), band(j)] = part
                if i != j:
                    target[band(j), band(i)] = part.T


def product(*pairs):
    blocks = {}
    for i in range(3):
        total = None
        for left, right in pairs:
            term = jnp.dot(left[band(i), :], right[:, THIRD * i :], preferred_element_type=F32)
            total = term if total is None else total + term
        for j in range(i, 3):
            blocks[i, j] = total[:, band(j - i)]
    return blocks


def combined(*terms):
    return {at: sum(factor * blocks[at] for factor, blocks in terms) for at in BLOCKS}


def on_diagonal():
    shape = (THIRD, THIRD)
    return lax.broadcasted_iota(jnp.int32, shape, 0) == lax.broadcasted_iota(jnp.int32, shape, 1)


def diagonal_mean(blocks):
    total = blocks[0, 0] + blocks[1, 1] + blocks[2, 2]
    return jnp.sum(jnp.where(on_diagonal(), total, 0.0), keepdims=True) * (1.0 / D)


def without(blocks, mean):
    shift = jnp.where(on_diagonal(), mean, 0.0)
    return {(i, j): block - shift if i == j else block for (i, j), block in blocks.items()}


def orthogonal_kernel(
    order_ref, pieces_ref, rows_ref, out_ref, packed, rest_h, rest_l, change_h, twice_h, twice_l
):
    a, b, c = NS_COEFFS
    height = pieces_ref.shape[2]
    for at in range(8):
        target = pl.ds(pl.multiple_of(order_ref[at] * height, 8), height)
        packed[target, :] = pieces_ref[at // 4, at % 4]
    gram = {pair: packed[THIRD * at : THIRD * (at + 1), :] for at, pair in enumerate(BLOCKS)}
    mean = diagonal_mean(gram)
    inverse = 1.0 / (jnp.sqrt(mean * D) + 1e-07)
    rows = rows_ref[...] * inverse
    square = inverse * inverse
    mean = mean * square
    rest = without(combined((square, gram)), mean)
    for sweep in range(ITERS):
        last, fine = sweep == ITERS - 1, 0 < sweep < ITERS - 1
        split_to(rest, rest_h, rest_l if fine else None)
        p0 = a + b * mean + c * mean * mean
        p1 = b + 2.0 * c * mean
        change = combined((p1, rest), (c, product((rest_h, rest_h))))
        split_to(change, change_h, None)
        rows = p0 * rows + jnp.dot(rows.astype(BF), change_h[...], preferred_element_type=F32)
        if not last:
            twice = combined((2.0 * p0, change), (1.0, product((change_h, change_h))))
            split_to(twice, twice_h, twice_l if fine else None)
            pairs = [(rest_h, twice_h)] + [(rest_h, twice_l), (rest_l, twice_h)] * fine
            rest = combined((p0 * p0, rest), (mean, twice), (1.0, product(*pairs)))
            shift = diagonal_mean(rest)
            rest = without(rest, shift)
            mean = mean * p0 * p0 + shift
    out_ref[...] = rows.astype(BF)


def orthogonal(order, pieces, rows):
    vmem = pl.BlockSpec(memory_space=pltpu.VMEM)
    return pl.pallas_call(
        orthogonal_kernel,
        out_shape=jax.ShapeDtypeStruct(rows.shape, BF),
        in_specs=[pl.BlockSpec(memory_space=pltpu.SMEM)] + [vmem] * 2,
        out_specs=vmem,
        scratch_shapes=[pltpu.VMEM((len(BLOCKS) * THIRD, THIRD), F32)] + [pltpu.VMEM((D, D), BF)] * 5,
        cost_estimate=cost(17),
        compiler_params=pltpu.CompilerParams(vmem_limit_bytes=20 * MIB),
    )(order.astype(jnp.int32), pieces, rows)


def shards(
    patches, cotangent, lengths,
    w_qkv, w_out, w_fc1, w_fc2,
    mom_qkv, mom_out, mom_fc1, mom_fc2,
    vectors, vec_first, vec_second,
):
    strip_count, part_rows, width = patches.shape
    dp, seq = lax.axis_size("dp"), lax.axis_size("seq")
    assert strip_count == seq == 4
    net = (Paths if (dp, seq) == (8, 4) else Plain)(dp, seq)
    row_count = part_rows * seq

    strip, upstream_low = net.to_strip(jnp.stack([patches, cotangent], axis=1))
    first = net.gather_rows([w_qkv.astype(BF), w_out.astype(BF)], vectors.astype(BF))
    net.gather_packed([w_fc1.astype(BF), w_fc2.astype(BF)], first)
    flat = strip.astype(F32)
    normed = layer_norm(flat)
    net.gather_neighbours(normed)
    w_query, w_proj, vec_low = net.placed_rows(normed, upstream_low)
    (gain_one, bias_one, query_bias, value_bias, out_bias,
     gain_two, bias_two, fc1_bias, fc2_bias) = split_vector(vec_low.astype(F32))
    normed_low = (normed * gain_one + bias_one).astype(BF)

    owners = net.owners()
    places = (owners[:, None] * part_rows + jnp.arange(part_rows, dtype=jnp.int32)[None]).reshape(-1)
    length = lax.dynamic_index_in_dim(lengths, net.seq_at, 0, keepdims=False)
    key_mask = places < length
    there, back = net.order()
    order = there.astype(jnp.int32)

    joint_bias = jnp.concatenate([query_bias, jnp.zeros_like(query_bias), value_bias])
    projected = (contract_cols(normed_low, w_query) + joint_bias).astype(BF)
    attn_low = attend_forward(projected, key_mask)
    first_sum = flat + contract_cols(attn_low, w_proj) + out_bias
    normed_two_low = (layer_norm(first_sum) * gain_two + bias_two).astype(BF)
    net.gather_diagonal(normed_two_low)

    bias_there = fc1_bias.reshape(PIECES, -1)[there].reshape(8, -1)
    sums, grad_bias_there, tokens = [], {}, ()
    for parts in ((0, 4), (5, 6), (1, 2), (3, 7)):
        bias = jnp.concatenate([bias_there[at] for at in parts])
        packed = [net.packed_part(at) for at in parts]
        *sums, grad_bias, grads = (
            lambda out, dh, dbias, *grads: (out, dh, dbias, grads)
        )(*mlp(after(normed_two_low, *tokens), upstream_low, bias, packed, sums))
        grad_bias_there |= dict(zip(parts, grad_bias.reshape(len(parts), -1)))
        net.hidden_ready(parts, grads)
        tokens = net.send_neighbours() if parts == (1, 2) else ()
    second_sum = first_sum + sums[0] + fc2_bias
    grad_bias_there = jnp.stack([grad_bias_there[at] for at in range(8)]).reshape(PIECES, -1)
    grad_fc1_bias = grad_bias_there[back].reshape(-1)
    grad_fc2_bias = jnp.sum(upstream_low.astype(F32), axis=0)

    grad_first_sum, grad_attn, proj_near, proj_far, middle_sums = middle(
        order, first_sum, after(sums[1], *tokens), upstream_low, attn_low, w_proj, gain_two
    )
    tokens = (*net.proj_ready(proj_near, proj_far), *net.send_diagonal())
    query_near, query_far, grad_patches, vector_blocks = attend_backward(
        order, projected, key_mask, after(grad_attn, *tokens), normed_low, w_query,
        strip, grad_first_sum, gain_one,
        (middle_sums, grad_fc1_bias.reshape(4, width), grad_fc2_bias[None]),
    )
    shares, share_vector = net.query_ready(query_near, query_far, vector_blocks)
    counts = [share.shape[0] for share in shares]
    most = max(counts)
    stack_low = lambda parts: jnp.stack(
        [jnp.pad(part.astype(BF), ((0, most - part.shape[0]), (0, 0))) for part in parts]
    )
    moments = (mom_qkv, mom_out, mom_fc1, mom_fc2)
    weights_old = (w_qkv, w_out, w_fc1, w_fc2)
    owned_moment = net.to_owner(stack_low([net.piece(moment) for moment in net.with_query(moments)]))
    squares = sum(jnp.sum(share * share, axis=0) for share in shares)
    squares = squares + net.vector_squares(share_vector)
    owned_share, total_squares = net.to_owner_and_sum(stack_low(shares), squares, shares)
    grad_norm = jnp.sqrt(total_squares)
    clip = jnp.minimum(1.0, CLIP / (grad_norm + 1e-06))

    mine = MOMENTUM * owned_moment.astype(F32) + clip * owned_share.astype(F32)
    mine = mine.reshape(-1, width)
    gram_part = lax.dot_general(
        mine, mine, ROWS_LAST, precision=lax.Precision.HIGH, preferred_element_type=F32
    )
    upper = [
        gram_part[THIRD * i : THIRD * (i + 1), THIRD * j : THIRD * (j + 1)] for i, j in BLOCKS
    ]
    moments_new = net.update(moments, shares, clip)
    vector_grad = clip * share_vector
    first_new = BETA_ONE * vec_first + (1.0 - BETA_ONE) * vector_grad
    second_new = BETA_TWO * vec_second + (1.0 - BETA_TWO) * vector_grad * vector_grad
    first_hat = first_new / (1.0 - BETA_ONE**ADAM_STEP)
    second_hat = second_new / (1.0 - BETA_TWO**ADAM_STEP)
    vectors_new = vectors - VEC_RATE * first_hat / (jnp.sqrt(second_hat) + 1e-08)
    strips = jnp.stack([v.reshape(seq, part_rows, width) for v in (second_sum.astype(BF), grad_patches)], axis=1)
    order, pieces, share = net.sum_owner(jnp.concatenate(upper, axis=0), (*moments_new, vectors_new))
    net.from_strip(strips, share)
    weights_new = net.finish(weights_old, orthogonal(order, pieces, mine))
    mixed, grad_patches = net.placed_strips()
    results = [value for pair in zip(moments_new, weights_new) for value in pair]
    return (mixed, grad_patches, grad_norm, *results, first_new, second_new, vectors_new)


def solution(mesh):
    rows, flat, full = P("dp", None), P("dp"), P("dp", "seq", None)
    return jax.shard_map(
        shards,
        mesh=mesh,
        in_specs=(full, full, flat) + (rows,) * 8 + (flat,) * 3,
        out_specs=(full, full, P()) + (rows,) * 8 + (flat,) * 3,
        check_vma=False,
    )
```
